32 devices in a mesh: dp: 8 (over y, x, core), tm: 4 (over z).
Axes of the slice: x: 2, y: 2, z: 4, core: 2. Of those that a mesh axis runs over, the one named last changes fastest.
Arguments:
- volume: bfloat16 [16, 32, 14, 14, 512], P('dp', 'tm'), may hold values from -6 to 6
- segments: int32 [16, 32], P('dp'), may hold values from 0 to 3, as said below
- keep: int32 [16, 2, 8], P('dp'), may hold values 0 or 1
- ln1_gain: float32 [512], replicated, may hold values from 0.1 to 1.9
- ln1_bias: float32 [512], replicated, may hold values from -1.75 to 1.75
- w_qkv: bfloat16 [512, 1536], replicated, may hold values from -0.25 to 0.25
- q_bias: float32 [512], replicated, may hold values from -3 to 3
- v_bias: float32 [512], replicated, may hold values from -3 to 3
- rel_table: float32 [2535, 16], replicated, may hold values from -6 to 6
- w_proj: bfloat16 [512, 512], replicated, may hold values from -2 to 2
- proj_bias: float32 [512], replicated, may hold values from -1.75 to 1.75
- ln2_gain: float32 [512], replicated, may hold values from 0.1 to 1.9
- ln2_bias: float32 [512], replicated, may hold values from -1.75 to 1.75
- w_fc1: bfloat16 [512, 2048], replicated, may hold values from -0.25 to 0.25
- fc1_bias: float32 [2048], replicated, may hold values from -3 to 3
- w_fc2: bfloat16 [2048, 512], replicated, may hold values from -0.125 to 0.125
- fc2_bias: float32 [512], replicated, may hold values from -1.75 to 1.75
- cotangent: bfloat16 [16, 32, 14, 14, 512], P('dp', 'tm'), may hold values from -6 to 6
Outputs:
- mixed_out: bfloat16 [16, 32, 14, 14, 512], P('dp', 'tm')
- volume_grad: float32 [16, 32, 14, 14, 512], P('dp', 'tm')
- ln1_gain_grad: float32 [512], replicated
- ln1_bias_grad: float32 [512], replicated
- w_qkv_grad: float32 [512, 1536], replicated
- q_bias_grad: float32 [512], replicated
- v_bias_grad: float32 [512], replicated
- rel_table_grad: float32 [2535, 16], replicated
- w_proj_grad: float32 [512, 512], replicated
- proj_bias_grad: float32 [512], replicated
- ln2_gain_grad: float32 [512], replicated
- ln2_bias_grad: float32 [512], replicated
- w_fc1_grad: float32 [512, 2048], replicated
- fc1_bias_grad: float32 [2048], replicated
- w_fc2_grad: float32 [2048, 512], replicated
- fc2_bias_grad: float32 [512], replicated
The draws below stay inside these ranges and needn't reach their ends.
Inputs may be any that keep to these rules, and one draw needn't show every extreme that they name: `segments`: in every volume the clip numbers start at 0 on the first frame and rise by one at each new clip; every clip but the last has 4 to 8 frames, and the numbering stops at min(7, 3), the last clip taking the remaining frames.
All inputs are finite; a program needn't handle non-finite values. No bound on the sum of `keep` on one device may be relied on, other than what follows from the above.
Results may differ from the reference program's by a relative error of at most 0.011.
Values may be sent and summed in bfloat16 or wider, within the bound.
No kernel may reach another device: no remote copies, remote signals or barrier semaphores. Data moves between devices by JAX's collectives and lax.ppermute only.
A program may use at most 576 MiB of HBM per device.

```python
from functools import partial
import jax
import jax.numpy as jnp
import numpy as np
from jax import lax

D = 512
HEADS = 16
FF = 2048
SIDE = 14
WT = 8
WIN_HW = 7
SHIFT_T = 4
SHIFT_HW = 3
TABLE = 2535
FRAMES = 32
BATCH = 16


def draw_segments(key, part):
    key = jax.random.fold_in(key, 7)
    clip_slots = FRAMES // SHIFT_T
    lengths = jax.random.randint(key, (BATCH, clip_slots), SHIFT_T, WT + 1)
    finishes = jnp.cumsum(lengths, axis=1)
    positions = jnp.arange(FRAMES)
    passed = (positions[None, :, None] >= finishes[:, None, :]).astype(jnp.int32)
    return jnp.minimum(jnp.sum(passed, axis=2), min(7, FRAMES // WT - 1)).astype(jnp.int32)


def set_ends(array, stream_key, smallest, largest):
    longest = array.shape.index(max(array.shape))
    spots = []
    for shift in (0, 1):
        where = [jax.random.randint(jax.random.fold_in(stream_key, axis), (), 0, length) for axis, length in enumerate(array.shape)]
        where[longest] = (where[longest] + shift) % array.shape[longest]
        spots.append(tuple(where))
    return array.at[spots[0]].set(smallest).at[spots[1]].set(largest)


def levels(key, shape, split, least, high):
    gain = 1.0
    for position, shards_of in split:
        heights = jax.random.uniform(jax.random.fold_in(jax.random.fold_in(key, 6), position), (shards_of,), jnp.float32, least / len(split), high / len(split))
        gain = gain * jnp.repeat(jnp.exp(heights), shape[position] // shards_of).reshape((-1,) + (1,) * (len(shape) - 1 - position))
    return gain


def gaussian(own_key, shape, width, bound, split=(), held_as=jnp.bfloat16):
    values = width * jax.random.normal(own_key, shape, jnp.float32)
    if split:
        values = values * levels(own_key, shape, split, -0.22, 0.18)
    return jnp.clip(values, -bound, bound).astype(held_as)


def setup_inputs(seed: int = 0) -> dict:
    keys = jax.random.split(jax.random.key(seed), 19)
    return {
        "volume": gaussian(keys[0], (BATCH, FRAMES, SIDE, SIDE, D), 1.0, 6.0, ((0, 8), (1, 4))),
        "segments": draw_segments(jax.random.fold_in(keys[18], 71), 0),
        "keep": set_ends((jax.random.randint(keys[2], (BATCH, 2, 8), 0, 4) < 3).astype(jnp.int32), jax.random.fold_in(keys[2], 1), 0, 1),
        "ln1_gain": jnp.clip(1.0 + 0.18 * jax.random.normal(keys[3], (D,), jnp.float32), 0.1, 1.9),
        "ln1_bias": gaussian(keys[4], (D,), 0.3, 1.75, (), jnp.float32),
        "w_qkv": gaussian(keys[5], (D, 3 * D), D ** -0.5, 0.25),
        "q_bias": gaussian(keys[6], (D,), 0.5, 3.0, (), jnp.float32),
        "v_bias": gaussian(keys[7], (D,), 0.5, 3.0, (), jnp.float32),
        "rel_table": gaussian(keys[8], (TABLE, HEADS), 1.0, 6.0, (), jnp.float32),
        "w_proj": gaussian(keys[9], (D, D), (max(D // 64, 1)) ** -0.5, 2.0),
        "proj_bias": gaussian(keys[10], (D,), 0.3, 1.75, (), jnp.float32),
        "ln2_gain": jnp.clip(1.0 + 0.18 * jax.random.normal(keys[11], (D,), jnp.float32), 0.1, 1.9),
        "ln2_bias": gaussian(keys[12], (D,), 0.3, 1.75, (), jnp.float32),
        "w_fc1": gaussian(keys[13], (D, FF), D ** -0.5, 0.25),
        "fc1_bias": gaussian(keys[14], (FF,), 0.5, 3.0, (), jnp.float32),
        "w_fc2": gaussian(keys[15], (FF, D), FF ** -0.5, 0.125),
        "fc2_bias": gaussian(keys[16], (D,), 0.3, 1.75, (), jnp.float32),
        "cotangent": gaussian(keys[17], (BATCH, FRAMES, SIDE, SIDE, D), 1.0, 6.0, ((0, 8), (1, 4))),
    }


EPS = 1e-05
KEEP_RATE = 0.75
PRECISE = lax.Precision.HIGHEST

@jax.custom_vjp
def low(v):
    return lax.optimization_barrier(v.astype(jnp.bfloat16)).astype(jnp.float32)

@jax.custom_vjp
def low_back(v):
    return v

def low_keep(v):
    return (low(v), None)

def low_pass(kept, grad):
    return (grad,)

def back_keep(v):
    return (v, None)

def back_low(kept, grad):
    return (low(grad),)
low.defvjp(low_keep, low_pass)
low_back.defvjp(back_keep, back_low)

def layer_norm(values, scaling, offset):
    centre = values - lax.optimization_barrier(jnp.mean(values, axis=-1, keepdims=True))
    spread = lax.optimization_barrier(jnp.mean(centre * centre, axis=-1, keepdims=True))
    return centre * lax.rsqrt(spread + EPS) * scaling + offset

def relative_index(frames_win, side_win):
    grid_t, grid_h, grid_w = np.meshgrid(np.arange(frames_win), np.arange(side_win), np.arange(side_win), indexing='ij')
    coords = np.stack([grid_t.ravel(), grid_h.ravel(), grid_w.ravel()])
    offsets = coords[:, :, None] - coords[:, None, :]
    across = 2 * side_win - 1
    return ((offsets[0] + frames_win - 1) * across * across + (offsets[1] + side_win - 1) * across + offsets[2] + side_win - 1).astype(np.int32)

def region_table(side_len, side_win, shift_hw):
    places = np.arange(side_len)
    region_marks = (places >= side_len - side_win).astype(np.int32) + (places >= side_len - shift_hw).astype(np.int32)
    region = region_marks[:, None] * 3 + region_marks[None, :]
    per_side = side_len // side_win
    windows = region.reshape(per_side, side_win, per_side, side_win).transpose(0, 2, 1, 3)
    return windows.reshape(per_side * per_side, side_win * side_win)

def to_windows(field_grid):
    channels = field_grid.shape[-1]
    per_time = field_grid.shape[0] // WT
    per_side = field_grid.shape[1] // WIN_HW
    pieces = field_grid.reshape(per_time, WT, per_side, WIN_HW, per_side, WIN_HW, channels)
    pieces = pieces.transpose(0, 2, 4, 1, 3, 5, 6)
    return pieces.reshape(per_time * per_side * per_side, WT * WIN_HW * WIN_HW, channels)

def from_windows(windows, frames):
    channels = windows.shape[-1]
    per_time = frames // WT
    per_side = SIDE // WIN_HW
    pieces = windows.reshape(per_time, per_side, per_side, WT, WIN_HW, WIN_HW, channels)
    return pieces.transpose(0, 3, 1, 4, 2, 5, 6).reshape(frames, SIDE, SIDE, channels)

def attend_window(inputs_pair, pos_bias):
    packed, combo_ids = inputs_pair
    tokens = packed.shape[0]
    head_dim = D // HEADS
    parts = packed.reshape(tokens, 3, HEADS, head_dim)
    query_part, key_part, value_part = (parts[:, 0], parts[:, 1], parts[:, 2])
    raw_scores = jnp.einsum('qhd,khd->hqk', query_part, key_part, precision=PRECISE) * head_dim ** (-0.5) + pos_bias
    raw_scores = low_back(raw_scores)
    allowed = combo_ids[:, None] == combo_ids[None, :]
    masked = jnp.where(allowed[None], raw_scores, -jnp.inf)
    prob_low = low(jax.nn.softmax(masked, axis=-1))
    attended = jnp.einsum('hqk,khd->qhd', prob_low, value_part, precision=PRECISE)
    return attended.reshape(tokens, D)

def forward_row(x_row, seg_row, keep_row, params):
    ln1_gain, ln1_bias, w_qkv, q_bias, v_bias, rel_table, w_proj, proj_bias, ln2_gain, ln2_bias, w_fc1, fc1_bias, w_fc2, fc2_bias = params
    frames = x_row.shape[0]
    normed = low(layer_norm(x_row, ln1_gain, ln1_bias))
    joined = jnp.dot(normed, w_qkv, precision=PRECISE) + jnp.concatenate([q_bias, jnp.zeros_like(q_bias), v_bias])
    joined = low_back(low(joined))
    rolled = jnp.roll(joined, (-SHIFT_T, -SHIFT_HW, -SHIFT_HW), axis=(0, 1, 2))
    windows = to_windows(rolled)
    frame_ids = jnp.arange(frames)
    time_key = jnp.roll(seg_row + 8 * (frame_ids < SHIFT_T).astype(jnp.int32), -SHIFT_T)
    regions = jnp.asarray(region_table(SIDE, WIN_HW, SHIFT_HW))
    combos = (time_key.reshape(-1, 1, WT, 1) * 9 + regions[None, :, None, :]).reshape(windows.shape[0], -1)
    rel_index = jnp.asarray(relative_index(WT, WIN_HW))
    pos_bias = jnp.transpose(rel_table[rel_index], (2, 0, 1))
    attended = lax.map(jax.checkpoint(partial(attend_window, pos_bias=pos_bias)), (windows, combos))
    attended = low_back(low(from_windows(attended, frames)))
    attended = jnp.roll(attended, (SHIFT_T, SHIFT_HW, SHIFT_HW), axis=(0, 1, 2))
    branch = low_back(jnp.dot(attended, w_proj, precision=PRECISE) + proj_bias)
    seg_hot = (seg_row[:, None] == jnp.arange(8)[None, :]).astype(jnp.float32)
    drop_attn = (lax.optimization_barrier(jnp.sum(seg_hot * keep_row[0][None, :], axis=1)) / KEEP_RATE)[:, None, None, None]
    drop_mlp = (lax.optimization_barrier(jnp.sum(seg_hot * keep_row[1][None, :], axis=1)) / KEEP_RATE)[:, None, None, None]
    middle = x_row + drop_attn * branch
    normed2 = low(layer_norm(middle, ln2_gain, ln2_bias))
    hidden = low_back(jnp.dot(normed2, w_fc1, precision=PRECISE) + fc1_bias)
    active = low(jax.nn.gelu(hidden, approximate=False))
    result = low_back(jnp.dot(active, w_fc2, precision=PRECISE) + fc2_bias)
    return middle + drop_mlp * result

def reference(volume, segments, keep, ln1_gain, ln1_bias, w_qkv, q_bias, v_bias, rel_table, w_proj, proj_bias, ln2_gain, ln2_bias, w_fc1, fc1_bias, w_fc2, fc2_bias, cotangent):
    weights = tuple((argument.astype(jnp.float32) for argument in (ln1_gain, ln1_bias, w_qkv, q_bias, v_bias, rel_table, w_proj, proj_bias, ln2_gain, ln2_bias, w_fc1, fc1_bias, w_fc2, fc2_bias)))
    keep_float = keep.astype(jnp.float32)

    def per_row(totals, row_inputs):
        x_row, seg_row, keep_row, cot_row = row_inputs

        def forward(x_in, params):
            return forward_row(x_in, seg_row, keep_row, params)
        out_row, pullback = jax.vjp(forward, x_row.astype(jnp.float32), weights)
        x_grad, param_grads = pullback(cot_row.astype(jnp.float32))
        totals = jax.tree.map(jnp.add, totals, param_grads)
        return (totals, (out_row.astype(jnp.bfloat16), x_grad))
    zero_grads = jax.tree.map(jnp.zeros_like, weights)
    grads, (mixed_out, volume_grad) = lax.scan(per_row, zero_grads, (volume, segments, keep_float, cotangent))
    return (mixed_out, volume_grad, grads[0], grads[1], grads[2], grads[3], grads[4], grads[5], grads[6], grads[7], grads[8], grads[9], grads[10], grads[11], grads[12], grads[13])
```

```python
import functools

import jax
import jax.numpy as jnp
import numpy as np
from jax import lax
from jax.experimental import pallas as pl
from jax.experimental.pallas import tpu as pltpu
from jax.sharding import PartitionSpec as P

SIDE = 14
WT = 8
WIN_HW = 7
SHIFT_T = 4
SHIFT_HW = 3
EPS = 1e-05
KEEP_RATE = 0.75
PRECISE = lax.Precision.HIGHEST
LOG2E = 1.4426950408889634
LN2 = 0.6931471805599453
FAR = 1e30
F32 = jnp.float32
BF16 = jnp.bfloat16

SPANS = (
    (SHIFT_HW, WIN_HW),
    (SHIFT_HW + WIN_HW, SIDE - SHIFT_HW - WIN_HW),
    (0, SHIFT_HW),
)
ACROSS = 2 * WIN_HW - 1
RECTS = (
    (0, 0, True, 0),
    (1, 0, True, 0),
    (0, 1, False, 1),
    (2, 0, True, 0),
    (0, 2, False, 1),
    (2, 2, True, 3),
    (2, 1, True, 2),
    (1, 2, True, 3),
    (1, 1, True, 2),
)
BIAS_DIMS = ((7, 7), (4, 7), (4, 4), (4, 3))


def up_to(value, unit):
    return -(-value // unit) * unit


class Rect:
    pass


def plan_rects():
    rects, slots, start = [], [], 0
    class_rows = [0, 0, 0]
    for row_span, col_span, rows_outer, table in RECTS:
        r0, rn = SPANS[row_span]
        c0, cn = SPANS[col_span]
        rect = Rect()
        if rows_outer:
            places = [(r0 + a, c0 + b) for a in range(rn) for b in range(cn)]
        else:
            places = [(r0 + b, c0 + a) for a in range(cn) for b in range(rn)]
        rect.count = len(places) * WT
        rect.rows = up_to(rect.count, 16)
        rect.lanes = up_to(rect.count, 128)
        rect.start = start
        rect.table = table
        rect.kind = {512: 0, 256: 1, 128: 2}[rect.lanes]
        rect.kind_row = class_rows[rect.kind]
        class_rows[rect.kind] += rect.rows
        slots += places + [None] * ((rect.rows - rect.count) // WT)
        start += rect.rows
        rects.append(rect)
    return rects, slots, class_rows


RECT, SLOTS, KIND_ROWS = plan_rects()
TOKENS = len(SLOTS) * WT
KIND_LANES = (512, 256, 128)
ROW_PAD = 16
FRAME_ROWS = SIDE * ROW_PAD


def nn(a, b):
    return lax.dot_general(a, b, (((1,), (0,)), ((), ())), preferred_element_type=F32)


def nt(a, b):
    return lax.dot_general(a, b, (((1,), (1,)), ((), ())), preferred_element_type=F32)


def wide(pattern, width):
    return jnp.concatenate([pattern] * (width // pattern.shape[-1]), axis=-1)


def by_frame(values, pattern):
    rows, width = values.shape
    scaled = values.reshape(rows // WT, WT, width) * wide(pattern, width)[None]
    return scaled.reshape(rows, width)


def column_sums(values):
    rows, width = values.shape
    return jnp.sum(values.reshape(rows // 8, 8, width), axis=0)


def gather_tokens(block_ref, offset, grid32):
    def frame(f, carry):
        base = pl.multiple_of((offset + f) * FRAME_ROWS, ROW_PAD)
        for h in range(SIDE):
            row = block_ref[f, h].astype(F32)
            for part in range(4):
                grid32[part, pl.ds(base + h * ROW_PAD, SIDE), :] = row[:, part * 128 : part * 128 + 128]
        return carry

    lax.fori_loop(0, SHIFT_T, frame, 0)


def grid_to_tokens(grid32, tokens):
    for slot, place in enumerate(SLOTS):
        rows = slice(slot * WT, slot * WT + WT)
        for part in range(4):
            lanes = slice(part * 128, part * 128 + 128)
            if place is None:
                tokens[rows, lanes] = jnp.zeros((WT, 128), F32)
            else:
                at = place[0] * ROW_PAD + place[1]
                tokens[rows, lanes] = grid32[part, pl.ds(at, WT, stride=FRAME_ROWS), :]


def tokens_to_grid(tokens, grid32):
    for slot, place in enumerate(SLOTS):
        if place is None:
            continue
        rows = slice(slot * WT, slot * WT + WT)
        at = place[0] * ROW_PAD + place[1]
        for part in range(4):
            grid32[part, pl.ds(at, WT, stride=FRAME_ROWS), :] = tokens[rows, part * 128 : part * 128 + 128]


def grid_to_frames(grid32, offset, block_ref):
    def frame(f, carry):
        base = pl.multiple_of((offset + f) * FRAME_ROWS, ROW_PAD)
        for h in range(SIDE):
            row = [grid32[part, pl.ds(base + h * ROW_PAD, SIDE), :] for part in range(4)]
            block_ref[f, h] = jnp.concatenate(row, axis=-1).astype(block_ref.dtype)
        return carry

    lax.fori_loop(0, SHIFT_T, frame, 0)


def spread_table(source, outer, inner, out_ref, lane):
    width = inner * WT
    total = outer * width
    for ok in range(outer):
        for ik in range(inner):
            pieces = []
            for oq in range(outer):
                shift = (oq * width - (WIN_HW - 1 - ik) * WT) % 128
                piece = source[oq - ok + WIN_HW - 1]
                pieces.append(pltpu.roll(piece, shift, 1) if shift else piece)
            row = (ok * inner + ik) * WT
            for tile in range(up_to(total, 128) // 128):
                value = None
                for oq in range(outer):
                    begin, end = oq * width, (oq + 1) * width
                    if end <= tile * 128 or begin >= tile * 128 + 128:
                        continue
                    if value is None:
                        value = pieces[oq]
                    else:
                        value = jnp.where(lane >= begin - tile * 128, pieces[oq], value)
                out_ref[0, row : row + WT, tile * 128 : tile * 128 + 128] = value


def bias_kernel(rows_ref, cols_ref, b0_ref, b1_ref, b2_ref, b3_ref):
    lane = lax.broadcasted_iota(jnp.int32, (WT, 128), 1)
    by_rows = [rows_ref[0, d] for d in range(ACROSS)]
    by_cols = [cols_ref[0, d] for d in range(ACROSS)]
    for out_ref, source, (outer, inner) in zip(
        (b0_ref, b1_ref, b2_ref, b3_ref), (by_rows, by_cols, by_rows, by_rows), BIAS_DIMS
    ):
        spread_table(source, outer, inner, out_ref, lane)


def bias_shapes(heads):
    shapes = []
    for outer, inner in BIAS_DIMS:
        count = outer * inner * WT
        shapes.append((heads, count, up_to(count, 128)))
    return shapes


def time_hot():
    places = np.arange(WT)
    hot = places[None, :, None] - places[:, None, None] + WT - 1 == np.arange(2 * WT - 1)[None, None, :]
    return jnp.asarray(hot.astype(np.float32))


def make_bias(rel_table):
    heads = rel_table.shape[1]
    cube = rel_table.reshape(2 * WT - 1, ACROSS, ACROSS, heads) * LOG2E
    both = jnp.einsum("ksd,dabn->nakbs", time_hot(), cube, precision=PRECISE)
    swapped = jnp.einsum("ksd,dabn->nbkas", time_hot(), cube, precision=PRECISE)
    pad = ((0, 0), (0, 0), (0, 0), (0, 128 - ACROSS * WT))
    by_rows = jnp.pad(both.reshape(heads, ACROSS, WT, ACROSS * WT), pad)
    by_cols = jnp.pad(swapped.reshape(heads, ACROSS, WT, ACROSS * WT), pad)
    strip = pl.BlockSpec((1, ACROSS, WT, 128), lambda h: (h, 0, 0, 0))
    shapes = bias_shapes(heads)
    return pl.pallas_call(
        bias_kernel,
        grid=(heads,),
        in_specs=[strip, strip],
        out_specs=[pl.BlockSpec((1,) + s[1:], lambda h: (h, 0, 0)) for s in shapes],
        out_shape=[jax.ShapeDtypeStruct(s, F32) for s in shapes],
        compiler_params=pltpu.CompilerParams(vmem_limit_bytes=48 << 20),
        name="position_bias",
    )(by_rows, by_cols)


def fold_table(acc, outer, inner, totals, lane):
    width = inner * WT
    for ok in range(outer):
        for ik in range(inner):
            row = (ok * inner + ik) * WT
            for oq in range(outer):
                shift = (oq * width - (WIN_HW - 1 - ik) * WT) % 128
                begin, end = oq * width, (oq + 1) * width
                tile, lo = begin // 128, begin % 128
                last = (end - 1) // 128
                value = acc(row, tile)
                if last == tile:
                    value = jnp.where((lane >= lo) & (lane < lo + width), value, 0.0)
                else:
                    after = jnp.where(lane < end - last * 128, acc(row, last), 0.0)
                    value = jnp.where(lane >= lo, value, after)
                d = oq - ok + WIN_HW - 1
                back = pltpu.roll(value, (128 - shift) % 128, 1) if shift else value
                totals[d] = totals[d] + back


def qkv_kernel(
    tile, scale, own_ref, recv_ref, gain_ref, bias_ref, w_ref, wb_ref, x_ref, n_ref, q_ref, k_ref, v_ref, grid32, tokens
):
    win, step = pl.program_id(0), pl.program_id(1)

    @pl.when(step == 0)
    def _():
        gather_tokens(own_ref.at[0], win * SHIFT_T, grid32)
        gather_tokens(recv_ref.at[0], SHIFT_T - win * SHIFT_T, grid32)
        grid_to_tokens(grid32, tokens)

    x = tokens[pl.ds(pl.multiple_of(step * tile, 16), tile), :]
    x_ref[0] = x.astype(BF16)
    centre = x - jnp.mean(x, axis=-1, keepdims=True)
    spread = jnp.mean(centre * centre, axis=-1, keepdims=True)
    normed = (centre * lax.rsqrt(spread + EPS) * gain_ref[...] + bias_ref[...]).astype(BF16)
    n_ref[0] = normed
    width = x.shape[1]
    q_ref[0] = ((nn(normed, w_ref[:, :width]) + wb_ref[:, :width]) * scale).astype(BF16)
    k_ref[0] = nn(normed, w_ref[:, width : 2 * width]).astype(BF16)
    v_ref[0] = (nn(normed, w_ref[:, 2 * width :]) + wb_ref[:, 2 * width :]).astype(BF16)


def whole(shape):
    return pl.BlockSpec(shape, lambda *_: (0,) * len(shape))


def half_spec(side, width):
    return pl.BlockSpec((1, SHIFT_T, side, side, width), lambda w, j: (w, 1 - w, 0, 0, 0))


def other_spec(side, width):
    return pl.BlockSpec((1, SHIFT_T, side, side, width), lambda w, j: (w, 0, 0, 0, 0))


def tile_spec(tile, width):
    return pl.BlockSpec((1, tile, width), lambda w, j: (w, j, 0))


def make_qkv(volume, recv, gain, bias, w_qkv, qkv_bias, scale, tile=400):
    width = volume.shape[-1]
    out = jax.ShapeDtypeStruct((2, TOKENS, width), BF16)
    return pl.pallas_call(
        functools.partial(qkv_kernel, tile, scale),
        grid=(2, TOKENS // tile),
        in_specs=[
            half_spec(SIDE, width),
            other_spec(SIDE, width),
            whole((1, width)),
            whole((1, width)),
            whole(w_qkv.shape),
            whole((1, 3 * width)),
        ],
        out_specs=[tile_spec(tile, width)] * 5,
        out_shape=[out] * 5,
        scratch_shapes=[
            pltpu.VMEM((4, WT * FRAME_ROWS, 128), F32),
            pltpu.VMEM((TOKENS, width), F32),
        ],
        compiler_params=pltpu.CompilerParams(vmem_limit_bytes=60 << 20),
        name="norm1_qkv",
    )(volume, recv, gain[None], bias[None], w_qkv, qkv_bias[None])


def head_rows(transposed, head, dim):
    rows, lanes = transposed.shape
    parts = []
    if head:
        parts.append(jnp.zeros((head * dim, lanes), transposed.dtype))
    parts.append(transposed[head * dim : head * dim + dim])
    if (head + 1) * dim < rows:
        parts.append(jnp.zeros((rows - (head + 1) * dim, lanes), transposed.dtype))
    return jnp.concatenate(parts, axis=0)


def attend_kernel(
    dim, q_ref, k_ref, v_ref, far_ref, b0, b1, b2, b3, e0_ref, e1_ref, e2_ref, o_ref, r_ref, scores
):
    biases = (b0, b1, b2, b3)
    e_refs = (e0_ref, e1_ref, e2_ref)
    far = far_ref[0]
    per = 128 // dim
    for rect in RECT:
        count, rows, lanes, start = rect.count, rect.rows, rect.lanes, rect.start
        kind_rows = slice(rect.kind_row, rect.kind_row + rows)
        e_ref = e_refs[rect.kind]
        queries = q_ref[0, start : start + lanes, :].T
        keys = k_ref[0, start : start + rows, :]
        values = v_ref[0, start : start + rows, :].T
        ones = jnp.ones((16, rows), BF16)
        wide_far = wide(far, lanes)
        outs, scales = [], []
        for head in range(per):
            raw = nn(keys, head_rows(queries, head, dim))[:count]
            raw = raw + biases[rect.table][head, :count, :lanes]
            scores[:count, :lanes] = raw
            blocks = raw.reshape(count // 8, 8, lanes)
            top = jnp.max(blocks, axis=0) - wide_far
            top = jnp.max(top, axis=0, keepdims=True) + wide_far
            exps = jnp.exp2(scores[:count, :lanes].reshape(count // 8, 8, lanes) - top[None])
            exps = exps.reshape(count, lanes).astype(BF16)
            if rows > count:
                exps = jnp.concatenate([exps, jnp.zeros((rows - count, lanes), BF16)], axis=0)
            e_ref[0, 0, kind_rows, head * lanes : head * lanes + lanes] = exps
            lhs = jnp.concatenate([values[head * dim : head * dim + dim], ones], axis=0)
            out = nn(lhs, exps)
            inverse = jnp.broadcast_to(1.0 / out[dim : dim + 1], (dim, lanes))
            outs.append(out[:dim] * inverse)
            scales.append(inverse)
        o_ref[0, start : start + rows, :] = jnp.concatenate(outs, axis=0).T[:rows].astype(BF16)
        r_ref[0, start : start + rows, :] = jnp.concatenate(scales, axis=0).T[:rows]


def head_group_specs(heads, per, biases):
    lane_tile = pl.BlockSpec((1, TOKENS, 128), lambda g, w: (w, 0, g))
    far = pl.BlockSpec((1, WT, 128), lambda g, w: (w, 0, 0))
    bias = [pl.BlockSpec((per,) + b[1:], lambda g, w: (g, 0, 0)) for b in biases]
    exps = [
        pl.BlockSpec((1, 1, KIND_ROWS[i], per * KIND_LANES[i]), lambda g, w: (w, g, 0, 0)) for i in range(3)
    ]
    return lane_tile, far, bias, exps


def exps_shapes(groups, per):
    return [jax.ShapeDtypeStruct((2, groups, KIND_ROWS[i], per * KIND_LANES[i]), BF16) for i in range(3)]


def attend(q, k, v, far, biases, dim):
    width = q.shape[-1]
    heads = width // dim
    per = 128 // dim
    groups = heads // per
    lane_tile, far_spec, bias_specs, exps_specs = head_group_specs(heads, per, [b.shape for b in biases])
    return pl.pallas_call(
        functools.partial(attend_kernel, dim),
        grid=(groups, 2),
        in_specs=[lane_tile] * 3 + [far_spec] + bias_specs,
        out_specs=exps_specs + [lane_tile, lane_tile],
        out_shape=exps_shapes(groups, per)
        + [jax.ShapeDtypeStruct((2, TOKENS, width), BF16), jax.ShapeDtypeStruct((2, TOKENS, width), F32)],
        scratch_shapes=[pltpu.VMEM((RECT[0].count, RECT[0].lanes), F32)],
        compiler_params=pltpu.CompilerParams(vmem_limit_bytes=60 << 20),
        name="attention",
    )(q, k, v, far, *biases)


def attend_back_kernel(
    dim,
    scale,
    q_ref,
    k_ref,
    v_ref,
    g_ref,
    o_ref,
    e0_ref,
    e1_ref,
    e2_ref,
    dq_ref,
    dk_ref,
    dv_ref,
    rows_ref,
    cols_ref,
    a0,
    a1,
    a2,
    a3,
    grads,
    queries,
    outgrads,
):
    win = pl.program_id(1)
    accs = (a0, a1, a2, a3)
    e_refs = (e0_ref, e1_ref, e2_ref)
    per = 128 // dim
    lane = lax.broadcasted_iota(jnp.int32, (16, 128), 1)

    @pl.when(win == 0)
    def _():
        for acc in accs:
            acc[...] = jnp.zeros_like(acc)

    for rect in RECT:
        count, rows, lanes, start = rect.count, rect.rows, rect.lanes, rect.start
        kind_rows = slice(rect.kind_row, rect.kind_row + rows)
        e_ref = e_refs[rect.kind]
        keys = k_ref[0, start : start + rows, :]
        values = v_ref[0, start : start + rows, :]
        out_grad = g_ref[0, start : start + rows, :]
        if lanes > rows:
            out_grad = jnp.concatenate([out_grad, jnp.zeros((lanes - rows, 128), BF16)], axis=0)
        query = q_ref[0, start : start + lanes, :]
        out_grad_t = out_grad.T
        out_t = o_ref[0, start : start + lanes, :].T
        keys_t = keys.T
        product = out_grad_t.astype(F32) * out_t.astype(F32)
        dqs = []
        for head in range(per):
            here = slice(head * lanes, head * lanes + lanes)
            mine = ((lane[:1] >= head * dim) & (lane[:1] < head * dim + dim)).astype(BF16)
            queries[here, :] = query * mine
            outgrads[here, :] = out_grad * mine
            inner = jnp.sum(product[head * dim : head * dim + dim], axis=0, keepdims=True)
            prob_grad = nn(values, head_rows(out_grad_t, head, dim))
            exps = e_ref[0, 0, kind_rows, here].astype(F32)
            score_grad = exps * (prob_grad - inner)
            low = score_grad.astype(BF16)
            accs[rect.table][head, :count, :lanes] += score_grad[:count]
            grads[:rows, here] = low
            dqs.append(nn(keys_t[head * dim : head * dim + dim], low))
        dq = jnp.concatenate(dqs, axis=0) * scale
        dq_ref[0, start : start + rows, :] = dq.T[:rows].astype(BF16)
        dk = nn(grads[:rows, : per * lanes], queries[: per * lanes, :])
        dk_ref[0, start : start + rows, :] = (dk * LN2).astype(BF16)
        dv = nn(e_ref[0, 0, kind_rows, :], outgrads[: per * lanes, :])
        dv_ref[0, start : start + rows, :] = dv.astype(BF16)

    @pl.when(win == 1)
    def _():
        lane8 = lax.broadcasted_iota(jnp.int32, (WT, 128), 1)
        for head in range(per):
            by_rows = [jnp.zeros((WT, 128), F32) for _ in range(ACROSS)]
            by_cols = [jnp.zeros((WT, 128), F32) for _ in range(ACROSS)]
            for acc, totals, (outer, inner) in zip(accs, (by_rows, by_cols, by_rows, by_rows), BIAS_DIMS):
                fold_table(
                    lambda row, tile: acc[head, row : row + WT, tile * 128 : tile * 128 + 128],
                    outer,
                    inner,
                    totals,
                    lane8,
                )
            for d in range(ACROSS):
                rows_ref[head, d] = by_rows[d]
                cols_ref[head, d] = by_cols[d]


def attend_back(q, k, v, out_grad, out, exps, dim):
    width = q.shape[-1]
    heads = width // dim
    per = 128 // dim
    groups = heads // per
    shapes = bias_shapes(heads)
    lane_tile, _, _, exps_specs = head_group_specs(heads, per, shapes)
    strip = pl.BlockSpec((per, ACROSS, WT, 128), lambda g, w: (g, 0, 0, 0))
    strip_shape = jax.ShapeDtypeStruct((heads, ACROSS, WT, 128), F32)
    grad = jax.ShapeDtypeStruct((2, TOKENS, width), BF16)
    most = per * RECT[0].lanes
    return pl.pallas_call(
        functools.partial(attend_back_kernel, dim, dim**-0.5),
        grid=(groups, 2),
        in_specs=[lane_tile] * 5 + exps_specs,
        out_specs=[lane_tile] * 3 + [strip] * 2,
        out_shape=[grad] * 3 + [strip_shape] * 2,
        scratch_shapes=[pltpu.VMEM((per,) + s[1:], F32) for s in shapes]
        + [
            pltpu.VMEM((RECT[0].rows, most), BF16),
            pltpu.VMEM((most, 128), BF16),
            pltpu.VMEM((most, 128), BF16),
        ],
        compiler_params=pltpu.CompilerParams(vmem_limit_bytes=60 << 20),
        name="attention_back",
    )(q, k, v, out_grad, out, *exps)


ERFC = (0.254829592, -0.284496736, 1.421413741, -1.453152027, 1.061405429)
ERFC_P = 0.3275911


def gelu_both(u):
    t = 1.0 / (1.0 + (ERFC_P * 0.5**0.5) * jnp.abs(u))
    bell = jnp.exp2((u * u) * (-0.5 * LOG2E))
    series = 0.5 * ERFC[4]
    for factor in ERFC[3::-1]:
        series = series * t + 0.5 * factor
    tail = series * t * bell
    area = jnp.where(u >= 0.0, 1.0 - tail, tail)
    return u * area, area + u * (bell * (1.0 / np.sqrt(2.0 * np.pi)))


def norm_stats(values):
    centre = values - jnp.mean(values, axis=-1, keepdims=True)
    spread = jnp.mean(centre * centre, axis=-1, keepdims=True)
    inverse = lax.rsqrt(spread + EPS)
    return centre * inverse, inverse


def norm_back(scaled, unit, inverse):
    first = jnp.mean(scaled, axis=-1, keepdims=True)
    second = jnp.mean(scaled * unit, axis=-1, keepdims=True)
    return (scaled - first - unit * second) * inverse


def mlp_kernel(
    tile,
    steps,
    chunk,
    x_ref,
    att_ref,
    r_ref,
    own_ref,
    recv_ref,
    da_ref,
    dm_ref,
    wp_ref,
    pb_ref,
    g_ref,
    b_ref,
    w1_ref,
    b1_ref,
    w2_ref,
    b2_ref,
    mine_ref,
    other_ref,
    mg_ref,
    og_ref,
    gp_ref,
    gw1_ref,
    gw2_ref,
    small_ref,
    fc1b_ref,
    grid32,
    tokens,
    acc_p,
    acc_1,
    acc_2,
    result,
    n2g,
):
    win, step = pl.program_id(0), pl.program_id(1)
    width = x_ref.shape[-1]

    @pl.when((win == 0) & (step == 0))
    def _():
        acc_p[...] = jnp.zeros_like(acc_p)
        acc_1[...] = jnp.zeros_like(acc_1)
        acc_2[...] = jnp.zeros_like(acc_2)
        small_ref[...] = jnp.zeros_like(small_ref)
        fc1b_ref[...] = jnp.zeros_like(fc1b_ref)

    @pl.when(step == 0)
    def _():
        gather_tokens(own_ref.at[0], win * SHIFT_T, grid32)
        gather_tokens(recv_ref.at[0], SHIFT_T - win * SHIFT_T, grid32)
        grid_to_tokens(grid32, tokens)

    here = pl.ds(pl.multiple_of(step * tile, 16), tile)
    da, dm = da_ref[0], dm_ref[0]
    attended = att_ref[0]
    branch = nn(attended, wp_ref[...]) + pb_ref[...]
    middle = x_ref[0].astype(F32) + by_frame(branch, da)
    unit, inverse = norm_stats(middle)
    normed = (unit * g_ref[...] + b_ref[...]).astype(BF16)
    upstream = tokens[here, :]
    result_grad = by_frame(upstream, dm).astype(BF16)
    small_ref[0] += column_sums(result_grad.astype(F32))
    normed_t = normed.T
    result_grad_t = result_grad.T
    for at in range(0, w1_ref.shape[1], chunk):
        part = slice(at, at + chunk)
        hidden = nn(normed, w1_ref[:, part]) + b1_ref[:, part]
        active, slope = gelu_both(hidden)
        active = active.astype(BF16)
        forward = nn(active, w2_ref[part, :])
        acc_2[:, part] += nn(result_grad_t, active)
        hidden_grad = (nt(result_grad, w2_ref[part, :]) * slope).astype(BF16)
        fc1b_ref[:, part] += column_sums(hidden_grad.astype(F32))
        acc_1[:, part] += nn(normed_t, hidden_grad)
        backward = nt(hidden_grad, w1_ref[:, part])
        if at == 0:
            result[...] = forward
            n2g[...] = backward
        else:
            result[...] += forward
            n2g[...] += backward
    tokens[here, :] = middle + by_frame(result[...] + b2_ref[...], dm)
    normed_grad = n2g[...]
    small_ref[1] += column_sums(normed_grad * unit)
    small_ref[2] += column_sums(normed_grad)
    middle_grad = upstream + norm_back(normed_grad * g_ref[...], unit, inverse)
    mg_ref[0] = middle_grad
    branch_grad = by_frame(middle_grad, da).astype(BF16)
    small_ref[3] += column_sums(branch_grad.astype(F32))
    acc_p[...] += nn(attended.T, branch_grad)
    out_grad = nt(branch_grad, wp_ref[...]).astype(BF16)
    og_ref[0] = (out_grad.astype(F32) * r_ref[0]).astype(BF16)

    @pl.when(step == steps - 1)
    def _():
        tokens_to_grid(tokens, grid32)
        grid_to_frames(grid32, win * SHIFT_T, mine_ref.at[0])
        grid_to_frames(grid32, SHIFT_T - win * SHIFT_T, other_ref.at[0])

    @pl.when((win == 1) & (step == steps - 1))
    def _():
        gp_ref[...] = acc_p[...].astype(BF16)
        gw1_ref[...] = acc_1[...].astype(BF16)
        gw2_ref[...] = acc_2[...].astype(BF16)


def mlp(x, att, inverse, cot, cot_recv, drop_attn, drop_mlp, wp, pb, g, b, w1, b1, w2, b2, tile=400, chunk=512):
    width, hidden = w1.shape
    steps = TOKENS // tile
    frames = pl.BlockSpec((1, WT, 128), lambda w, j: (w, 0, 0))
    return pl.pallas_call(
        functools.partial(mlp_kernel, tile, steps, chunk),
        grid=(2, steps),
        in_specs=[
            tile_spec(tile, width),
            tile_spec(tile, width),
            tile_spec(tile, width),
            half_spec(SIDE, width),
            other_spec(SIDE, width),
            frames,
            frames,
            whole(wp.shape),
            whole((1, width)),
            whole((1, width)),
            whole((1, width)),
            whole(w1.shape),
            whole((1, hidden)),
            whole(w2.shape),
            whole((1, width)),
        ],
        out_specs=[
            half_spec(SIDE, width),
            other_spec(SIDE, width),
            tile_spec(tile, width),
            tile_spec(tile, width),
            whole((width, width)),
            whole((width, hidden)),
            whole((width, hidden)),
            whole((4, 8, width)),
            whole((8, hidden)),
        ],
        out_shape=[
            jax.ShapeDtypeStruct(cot.shape, BF16),
            jax.ShapeDtypeStruct(cot_recv.shape, BF16),
            jax.ShapeDtypeStruct((2, TOKENS, width), F32),
            jax.ShapeDtypeStruct((2, TOKENS, width), BF16),
            jax.ShapeDtypeStruct((width, width), BF16),
            jax.ShapeDtypeStruct((width, hidden), BF16),
            jax.ShapeDtypeStruct((width, hidden), BF16),
            jax.ShapeDtypeStruct((4, 8, width), F32),
            jax.ShapeDtypeStruct((8, hidden), F32),
        ],
        scratch_shapes=[
            pltpu.VMEM((4, WT * FRAME_ROWS, 128), F32),
            pltpu.VMEM((TOKENS, width), F32),
            pltpu.VMEM((width, width), F32),
            pltpu.VMEM((width, hidden), F32),
            pltpu.VMEM((width, hidden), F32),
            pltpu.VMEM((tile, width), F32),
            pltpu.VMEM((tile, width), F32),
        ],
        compiler_params=pltpu.CompilerParams(vmem_limit_bytes=62 << 20),
        name="mlp",
    )(x, att, inverse, cot, cot_recv, drop_attn, drop_mlp, wp, pb[None], g[None], b[None], w1, b1[None], w2, b2[None])


def qkv_back_kernel(
    tile,
    steps,
    dq_ref,
    dk_ref,
    dv_ref,
    n_ref,
    x_ref,
    mg_ref,
    w_ref,
    g_ref,
    mine_ref,
    other_ref,
    gw_ref,
    small_ref,
    grid32,
    tokens,
    acc,
):
    win, step = pl.program_id(0), pl.program_id(1)
    width = x_ref.shape[-1]

    @pl.when((win == 0) & (step == 0))
    def _():
        acc[...] = jnp.zeros_like(acc)
        small_ref[...] = jnp.zeros_like(small_ref)

    here = pl.ds(pl.multiple_of(step * tile, 16), tile)
    dq, dk, dv = dq_ref[0], dk_ref[0], dv_ref[0]
    normed_t = n_ref[0].T
    acc[:, :width] += nn(normed_t, dq)
    acc[:, width : 2 * width] += nn(normed_t, dk)
    acc[:, 2 * width :] += nn(normed_t, dv)
    small_ref[0] += column_sums(dq.astype(F32))
    small_ref[1] += column_sums(dv.astype(F32))
    normed_grad = (
        nt(dq, w_ref[:, :width]) + nt(dk, w_ref[:, width : 2 * width]) + nt(dv, w_ref[:, 2 * width :])
    )
    unit, inverse = norm_stats(x_ref[0].astype(F32))
    small_ref[2] += column_sums(normed_grad * unit)
    small_ref[3] += column_sums(normed_grad)
    tokens[here, :] = mg_ref[0] + norm_back(normed_grad * g_ref[...], unit, inverse)

    @pl.when(step == steps - 1)
    def _():
        tokens_to_grid(tokens, grid32)
        grid_to_frames(grid32, win * SHIFT_T, mine_ref.at[0])
        grid_to_frames(grid32, SHIFT_T - win * SHIFT_T, other_ref.at[0])

    @pl.when((win == 1) & (step == steps - 1))
    def _():
        gw_ref[...] = acc[...].astype(BF16)


def qkv_back(dq, dk, dv, normed, x, middle_grad, w_qkv, gain, tile=400):
    width = x.shape[-1]
    steps = TOKENS // tile
    return pl.pallas_call(
        functools.partial(qkv_back_kernel, tile, steps),
        grid=(2, steps),
        in_specs=[tile_spec(tile, width)] * 6 + [whole(w_qkv.shape), whole((1, width))],
        out_specs=[
            half_spec(SIDE, width),
            other_spec(SIDE, width),
            whole(w_qkv.shape),
            whole((4, 8, width)),
        ],
        out_shape=[
            jax.ShapeDtypeStruct((2, 2 * SHIFT_T, SIDE, SIDE, width), F32),
            jax.ShapeDtypeStruct((2, SHIFT_T, SIDE, SIDE, width), BF16),
            jax.ShapeDtypeStruct(w_qkv.shape, BF16),
            jax.ShapeDtypeStruct((4, 8, width), F32),
        ],
        scratch_shapes=[
            pltpu.VMEM((4, WT * FRAME_ROWS, 128), F32),
            pltpu.VMEM((TOKENS, width), F32),
            pltpu.VMEM(w_qkv.shape, F32),
        ],
        compiler_params=pltpu.CompilerParams(vmem_limit_bytes=60 << 20),
        name="qkv_back",
    )(dq, dk, dv, normed, x, middle_grad, w_qkv, gain[None])


def neighbours():
    count = lax.axis_size("tm")
    down = [(i, i - 1) for i in range(1, count)]
    up = [(i, i + 1) for i in range(count - 1)]
    return count, down, up


def fetch_halves(field):
    count, down, up = neighbours()
    me = lax.axis_index("tm")
    above = lax.ppermute(field[0, :SHIFT_T], "tm", down)
    below = lax.ppermute(field[1, SHIFT_T:], "tm", up)
    above = jnp.where(me == count - 1, field[1, SHIFT_T:], above)
    below = jnp.where(me == 0, field[0, :SHIFT_T], below)
    return jnp.stack([above, below])


def return_halves(mine, other):
    count, down, up = neighbours()
    me = lax.axis_index("tm")
    from_below = lax.ppermute(other[0], "tm", up)
    from_above = lax.ppermute(other[1], "tm", down)
    first = jnp.where(me == 0, other[1], from_below).astype(mine.dtype)
    last = jnp.where(me == count - 1, other[0], from_above).astype(mine.dtype)
    mine = lax.dynamic_update_slice(mine, first[None], (0, 0, 0, 0, 0))
    return lax.dynamic_update_slice(mine, last[None], (1, SHIFT_T, 0, 0, 0))


def frame_facts(segments, keep):
    count = lax.axis_size("tm")
    me = lax.axis_index("tm")
    own = 2 * SHIFT_T
    first = me * own
    t = jnp.arange(SHIFT_T)
    zero, one = jnp.zeros((SHIFT_T,), jnp.int32), jnp.ones((SHIFT_T,), jnp.int32)
    top, bottom = me == count - 1, me == 0
    frames = jnp.stack(
        [
            jnp.concatenate([first + SHIFT_T + t, jnp.where(top, first + SHIFT_T + t, first + own + t)]),
            jnp.concatenate([jnp.where(bottom, t, first - SHIFT_T + t), first + t]),
        ]
    )
    volumes = jnp.stack(
        [jnp.concatenate([zero, jnp.where(top, one, zero)]), jnp.concatenate([jnp.where(bottom, zero, one), one])]
    )
    pick = (frames[:, :, None] == jnp.arange(segments.shape[1])).astype(jnp.int32)
    by_volume = jnp.sum(pick[:, :, None, :] * segments[None, None], axis=-1)
    segment = jnp.where(volumes == 0, by_volume[..., 0], by_volume[..., 1])
    key = segment + 8 * (frames < SHIFT_T) + 16 * volumes
    apart = (key[:, :, None] != key[:, None, :]).astype(F32) * FAR
    far = jnp.tile(apart, (1, 1, 128 // WT))
    seg_hot = (segment[:, :, None] == jnp.arange(keep.shape[2])).astype(F32)
    kept = jnp.where(volumes[:, :, None, None] == 0, keep[0], keep[1]).astype(F32)
    drops = jnp.sum(seg_hot[:, :, None, :] * kept, axis=-1) / KEEP_RATE
    drops = jnp.broadcast_to(drops[..., None], drops.shape + (128,))
    return far, drops[:, :, 0], drops[:, :, 1]


def shards(
    volume,
    segments,
    keep,
    ln1_gain,
    ln1_bias,
    w_qkv,
    q_bias,
    v_bias,
    rel_table,
    w_proj,
    proj_bias,
    ln2_gain,
    ln2_bias,
    w_fc1,
    fc1_bias,
    w_fc2,
    fc2_bias,
    cotangent,
):
    width = volume.shape[-1]
    heads = rel_table.shape[1]
    dim = width // heads
    recv = fetch_halves(volume)
    cot_recv = fetch_halves(cotangent)
    far, drop_attn, drop_mlp = frame_facts(segments, keep)
    biases = make_bias(rel_table)
    qkv_bias = jnp.concatenate([q_bias, jnp.zeros_like(q_bias), v_bias])
    x, normed, q, k, v = make_qkv(volume, recv, ln1_gain, ln1_bias, w_qkv, qkv_bias, dim**-0.5 * LOG2E)
    *exps, att, inverse = attend(q, k, v, far, biases, dim)
    mixed, mixed_other, middle_grad, out_grad, g_proj, g_fc1, g_fc2, small2, small_fc1 = mlp(
        x,
        att,
        inverse,
        cotangent,
        cot_recv,
        drop_attn,
        drop_mlp,
        w_proj,
        proj_bias,
        ln2_gain,
        ln2_bias,
        w_fc1,
        fc1_bias,
        w_fc2,
        fc2_bias,
    )
    mixed_out = return_halves(mixed, mixed_other)
    g_proj, g_fc1, g_fc2 = lax.psum((g_proj, g_fc1, g_fc2), ("dp", "tm"))
    dq, dk, dv, by_rows, by_cols = attend_back(q, k, v, out_grad, att, exps, dim)
    grad, grad_other, g_qkv, small1 = qkv_back(dq, dk, dv, normed, x, middle_grad, w_qkv, ln1_gain)
    volume_grad = return_halves(grad, grad_other)
    shape = (heads, ACROSS, WT, 128)
    by_rows = by_rows.reshape(shape)[..., : ACROSS * WT].reshape(heads, ACROSS, WT, ACROSS, WT)
    by_cols = by_cols.reshape(shape)[..., : ACROSS * WT].reshape(heads, ACROSS, WT, ACROSS, WT)
    table = jnp.einsum("nakbs,ksd->dabn", by_rows, time_hot(), precision=PRECISE) + jnp.einsum(
        "nbkas,ksd->dabn", by_cols, time_hot(), precision=PRECISE
    )
    vectors = jnp.concatenate(
        [
            jnp.sum(small2, axis=1).reshape(-1),
            jnp.sum(small_fc1, axis=0).reshape(-1),
            jnp.sum(small1, axis=1).reshape(-1),
            table.reshape(-1),
        ]
    )
    g_qkv, vectors = lax.psum((g_qkv, vectors), ("dp", "tm"))
    hidden = w_fc1.shape[1]
    small2 = vectors[: 4 * width].reshape(4, width)
    fc1_b = vectors[4 * width : 4 * width + hidden]
    small1 = vectors[4 * width + hidden : 8 * width + hidden].reshape(4, width)
    table = vectors[8 * width + hidden :].reshape(rel_table.shape)
    return (
        mixed_out,
        volume_grad,
        small1[2],
        small1[3],
        g_qkv.astype(F32),
        small1[0],
        small1[1],
        table,
        g_proj.astype(F32),
        small2[3],
        small2[1],
        small2[2],
        g_fc1.astype(F32),
        fc1_b,
        g_fc2.T.astype(F32),
        small2[0],
    )


def solution(mesh):
    split = P("dp", "tm", None, None, None)
    return jax.shard_map(
        shards,
        mesh=mesh,
        in_specs=(split, P("dp", None), P("dp", None, None)) + (P(),) * 14 + (split,),
        out_specs=(split, split) + (P(),) * 14,
        check_vma=False,
    )
```

```python
import functools

import jax
import jax.numpy as jnp
import numpy as np
from jax import lax
from jax.experimental import pallas as pl
from jax.experimental.pallas import tpu as pltpu
from jax.sharding import PartitionSpec as P

SIDE = 14
WT = 8
WIN_HW = 7
SHIFT_T = 4
SHIFT_HW = 3
EPS = 1e-05
KEEP_RATE = 0.75
PRECISE = lax.Precision.HIGHEST
LOG2E = 1.4426950408889634
LN2 = 0.6931471805599453
FAR = 1e30
F32 = jnp.float32
BF16 = jnp.bfloat16

SPANS = (
    (SHIFT_HW, WIN_HW),
    (SHIFT_HW + WIN_HW, SIDE - SHIFT_HW - WIN_HW),
    (0, SHIFT_HW),
)
ACROSS = 2 * WIN_HW - 1
RECTS = (
    (0, 0, True, 0),
    (1, 0, True, 0),
    (0, 1, False, 1),
    (2, 0, True, 0),
    (0, 2, False, 1),
    (2, 2, True, 3),
    (2, 1, True, 2),
    (1, 2, True, 3),
    (1, 1, True, 2),
)
BIAS_DIMS = ((7, 7), (4, 7), (4, 4), (4, 3))


def up_to(value, unit):
    return -(-value // unit) * unit


class Rect:
    pass


def plan_rects():
    rects, slots, start = [], [], 0
    class_rows = [0, 0, 0]
    for row_span, col_span, rows_outer, table in RECTS:
        r0, rn = SPANS[row_span]
        c0, cn = SPANS[col_span]
        rect = Rect()
        if rows_outer:
            places = [(r0 + a, c0 + b) for a in range(rn) for b in range(cn)]
        else:
            places = [(r0 + b, c0 + a) for a in range(cn) for b in range(rn)]
        rect.count = len(places) * WT
        rect.rows = up_to(rect.count, 16)
        rect.lanes = up_to(rect.count, 128)
        rect.start = start
        rect.table = table
        rect.kind = {512: 0, 256: 1, 128: 2}[rect.lanes]
        rect.kind_row = class_rows[rect.kind]
        class_rows[rect.kind] += rect.rows
        slots += places + [None] * ((rect.rows - rect.count) // WT)
        start += rect.rows
        rects.append(rect)
    return rects, slots, class_rows


RECT, SLOTS, KIND_ROWS = plan_rects()
TOKENS = len(SLOTS) * WT
KIND_LANES = (512, 256, 128)
PLACES = SIDE * SIDE


def nn(a, b):
    return lax.dot_general(a, b, (((1,), (0,)), ((), ())), preferred_element_type=F32)


def nt(a, b):
    return lax.dot_general(a, b, (((1,), (1,)), ((), ())), preferred_element_type=F32)


def wide(pattern, width):
    return jnp.concatenate([pattern] * (width // pattern.shape[-1]), axis=-1)


def by_frame(values, pattern):
    rows, width = values.shape
    scaled = values.reshape(rows // WT, WT, width) * wide(pattern, width)[None]
    return scaled.reshape(rows, width)


def column_sums(values):
    rows, width = values.shape
    return jnp.sum(values.reshape(rows // 8, 8, width), axis=0)


def row_half(shape):
    return lax.broadcasted_iota(jnp.int32, shape, 0) % WT < SHIFT_T


def turned(tile):
    return pltpu.roll(tile, SHIFT_T, 0)


def spread_message(message_ref, doubled):
    def pair(i, carry):
        both = message_ref[pl.ds(pl.multiple_of(i * 16, 16), 16), :].astype(F32)
        for k in range(2):
            tile = both[k * WT : k * WT + WT]
            low = row_half(tile.shape)
            swap = turned(tile)
            at = pl.multiple_of(i * 32 + k * 16, 16)
            doubled[pl.ds(at, WT), :] = jnp.where(low, tile, swap)
            doubled[pl.ds(at + WT, WT), :] = jnp.where(low, swap, tile)
        return carry

    lax.fori_loop(0, message_ref.shape[0] // 16, pair, 0)


def assemble_tokens(win, edge_ref, own_ref, alt_ref, above_ref, below_ref, doubled, tokens):
    @pl.when(win == 0)
    def _():
        spread_message(above_ref, doubled)

    @pl.when(win == 1)
    def _():
        spread_message(below_ref, doubled)

    width = tokens.shape[1]
    own_low = row_half((WT, width)) == (win == 0)
    edge = edge_ref[win] == 1
    for slot, place in enumerate(SLOTS):
        rows = slice(slot * WT, slot * WT + WT)
        if place is None:
            tokens[rows, :] = jnp.zeros((WT, width), F32)
            continue
        h, w = place
        at = (h * SIDE + w) * WT
        own = turned(own_ref[0, h, w].astype(F32))
        other = jnp.where(edge, alt_ref[0, h, w].astype(F32), doubled[at : at + WT, :])
        tokens[rows, :] = jnp.where(own_low, own, other)


def pack_message(win, tokens, first, count, message_ref):
    def pair(i, carry):
        both = tokens[pl.ds(pl.multiple_of(first + i * 32, 16), 32), :]
        tiles = []
        for k in range(2):
            one, two = both[k * 16 : k * 16 + WT], both[k * 16 + WT : k * 16 + 16]
            low = row_half(one.shape)
            late = jnp.where(low, turned(one), two)
            early = jnp.where(low, one, turned(two))
            tiles.append(jnp.where(win == 0, late, early))
        message_ref[pl.ds(pl.multiple_of(i * 16, 16), 16), :] = jnp.concatenate(tiles, axis=0).astype(
            message_ref.dtype
        )
        return carry

    lax.fori_loop(0, count // 32, pair, 0)


def spread_table(source, outer, inner, out_ref, lane):
    width = inner * WT
    total = outer * width
    for ok in range(outer):
        for ik in range(inner):
            pieces = []
            for oq in range(outer):
                shift = (oq * width - (WIN_HW - 1 - ik) * WT) % 128
                piece = source[oq - ok + WIN_HW - 1]
                pieces.append(pltpu.roll(piece, shift, 1) if shift else piece)
            row = (ok * inner + ik) * WT
            for tile in range(up_to(total, 128) // 128):
                value = None
                for oq in range(outer):
                    begin, end = oq * width, (oq + 1) * width
                    if end <= tile * 128 or begin >= tile * 128 + 128:
                        continue
                    if value is None:
                        value = pieces[oq]
                    else:
                        value = jnp.where(lane >= begin - tile * 128, pieces[oq], value)
                out_ref[0, row : row + WT, tile * 128 : tile * 128 + 128] = value


def split3(values):
    parts = []
    for _ in range(3):
        part = values.astype(BF16)
        parts.append(part)
        values = values - part.astype(F32)
    return parts


def hot_times(tk):
    count = ACROSS * (2 * WT - 1)
    place = lax.broadcasted_iota(jnp.int32, (count, 128), 0)
    lane = lax.broadcasted_iota(jnp.int32, (count, 128), 1)
    return ((lane // WT) * (2 * WT - 1) + lane % WT - tk + WT - 1 == place).astype(BF16)


def bias_kernel(rows_ref, cols_ref, b0_ref, b1_ref, b2_ref, b3_ref, strips):
    head = pl.program_id(0)

    @pl.when(head == 0)
    def _():
        for kind, table_ref in enumerate((rows_ref, cols_ref)):
            parts = split3(table_ref[...] * LOG2E)
            for tk in range(WT):
                hot = hot_times(tk)
                strips[kind, pl.ds(tk, table_ref.shape[0], stride=WT), :] = sum(nn(p, hot) for p in parts)

    lane = lax.broadcasted_iota(jnp.int32, (WT, 128), 1)
    base = pl.multiple_of(head * (ACROSS * WT), WT)
    by_rows = [strips[0, pl.ds(base + d * WT, WT), :] for d in range(ACROSS)]
    by_cols = [strips[1, pl.ds(base + d * WT, WT), :] for d in range(ACROSS)]
    for out_ref, source, (outer, inner) in zip(
        (b0_ref, b1_ref, b2_ref, b3_ref), (by_rows, by_cols, by_rows, by_rows), BIAS_DIMS
    ):
        spread_table(source, outer, inner, out_ref, lane)


def bias_shapes(heads):
    shapes = []
    for outer, inner in BIAS_DIMS:
        count = outer * inner * WT
        shapes.append((heads, count, up_to(count, 128)))
    return shapes


def make_bias(rel_table):
    heads = rel_table.shape[1]
    times = 2 * WT - 1
    cube = rel_table.T.reshape(heads, times, ACROSS, ACROSS)
    by_rows = cube.transpose(0, 2, 3, 1).reshape(heads * ACROSS, ACROSS * times)
    by_cols = cube.transpose(0, 3, 2, 1).reshape(heads * ACROSS, ACROSS * times)
    shapes = bias_shapes(heads)
    return pl.pallas_call(
        bias_kernel,
        grid=(heads,),
        in_specs=[whole(by_rows.shape), whole(by_cols.shape)],
        out_specs=[pl.BlockSpec((1,) + s[1:], lambda h: (h, 0, 0)) for s in shapes],
        out_shape=[jax.ShapeDtypeStruct(s, F32) for s in shapes],
        scratch_shapes=[pltpu.VMEM((2, heads * ACROSS * WT, 128), F32)],
        compiler_params=pltpu.CompilerParams(vmem_limit_bytes=48 << 20),
        cost_estimate=cost(10),
        name="position_bias",
    )(by_rows, by_cols)


def fold_table(acc, outer, inner, totals, lane):
    width = inner * WT
    for ok in range(outer):
        for ik in range(inner):
            row = (ok * inner + ik) * WT
            for oq in range(outer):
                shift = (oq * width - (WIN_HW - 1 - ik) * WT) % 128
                begin, end = oq * width, (oq + 1) * width
                tile, lo = begin // 128, begin % 128
                last = (end - 1) // 128
                value = acc(row, tile)
                if last == tile:
                    value = jnp.where((lane >= lo) & (lane < lo + width), value, 0.0)
                else:
                    after = jnp.where(lane < end - last * 128, acc(row, last), 0.0)
                    value = jnp.where(lane >= lo, value, after)
                d = oq - ok + WIN_HW - 1
                back = pltpu.roll(value, (128 - shift) % 128, 1) if shift else value
                totals[d] = totals[d] + back


def qkv_kernel(
    tile,
    scale,
    edge_ref,
    own_ref,
    alt_ref,
    above_ref,
    below_ref,
    gain_ref,
    bias_ref,
    w_ref,
    wb_ref,
    x_ref,
    n_ref,
    q_ref,
    k_ref,
    v_ref,
    doubled,
    tokens,
):
    win, step = pl.program_id(0), pl.program_id(1)

    @pl.when(step == 0)
    def _():
        assemble_tokens(win, edge_ref, own_ref, alt_ref, above_ref, below_ref, doubled, tokens)

    x = tokens[pl.ds(pl.multiple_of(step * tile, 16), tile), :]
    x_ref[0] = x.astype(BF16)
    unit, _ = norm_stats(x)
    n_ref[0] = unit.astype(BF16)
    normed = (unit * gain_ref[...] + bias_ref[...]).astype(BF16)
    width = x.shape[1]
    q_ref[0] = ((nn(normed, w_ref[:, :width]) + wb_ref[:, :width]) * scale).astype(BF16)
    k_ref[0] = nn(normed, w_ref[:, width : 2 * width]).astype(BF16)
    v_ref[0] = (nn(normed, w_ref[:, 2 * width :]) + wb_ref[:, 2 * width :]).astype(BF16)


def cost(micros):
    return pl.CostEstimate(flops=int(micros * 1.1e9), bytes_accessed=1 << 20, transcendentals=0)


def norm_stats(values):
    centre = values - jnp.mean(values, axis=-1, keepdims=True)
    spread = jnp.mean(centre * centre, axis=-1, keepdims=True)
    inverse = lax.rsqrt(spread + EPS)
    return centre * inverse, inverse


def norm_back(scaled, unit, inverse):
    first = jnp.mean(scaled, axis=-1, keepdims=True)
    second = jnp.mean(scaled * unit, axis=-1, keepdims=True)
    return (scaled - first - unit * second) * inverse


def whole(shape):
    return pl.BlockSpec(shape, lambda *_: (0,) * len(shape))


def scalars():
    return pl.BlockSpec(memory_space=pltpu.SMEM)


def volume_specs(width):
    block = (1, SIDE, SIDE, WT, width)
    return [
        pl.BlockSpec(block, lambda w, *_: (w, 0, 0, 0, 0)),
        pl.BlockSpec(block, lambda w, *_: (1 - w, 0, 0, 0, 0)),
        whole((PLACES * SHIFT_T, width)),
        whole((PLACES * SHIFT_T, width)),
    ]


def tile_spec(tile, width):
    return pl.BlockSpec((1, tile, width), lambda w, j: (w, j, 0))


def make_qkv(edges, volume, above, below, gain, bias, w_qkv, qkv_bias, scale, tile=400):
    width = volume.shape[-1]
    out = jax.ShapeDtypeStruct((2, TOKENS, width), BF16)
    return pl.pallas_call(
        functools.partial(qkv_kernel, tile, scale),
        grid=(2, TOKENS // tile),
        in_specs=[scalars()]
        + volume_specs(width)
        + [whole((1, width)), whole((1, width)), whole(w_qkv.shape), whole((1, 3 * width))],
        out_specs=[tile_spec(tile, width)] * 5,
        out_shape=[out] * 5,
        scratch_shapes=[
            pltpu.VMEM((PLACES * WT, width), F32),
            pltpu.VMEM((TOKENS, width), F32),
        ],
        compiler_params=pltpu.CompilerParams(vmem_limit_bytes=60 << 20),
        cost_estimate=cost(17),
        name="norm1_qkv",
    )(edges, volume, volume, above, below, gain[None], bias[None], w_qkv, qkv_bias[None])


def head_rows(transposed, head, dim):
    rows, lanes = transposed.shape
    parts = []
    if head:
        parts.append(jnp.zeros((head * dim, lanes), transposed.dtype))
    parts.append(transposed[head * dim : head * dim + dim])
    if (head + 1) * dim < rows:
        parts.append(jnp.zeros((rows - (head + 1) * dim, lanes), transposed.dtype))
    return jnp.concatenate(parts, axis=0)


def attend_kernel(
    dim, q_ref, k_ref, v_ref, far_ref, b0, b1, b2, b3, e0_ref, e1_ref, e2_ref, o_ref, r_ref, scores
):
    biases = (b0, b1, b2, b3)
    e_refs = (e0_ref, e1_ref, e2_ref)
    far = far_ref[0]
    per = 128 // dim
    for rect in RECT:
        count, rows, lanes, start = rect.count, rect.rows, rect.lanes, rect.start
        kind_rows = slice(rect.kind_row, rect.kind_row + rows)
        e_ref = e_refs[rect.kind]
        queries = q_ref[0, start : start + lanes, :].T
        keys = k_ref[0, start : start + rows, :]
        values = v_ref[0, start : start + rows, :].T
        ones = jnp.ones((16, rows), BF16)
        wide_far = wide(far, lanes)
        outs, scales = [], []
        for head in range(per):
            raw = nn(keys, head_rows(queries, head, dim))[:count]
            raw = raw + biases[rect.table][head, :count, :lanes]
            scores[:count, :lanes] = raw
            blocks = raw.reshape(count // 8, 8, lanes)
            top = jnp.max(blocks, axis=0) - wide_far
            top = jnp.max(top, axis=0, keepdims=True) + wide_far
            exps = jnp.exp2(scores[:count, :lanes].reshape(count // 8, 8, lanes) - top[None])
            exps = exps.reshape(count, lanes).astype(BF16)
            if rows > count:
                exps = jnp.concatenate([exps, jnp.zeros((rows - count, lanes), BF16)], axis=0)
            e_ref[0, 0, kind_rows, head * lanes : head * lanes + lanes] = exps
            lhs = jnp.concatenate([values[head * dim : head * dim + dim], ones], axis=0)
            out = nn(lhs, exps)
            inverse = jnp.broadcast_to(1.0 / out[dim : dim + 1], (dim, lanes))
            outs.append(out[:dim] * inverse)
            scales.append(inverse)
        o_ref[0, start : start + rows, :] = jnp.concatenate(outs, axis=0).T[:rows].astype(BF16)
        r_ref[0, start : start + rows, :] = jnp.concatenate(scales, axis=0).T[:rows]


def head_group_specs(heads, per, biases):
    lane_tile = pl.BlockSpec((1, TOKENS, 128), lambda g, w: (w, 0, g))
    far = pl.BlockSpec((1, WT, 128), lambda g, w: (w, 0, 0))
    bias = [pl.BlockSpec((per,) + b[1:], lambda g, w: (g, 0, 0)) for b in biases]
    exps = [
        pl.BlockSpec((1, 1, KIND_ROWS[i], per * KIND_LANES[i]), lambda g, w: (w, g, 0, 0)) for i in range(3)
    ]
    return lane_tile, far, bias, exps


def exps_shapes(groups, per):
    return [jax.ShapeDtypeStruct((2, groups, KIND_ROWS[i], per * KIND_LANES[i]), BF16) for i in range(3)]


def attend(q, k, v, far, biases, dim):
    width = q.shape[-1]
    heads = width // dim
    per = 128 // dim
    groups = heads // per
    lane_tile, far_spec, bias_specs, exps_specs = head_group_specs(heads, per, [b.shape for b in biases])
    return pl.pallas_call(
        functools.partial(attend_kernel, dim),
        grid=(groups, 2),
        in_specs=[lane_tile] * 3 + [far_spec] + bias_specs,
        out_specs=exps_specs + [lane_tile, lane_tile],
        out_shape=exps_shapes(groups, per)
        + [jax.ShapeDtypeStruct((2, TOKENS, width), BF16), jax.ShapeDtypeStruct((2, TOKENS, width), F32)],
        scratch_shapes=[pltpu.VMEM((RECT[0].count, RECT[0].lanes), F32)],
        compiler_params=pltpu.CompilerParams(vmem_limit_bytes=60 << 20),
        cost_estimate=cost(55),
        name="attention",
    )(q, k, v, far, *biases)


def attend_back_kernel(
    dim,
    scale,
    q_ref,
    k_ref,
    v_ref,
    g_ref,
    o_ref,
    n_ref,
    e0_ref,
    e1_ref,
    e2_ref,
    d_ref,
    gw_ref,
    sums_ref,
    rows_ref,
    cols_ref,
    a0,
    a1,
    a2,
    a3,
    grads,
    queries,
    outgrads,
    acc_w,
    strips,
):
    win = pl.program_id(0)
    accs = (a0, a1, a2, a3)
    e_refs = (e0_ref, e1_ref, e2_ref)
    per = 128 // dim
    lane = lax.broadcasted_iota(jnp.int32, (16, 128), 1)

    @pl.when(win == 0)
    def _():
        for acc in accs:
            acc[...] = jnp.zeros_like(acc)
        acc_w[...] = jnp.zeros_like(acc_w)
        sums_ref[...] = jnp.zeros_like(sums_ref)

    for rect in RECT:
        count, rows, lanes, start = rect.count, rect.rows, rect.lanes, rect.start
        kind_rows = slice(rect.kind_row, rect.kind_row + rows)
        e_ref = e_refs[rect.kind]
        keys = k_ref[0, start : start + rows, :]
        values = v_ref[0, start : start + rows, :]
        out_grad = g_ref[0, start : start + rows, :]
        if lanes > rows:
            out_grad = jnp.concatenate([out_grad, jnp.zeros((lanes - rows, 128), BF16)], axis=0)
        query = q_ref[0, start : start + lanes, :]
        out_grad_t = out_grad.T
        out_t = o_ref[0, start : start + lanes, :].T
        keys_t = keys.T
        product = out_grad_t.astype(F32) * out_t.astype(F32)
        dqs = []
        for head in range(per):
            here = slice(head * lanes, head * lanes + lanes)
            mine = ((lane[:1] >= head * dim) & (lane[:1] < head * dim + dim)).astype(BF16)
            queries[here, :] = query * mine
            outgrads[here, :] = out_grad * mine
            inner = jnp.sum(product[head * dim : head * dim + dim], axis=0, keepdims=True)
            prob_grad = nn(values, head_rows(out_grad_t, head, dim))
            exps = e_ref[0, 0, kind_rows, here].astype(F32)
            score_grad = exps * (prob_grad - inner)
            low = score_grad.astype(BF16)
            accs[rect.table][head, :count, :lanes] += score_grad[:count]
            grads[:rows, here] = low
            dqs.append(nn(keys_t[head * dim : head * dim + dim], low))
        dq = jnp.concatenate(dqs, axis=0) * scale
        d_ref[0, start : start + rows, :128] = dq.T[:rows].astype(BF16)
        dk = nn(grads[:rows, : per * lanes], queries[: per * lanes, :])
        d_ref[0, start : start + rows, 128:256] = (dk * LN2).astype(BF16)
        dv = nn(e_ref[0, 0, kind_rows, :], outgrads[: per * lanes, :])
        d_ref[0, start : start + rows, 256:] = dv.astype(BF16)

    all_grads = d_ref[0]
    acc_w[...] += lax.dot_general(n_ref[0], all_grads, (((0,), (0,)), ((), ())), preferred_element_type=F32)
    sums_ref[...] += column_sums(all_grads.astype(F32))

    @pl.when(win == 1)
    def _():
        gw_ref[...] = acc_w[...].astype(BF16)
        lane8 = lax.broadcasted_iota(jnp.int32, (WT, 128), 1)
        for head in range(per):
            by_rows = [jnp.zeros((WT, 128), F32) for _ in range(ACROSS)]
            by_cols = [jnp.zeros((WT, 128), F32) for _ in range(ACROSS)]
            for acc, totals, (outer, inner) in zip(accs, (by_rows, by_cols, by_rows, by_rows), BIAS_DIMS):
                fold_table(
                    lambda row, tile: acc[head, row : row + WT, tile * 128 : tile * 128 + 128],
                    outer,
                    inner,
                    totals,
                    lane8,
                )
            for d in range(ACROSS):
                strips[0, (head * ACROSS + d) * WT : (head * ACROSS + d + 1) * WT, :] = by_rows[d]
                strips[1, (head * ACROSS + d) * WT : (head * ACROSS + d + 1) * WT, :] = by_cols[d]
        for kind, out_ref in enumerate((rows_ref, cols_ref)):
            total = jnp.zeros(out_ref.shape, F32)
            for tk in range(WT):
                hot = hot_times(tk)
                for part in split3(strips[kind, pl.ds(tk, per * ACROSS, stride=WT), :]):
                    total = total + nt(part, hot)
            out_ref[...] = total


def attend_back(group, q, k, v, out_grad, out, unit, exps, dim):
    width = q.shape[-1]
    per = 128 // dim
    shapes = bias_shapes(per)
    lane_tile = pl.BlockSpec((1, TOKENS, 128), lambda w: (w, 0, group))
    exps_specs = [
        pl.BlockSpec((1, 1, KIND_ROWS[i], per * KIND_LANES[i]), lambda w: (w, group, 0, 0)) for i in range(3)
    ]
    times = 2 * WT - 1
    strip = (per * ACROSS, ACROSS * times)
    most = per * RECT[0].lanes
    return pl.pallas_call(
        functools.partial(attend_back_kernel, dim, dim**-0.5),
        grid=(2,),
        in_specs=[lane_tile] * 5 + [pl.BlockSpec((1, TOKENS, width), lambda w: (w, 0, 0))] + exps_specs,
        out_specs=[
            pl.BlockSpec((1, TOKENS, 384), lambda w: (w, 0, 0)),
            whole((width, 384)),
            whole((8, 384)),
            whole(strip),
            whole(strip),
        ],
        out_shape=[
            jax.ShapeDtypeStruct((2, TOKENS, 384), BF16),
            jax.ShapeDtypeStruct((width, 384), BF16),
            jax.ShapeDtypeStruct((8, 384), F32),
            jax.ShapeDtypeStruct(strip, F32),
            jax.ShapeDtypeStruct(strip, F32),
        ],
        scratch_shapes=[pltpu.VMEM(s, F32) for s in shapes]
        + [
            pltpu.VMEM((RECT[0].rows, most), BF16),
            pltpu.VMEM((most, 128), BF16),
            pltpu.VMEM((most, 128), BF16),
            pltpu.VMEM((width, 384), F32),
            pltpu.VMEM((2, per * ACROSS * WT, 128), F32),
        ],
        compiler_params=pltpu.CompilerParams(vmem_limit_bytes=60 << 20),
        cost_estimate=cost(20),
        name="attention_back",
    )(q, k, v, out_grad, out, unit, *exps)


ERFC = (0.254829592, -0.284496736, 1.421413741, -1.453152027, 1.061405429)
ERFC_P = 0.3275911


def gelu_both(u):
    t = 1.0 / (1.0 + (ERFC_P * 0.5**0.5) * jnp.abs(u))
    bell = jnp.exp2((u * u) * (-0.5 * LOG2E))
    series = 0.5 * ERFC[4]
    for factor in ERFC[3::-1]:
        series = series * t + 0.5 * factor
    tail = series * t * bell
    area = jnp.where(u >= 0.0, 1.0 - tail, tail)
    return u * area, area + u * (bell * (1.0 / np.sqrt(2.0 * np.pi)))


def mlp_kernel(
    tile,
    steps,
    chunk,
    edge_ref,
    x_ref,
    att_ref,
    r_ref,
    own_ref,
    alt_ref,
    above_ref,
    below_ref,
    da_ref,
    dm_ref,
    wp_ref,
    pb_ref,
    g_ref,
    b_ref,
    w1_ref,
    b1_ref,
    w2_ref,
    b2_ref,
    mixed_ref,
    message_ref,
    mg_ref,
    og_ref,
    gw_ref,
    small_ref,
    fc1b_ref,
    doubled,
    tokens,
    acc_p,
    acc_1,
    acc_2,
    result,
    n2g,
):
    win, step = pl.program_id(0), pl.program_id(1)
    width = x_ref.shape[-1]

    @pl.when((win == 0) & (step == 0))
    def _():
        acc_p[...] = jnp.zeros_like(acc_p)
        acc_1[...] = jnp.zeros_like(acc_1)
        acc_2[...] = jnp.zeros_like(acc_2)
        small_ref[...] = jnp.zeros_like(small_ref)
        fc1b_ref[...] = jnp.zeros_like(fc1b_ref)

    @pl.when(step == 0)
    def _():
        assemble_tokens(win, edge_ref, own_ref, alt_ref, above_ref, below_ref, doubled, tokens)

    here = pl.ds(pl.multiple_of(step * tile, 16), tile)
    da, dm = da_ref[0], dm_ref[0]
    attended = att_ref[0]
    branch = nn(attended, wp_ref[...]) + pb_ref[...]
    middle = x_ref[0].astype(F32) + by_frame(branch, da)
    unit, inverse = norm_stats(middle)
    normed = (unit * g_ref[...] + b_ref[...]).astype(BF16)
    upstream = tokens[here, :]
    result_grad = by_frame(upstream, dm).astype(BF16)
    small_ref[0] += column_sums(result_grad.astype(F32))
    normed_t = normed.T
    result_grad_t = result_grad.T
    for at in range(0, w1_ref.shape[1], chunk):
        part = slice(at, at + chunk)
        hidden = nn(normed, w1_ref[:, part]) + b1_ref[:, part]
        active, slope = gelu_both(hidden)
        active = active.astype(BF16)
        forward = nn(active, w2_ref[part, :])
        acc_2[:, part] += nn(result_grad_t, active)
        hidden_grad = (nt(result_grad, w2_ref[part, :]) * slope).astype(BF16)
        fc1b_ref[:, part] += column_sums(hidden_grad.astype(F32))
        acc_1[:, part] += nn(normed_t, hidden_grad)
        backward = nt(hidden_grad, w1_ref[:, part])
        if at == 0:
            result[...] = forward
            n2g[...] = backward
        else:
            result[...] += forward
            n2g[...] += backward
    mixed = middle + by_frame(result[...] + b2_ref[...], dm)
    mixed_ref[0] = mixed.astype(BF16)
    tokens[here, :] = mixed
    normed_grad = n2g[...]
    small_ref[1] += column_sums(normed_grad * unit)
    small_ref[2] += column_sums(normed_grad)
    middle_grad = upstream + norm_back(normed_grad * g_ref[...], unit, inverse)
    mg_ref[0] = middle_grad
    branch_grad = by_frame(middle_grad, da).astype(BF16)
    small_ref[3] += column_sums(branch_grad.astype(F32))
    acc_p[...] += nn(attended.T, branch_grad)
    out_grad = nt(branch_grad, wp_ref[...]).astype(BF16)
    og_ref[0] = (out_grad.astype(F32) * r_ref[0]).astype(BF16)

    @pl.when(step == steps - 1)
    def _():
        pack_message(win, tokens, 0, TOKENS, message_ref.at[0])

    @pl.when((win == 1) & (step == steps - 1))
    def _():
        blocks = acc_1.shape[1] // width
        for i in range(blocks):
            part = slice(i * width, i * width + width)
            gw_ref[part, :] = acc_1[:, part].astype(BF16)
            gw_ref[(blocks + i) * width : (blocks + i + 1) * width, :] = acc_2[:, part].T.astype(BF16)
        gw_ref[2 * blocks * width :, :] = acc_p[...].astype(BF16)


def mlp(
    edges, x, att, inverse, cot, above, below, drop_attn, drop_mlp, wp, pb, g, b, w1, b1, w2, b2, tile=400, chunk=512
):
    width, hidden = w1.shape
    steps = TOKENS // tile
    frames = pl.BlockSpec((1, WT, 128), lambda w, j: (w, 0, 0))
    return pl.pallas_call(
        functools.partial(mlp_kernel, tile, steps, chunk),
        grid=(2, steps),
        in_specs=[scalars(), tile_spec(tile, width), tile_spec(tile, width), tile_spec(tile, width)]
        + volume_specs(width)
        + [
            frames,
            frames,
            whole(wp.shape),
            whole((1, width)),
            whole((1, width)),
            whole((1, width)),
            whole(w1.shape),
            whole((1, hidden)),
            whole(w2.shape),
            whole((1, width)),
        ],
        out_specs=[
            tile_spec(tile, width),
            pl.BlockSpec((1, TOKENS // 2, width), lambda w, j: (w, 0, 0)),
            tile_spec(tile, width),
            tile_spec(tile, width),
            whole((2 * hidden + width, width)),
            whole((4, 8, width)),
            whole((8, hidden)),
        ],
        out_shape=[
            jax.ShapeDtypeStruct((2, TOKENS, width), BF16),
            jax.ShapeDtypeStruct((2, TOKENS // 2, width), BF16),
            jax.ShapeDtypeStruct((2, TOKENS, width), F32),
            jax.ShapeDtypeStruct((2, TOKENS, width), BF16),
            jax.ShapeDtypeStruct((2 * hidden + width, width), BF16),
            jax.ShapeDtypeStruct((4, 8, width), F32),
            jax.ShapeDtypeStruct((8, hidden), F32),
        ],
        scratch_shapes=[
            pltpu.VMEM((PLACES * WT, width), F32),
            pltpu.VMEM((TOKENS, width), F32),
            pltpu.VMEM((width, width), F32),
            pltpu.VMEM((width, hidden), F32),
            pltpu.VMEM((width, hidden), F32),
            pltpu.VMEM((tile, width), F32),
            pltpu.VMEM((tile, width), F32),
        ],
        compiler_params=pltpu.CompilerParams(vmem_limit_bytes=63 << 20),
        cost_estimate=cost(100),
        name="mlp",
    )(
        edges,
        x,
        att,
        inverse,
        cot,
        cot,
        above,
        below,
        drop_attn,
        drop_mlp,
        wp,
        pb[None],
        g[None],
        b[None],
        w1,
        b1[None],
        w2,
        b2[None],
    )


def qkv_back_kernel(d0, d1, d2, d3, x_ref, mg_ref, w_ref, g_ref, out_ref, message_ref, tokens):
    win = pl.program_id(0)
    grads = jnp.concatenate([d[0] for d in (d0, d1, d2, d3)], axis=-1)
    normed_grad = nt(grads, w_ref[...])
    unit, inverse = norm_stats(x_ref[0].astype(F32))
    grad = mg_ref[0] + norm_back(normed_grad * g_ref[...], unit, inverse)
    out_ref[0] = grad
    tokens[...] = grad
    pack_message(win, tokens, 0, tokens.shape[0], message_ref.at[0])


def qkv_back(part, grads, x, middle_grad, w_groups, gain):
    width = x.shape[-1]
    rows = TOKENS // 2
    tile = pl.BlockSpec((1, rows, width), lambda w: (w, part, 0))
    grad = pl.BlockSpec((1, rows, 384), lambda w: (w, part, 0))

    def kernel(*refs):
        qkv_back_kernel(*refs)

    return pl.pallas_call(
        kernel,
        grid=(2,),
        in_specs=[grad] * 4 + [tile] * 2 + [whole(w_groups.shape), whole((1, width))],
        out_specs=[
            pl.BlockSpec((1, rows, width), lambda w: (w, 0, 0)),
            pl.BlockSpec((1, rows // 2, width), lambda w: (w, 0, 0)),
        ],
        out_shape=[
            jax.ShapeDtypeStruct((2, rows, width), F32),
            jax.ShapeDtypeStruct((2, rows // 2, width), BF16),
        ],
        scratch_shapes=[pltpu.VMEM((rows, width), F32)],
        compiler_params=pltpu.CompilerParams(vmem_limit_bytes=60 << 20),
        cost_estimate=cost(11),
        name="qkv_back",
    )(*grads, x, middle_grad, w_groups, gain[None])


def place_kernel(parts, edge_ref, *refs):
    vol = pl.program_id(0)
    owns, alts = refs[:parts], refs[parts : 2 * parts]
    belows, aboves = refs[2 * parts : 3 * parts], refs[3 * parts : 4 * parts]
    out_ref, doubled = refs[4 * parts :]
    size = TOKENS // parts
    for part in range(parts):

        @pl.when(vol == 0)
        def _():
            spread_message(belows[part], doubled.at[pl.ds(part * size, size)])

        @pl.when(vol == 1)
        def _():
            spread_message(aboves[part], doubled.at[pl.ds(part * size, size)])

    width = out_ref.shape[-1]
    low = row_half((WT, width)) == (vol == 0)
    edge = edge_ref[vol] == 1
    for slot, place in enumerate(SLOTS):
        if place is None:
            continue
        part, at = slot * WT // size, slot * WT % size
        own = turned(owns[part][0, at : at + WT, :].astype(F32))
        alt = alts[part][0, at : at + WT, :].astype(F32)
        other = jnp.where(edge, alt, doubled[slot * WT : slot * WT + WT, :])
        out_ref[0, place[0], place[1]] = jnp.where(low, other, own).astype(out_ref.dtype)


def to_frames(edges, tokens, belows, aboves):
    parts = len(tokens)
    size = TOKENS // parts
    width = tokens[0].shape[-1]
    dtype = tokens[0].dtype
    lanes = 256
    own = pl.BlockSpec((1, size, lanes), lambda v, c: (v, 0, c))
    alt = pl.BlockSpec((1, size, lanes), lambda v, c: (1 - v, 0, c))
    message = pl.BlockSpec((size // 2, lanes), lambda v, c: (0, c))
    return pl.pallas_call(
        functools.partial(place_kernel, parts),
        grid=(2, width // lanes),
        in_specs=[scalars()] + [own] * parts + [alt] * parts + [message] * (2 * parts),
        out_specs=pl.BlockSpec((1, SIDE, SIDE, WT, lanes), lambda v, c: (v, 0, 0, 0, c)),
        out_shape=jax.ShapeDtypeStruct((2, SIDE, SIDE, WT, width), dtype),
        scratch_shapes=[pltpu.VMEM((TOKENS, lanes), F32)],
        compiler_params=pltpu.CompilerParams(vmem_limit_bytes=60 << 20),
        cost_estimate=cost(6),
        name="to_frames",
    )(edges, *tokens, *tokens, *belows, *aboves)


def tie(value, *after):
    return lax.optimization_barrier((value,) + after)[0]


def pick(array, index, axis=0):
    return lax.dynamic_index_in_dim(array, index, axis, keepdims=False)


def add_low(*values):
    return sum(v.astype(F32) for v in values).astype(BF16)


class Sum:
    def __init__(self, buffer):
        self.n = lax.axis_size("tm")
        self.size = lax.axis_size("dp")
        self.m = self.size // 2
        dp = lax.axis_index("dp")
        self.core, self.chip, self.plane = dp % 2, dp // 2, lax.axis_index("tm")
        rows, width = buffer.shape
        self.piece = (rows // (2 * self.m * self.n), width)
        self.whole = buffer.reshape((self.m, 2, self.n) + self.piece)

    def to_core(self, values):
        return lax.ppermute(values, "dp", [(i, i ^ 1) for i in range(self.size)])

    def to_chip(self, values, s):
        return lax.ppermute(values, "dp", [(i, i ^ (2 * s)) for i in range(self.size)])

    def to_plane(self, values, s):
        return lax.ppermute(values, "tm", [(i, i ^ s) for i in range(self.n)])

    def step0(self):
        self.got = self.to_core(pick(self.whole, 1 - self.core, 1))
        return self

    def step1(self):
        mine = pick(self.whole, self.core, 1)
        parts = [add_low(pick(mine, self.chip ^ s), pick(self.got, self.chip ^ s)) for s in range(self.m)]
        self.mine = parts[0]
        self.got = [self.to_chip(parts[s], s) for s in range(1, self.m)]
        return parts[-1]

    def step2(self):
        total = add_low(self.mine, *self.got)
        parts = [pick(total, self.plane ^ s) for s in range(self.n)]
        self.mine = parts[0]
        self.got = [self.to_plane(parts[s], s) for s in range(1, self.n)]
        return parts[-1]

    def step3(self):
        self.mine = add_low(self.mine, *self.got)
        return self.mine

    def gathered(self):
        return lax.all_gather(self.mine, ("dp", "tm"), tiled=True)

    def step3_back(self):
        self.step3()
        self.got = [self.to_plane(self.mine, s) for s in range(1, self.n)]
        return self.mine

    def step4_back(self):
        self.mine = jnp.stack([self.mine] + self.got)
        self.got = [self.to_chip(self.mine, s) for s in range(1, self.m)]
        return self.mine

    def step5_back(self):
        self.mine = jnp.stack([self.mine] + self.got)
        self.other = self.to_core(self.mine)
        return self.mine


def finish_kernel(m, n, groups, ids_ref, mine_ref, other_ref, w_ref, gain_ref, bias_ref, gw_ref, lg_ref, lb_ref, extra_ref, total):
    core, chip, plane = ids_ref[0], ids_ref[1], ids_ref[2]
    rows = mine_ref.shape[1]
    for c in range(m):
        for k in range(2):
            for z in range(n):
                at = (chip ^ c) * n + (plane ^ z)
                block = jnp.where(core == k, mine_ref[at].astype(F32), other_ref[at].astype(F32))
                first = ((c * 2 + k) * n + z) * rows
                total[first : first + rows, :] = block
    width = w_ref.shape[0]
    step = total.shape[1]
    lane_sum = jnp.zeros((width, 128), F32)
    bias_sum = jnp.zeros((width, 128), F32)
    gain = gain_ref[...]
    bias = bias_ref[...]
    for g in range(groups):
        part = total[g * width : (g + 1) * width, :]
        sums = total[groups * width + g : groups * width + g + 1, :]
        grad = gain * part + bias * sums
        for third in range(3):
            lanes = slice(third * 128, third * 128 + 128)
            at = third * width + g * 128
            gw_ref[:, at : at + 128] = grad[:, lanes]
            weight = w_ref[:, at : at + 128].astype(F32)
            lane_sum = lane_sum + weight * part[:, lanes]
            bias_sum = bias_sum + weight * sums[:, lanes]
    lg_ref[...] = jnp.sum(lane_sum, axis=1, keepdims=True)
    lb_ref[...] = jnp.sum(bias_sum, axis=1, keepdims=True)
    extra_ref[...] = total[groups * width :, :]


def finish(sums, w_qkv, gain, bias):
    width = w_qkv.shape[0]
    groups = width // 128
    rows, lanes = sums.piece
    count = sums.m * sums.n
    extras = 2 * count * rows - groups * width
    ids = jnp.stack([sums.core, sums.chip, sums.plane])
    return pl.pallas_call(
        functools.partial(finish_kernel, sums.m, sums.n, groups),
        in_specs=[scalars()] + [pl.BlockSpec(memory_space=pltpu.VMEM)] * 5,
        out_specs=[pl.BlockSpec(memory_space=pltpu.VMEM)] * 4,
        out_shape=[
            jax.ShapeDtypeStruct(w_qkv.shape, F32),
            jax.ShapeDtypeStruct((width, 1), F32),
            jax.ShapeDtypeStruct((width, 1), F32),
            jax.ShapeDtypeStruct((extras, lanes), F32),
        ],
        scratch_shapes=[pltpu.VMEM((2 * count * rows, lanes), F32)],
        compiler_params=pltpu.CompilerParams(vmem_limit_bytes=60 << 20),
        cost_estimate=cost(5),
        name="finish",
    )(
        ids,
        sums.mine.reshape(count, rows, lanes),
        sums.other.reshape(count, rows, lanes),
        w_qkv,
        gain[:, None],
        bias[:, None],
    )


def neighbours():
    count = lax.axis_size("tm")
    down = [(i, i - 1) for i in range(1, count)]
    up = [(i, i + 1) for i in range(count - 1)]
    return down, up


def fetch_halves(field):
    down, up = neighbours()
    width = field.shape[-1]
    above = lax.ppermute(field[0, :, :, :SHIFT_T].reshape(PLACES * SHIFT_T, width), "tm", down)
    below = lax.ppermute(field[1, :, :, SHIFT_T:].reshape(PLACES * SHIFT_T, width), "tm", up)
    return above, below


def send_back(message):
    down, up = neighbours()
    return lax.ppermute(message[0], "tm", up), lax.ppermute(message[1], "tm", down)


def frame_facts(segments, keep):
    count = lax.axis_size("tm")
    me = lax.axis_index("tm")
    own = 2 * SHIFT_T
    first = me * own
    t = jnp.arange(SHIFT_T)
    zero, one = jnp.zeros((SHIFT_T,), jnp.int32), jnp.ones((SHIFT_T,), jnp.int32)
    top, bottom = me == count - 1, me == 0
    frames = jnp.stack(
        [
            jnp.concatenate([first + SHIFT_T + t, jnp.where(top, first + SHIFT_T + t, first + own + t)]),
            jnp.concatenate([jnp.where(bottom, t, first - SHIFT_T + t), first + t]),
        ]
    )
    volumes = jnp.stack(
        [jnp.concatenate([zero, jnp.where(top, one, zero)]), jnp.concatenate([jnp.where(bottom, zero, one), one])]
    )
    pick_frame = (frames[:, :, None] == jnp.arange(segments.shape[1])).astype(jnp.int32)
    by_volume = jnp.sum(pick_frame[:, :, None, :] * segments[None, None], axis=-1)
    segment = jnp.where(volumes == 0, by_volume[..., 0], by_volume[..., 1])
    key = segment + 8 * (frames < SHIFT_T) + 16 * volumes
    apart = (key[:, :, None] != key[:, None, :]).astype(F32) * FAR
    far = jnp.tile(apart, (1, 1, 128 // WT))
    seg_hot = (segment[:, :, None] == jnp.arange(keep.shape[2])).astype(F32)
    kept = jnp.where(volumes[:, :, None, None] == 0, keep[0], keep[1]).astype(F32)
    drops = jnp.sum(seg_hot[:, :, None, :] * kept, axis=-1) / KEEP_RATE
    drops = jnp.broadcast_to(drops[..., None], drops.shape + (128,))
    return far, drops[:, :, 0], drops[:, :, 1]


def shards(
    volume,
    segments,
    keep,
    ln1_gain,
    ln1_bias,
    w_qkv,
    q_bias,
    v_bias,
    rel_table,
    w_proj,
    proj_bias,
    ln2_gain,
    ln2_bias,
    w_fc1,
    fc1_bias,
    w_fc2,
    fc2_bias,
    cotangent,
):
    width = volume.shape[-1]
    heads = rel_table.shape[1]
    dim = width // heads
    hidden = w_fc1.shape[1]
    groups = width // 128
    me = lax.axis_index("tm")
    top, bottom = me == lax.axis_size("tm") - 1, me == 0
    edges_in = jnp.stack([top, bottom]).astype(jnp.int32)
    edges_out = jnp.stack([bottom, top]).astype(jnp.int32)
    places = volume.transpose(0, 2, 3, 1, 4)
    cot = cotangent.transpose(0, 2, 3, 1, 4)
    above, below = fetch_halves(places)
    cot_above, cot_below = fetch_halves(cot)
    far, drop_attn, drop_mlp = frame_facts(segments, keep)
    biases = make_bias(rel_table)
    qkv_bias = jnp.concatenate([q_bias, jnp.zeros_like(q_bias), v_bias])
    w_groups = w_qkv.reshape(width, 3, groups, 128).transpose(0, 2, 1, 3).reshape(width, 3 * width)
    x, unit, q, k, v = make_qkv(
        edges_in, places, above, below, ln1_gain, ln1_bias, w_qkv, qkv_bias, dim**-0.5 * LOG2E
    )
    *exps, att, inverse = attend(q, k, v, far, biases, dim)
    mixed, mixed_message, middle_grad, out_grad, g_mlp, small2, small_fc1 = mlp(
        edges_in,
        x,
        att,
        inverse,
        cot,
        cot_above,
        cot_below,
        drop_attn,
        drop_mlp,
        w_proj,
        proj_bias,
        ln2_gain,
        ln2_bias,
        w_fc1,
        fc1_bias,
        w_fc2,
        fc2_bias,
    )
    mixed_below, mixed_above = send_back(mixed_message)
    mlp_sum = Sum(g_mlp).step0()
    grads, pieces, sums, tables = [], [], [], []
    wait = mlp_sum.whole
    for group in range(groups):
        d, gw, colsum, by_rows, by_cols = attend_back(
            group, q, k, v, tie(out_grad, wait), att, unit, exps, dim
        )
        grads.append(d)
        pieces.append(gw)
        sums.append(jnp.sum(colsum, axis=0))
        tables.append((by_rows, by_cols))
        if group < 3:
            mlp_sum.got = lax.optimization_barrier((mlp_sum.got, d))[0]
            wait = (mlp_sum.step1, mlp_sum.step2, mlp_sum.step3)[group]()
    all_mlp = mlp_sum.gathered()
    times = 2 * WT - 1
    table = jnp.concatenate([t[0] for t in tables]).reshape(heads, ACROSS, ACROSS, times)
    table = table + jnp.concatenate([t[1] for t in tables]).reshape(heads, ACROSS, ACROSS, times).swapaxes(1, 2)
    table = table.transpose(0, 3, 1, 2).reshape(-1)
    extras = jnp.concatenate(
        sums + [jnp.sum(small2, axis=1).reshape(-1), jnp.sum(small_fc1, axis=0).reshape(-1), table]
    ).astype(BF16)
    lanes = 3 * 128
    unit_rows = 8 * lax.axis_size("dp") * lax.axis_size("tm")
    rows = up_to(groups * width + -(-extras.size // lanes), unit_rows)
    extras = jnp.pad(extras, (0, (rows - groups * width) * lanes - extras.size)).reshape(-1, lanes)
    qkv_sum = Sum(jnp.concatenate(pieces + [extras])).step0()
    grad0, message0 = qkv_back(0, grads, tie(x, qkv_sum.whole), middle_grad, w_groups, ln1_gain)
    below0, above0 = send_back(message0)
    qkv_sum.got = tie(qkv_sum.got, grad0)
    wait = qkv_sum.step1()
    grad1, message1 = qkv_back(1, grads, tie(x, wait, message0), middle_grad, w_groups, ln1_gain)
    below1, above1 = send_back(message1)
    qkv_sum.got = lax.optimization_barrier((qkv_sum.got, grad1))[0]
    wait = qkv_sum.step2()
    mixed_out = to_frames(edges_out, [tie(mixed, wait)], [mixed_below], [mixed_above])
    qkv_sum.got = lax.optimization_barrier((qkv_sum.got, mixed_out))[0]
    wait = qkv_sum.step3_back()
    all_mlp = tie(all_mlp, wait)
    g_fc1 = all_mlp[: hidden].reshape(hidden // width, width, width).transpose(1, 0, 2).reshape(width, hidden)
    g_fc1, g_fc2, g_proj = g_fc1.astype(F32), all_mlp[hidden : 2 * hidden].astype(F32), all_mlp[2 * hidden :].astype(F32)
    qkv_sum.got = lax.optimization_barrier((qkv_sum.got, g_fc1, g_fc2, g_proj))[0]
    wait = qkv_sum.step4_back()
    volume_grad = to_frames(edges_out, [tie(grad0, wait), grad1], [below0, below1], [above0, above1])
    qkv_sum.got = lax.optimization_barrier((qkv_sum.got, volume_grad))[0]
    qkv_sum.step5_back()
    g_qkv, ln1_g, ln1_b, extras = finish(qkv_sum, w_qkv, ln1_gain, ln1_bias)
    extras = extras.reshape(-1)
    colsum = extras[: 3 * width].reshape(groups, 3, 128)
    at = 3 * width
    small2 = extras[at : at + 4 * width].reshape(4, width)
    at += 4 * width
    fc1_b = extras[at : at + hidden]
    at += hidden
    table = extras[at : at + rel_table.size].reshape(heads, -1).T
    return (
        mixed_out.transpose(0, 3, 1, 2, 4),
        volume_grad.transpose(0, 3, 1, 2, 4),
        ln1_g[:, 0],
        ln1_b[:, 0],
        g_qkv,
        colsum[:, 0].reshape(-1),
        colsum[:, 2].reshape(-1),
        table,
        g_proj,
        small2[3],
        small2[1],
        small2[2],
        g_fc1,
        fc1_b,
        g_fc2,
        small2[0],
    )


def solution(mesh):
    split = P("dp", "tm", None, None, None)
    return jax.shard_map(
        shards,
        mesh=mesh,
        in_specs=(split, P("dp", None), P("dp", None, None)) + (P(),) * 14 + (split,),
        out_specs=(split, split) + (P(),) * 14,
        check_vma=False,
    )
```

```python
import functools

import jax
import jax.numpy as jnp
import numpy as np
from jax import lax
from jax.experimental import pallas as pl
from jax.experimental.pallas import tpu as pltpu
from jax.sharding import PartitionSpec as P

SIDE = 14
WT = 8
WIN_HW = 7
SHIFT_T = 4
SHIFT_HW = 3
EPS = 1e-05
KEEP_RATE = 0.75
PRECISE = lax.Precision.HIGHEST
LOG2E = 1.4426950408889634
LN2 = 0.6931471805599453
FAR = 1e30
F32 = jnp.float32
BF16 = jnp.bfloat16

SPANS = (
    (SHIFT_HW, WIN_HW),
    (SHIFT_HW + WIN_HW, SIDE - SHIFT_HW - WIN_HW),
    (0, SHIFT_HW),
)
ACROSS = 2 * WIN_HW - 1
RECTS = (
    (0, 0, True, 0),
    (1, 0, True, 0),
    (0, 1, False, 1),
    (2, 0, True, 0),
    (0, 2, False, 1),
    (2, 2, True, 3),
    (2, 1, True, 2),
    (1, 2, True, 3),
    (1, 1, True, 2),
)
BIAS_DIMS = ((7, 7), (4, 7), (4, 4), (4, 3))


def up_to(value, unit):
    return -(-value // unit) * unit


class Rect:
    pass


def plan_rects():
    rects, slots, start = [], [], 0
    class_rows = [0, 0, 0]
    for row_span, col_span, rows_outer, table in RECTS:
        r0, rn = SPANS[row_span]
        c0, cn = SPANS[col_span]
        rect = Rect()
        if rows_outer:
            places = [(r0 + a, c0 + b) for a in range(rn) for b in range(cn)]
        else:
            places = [(r0 + b, c0 + a) for a in range(cn) for b in range(rn)]
        rect.count = len(places) * WT
        rect.rows = up_to(rect.count, 16)
        rect.lanes = up_to(rect.count, 128)
        rect.start = start
        rect.table = table
        rect.kind = {512: 0, 256: 1, 128: 2}[rect.lanes]
        rect.kind_row = class_rows[rect.kind]
        class_rows[rect.kind] += rect.rows
        slots += places + [None] * ((rect.rows - rect.count) // WT)
        start += rect.rows
        rects.append(rect)
    return rects, slots, class_rows


RECT, SLOTS, KIND_ROWS = plan_rects()
TOKENS = len(SLOTS) * WT
KIND_LANES = (512, 256, 128)
PLACES = SIDE * SIDE


def nn(a, b):
    return lax.dot_general(a, b, (((1,), (0,)), ((), ())), preferred_element_type=F32)


def nt(a, b):
    return lax.dot_general(a, b, (((1,), (1,)), ((), ())), preferred_element_type=F32)


def wide(pattern, width):
    return jnp.concatenate([pattern] * (width // pattern.shape[-1]), axis=-1)


def by_frame(values, pattern):
    rows, width = values.shape
    scaled = values.reshape(rows // WT, WT, width) * wide(pattern, width)[None]
    return scaled.reshape(rows, width)


def column_sums(values):
    rows, width = values.shape
    return jnp.sum(values.reshape(rows // 8, 8, width), axis=0)


def row_half(shape):
    return (lax.broadcasted_iota(jnp.int32, shape, 0) & (WT - 1)) < SHIFT_T


def turned(tile):
    return pltpu.roll(tile, SHIFT_T, 0)


def spread_message(message_ref, doubled):
    def pair(i, carry):
        both = message_ref[pl.ds(pl.multiple_of(i * 16, 16), 16), :].astype(F32)
        for k in range(2):
            tile = both[k * WT : k * WT + WT]
            low = row_half(tile.shape)
            swap = turned(tile)
            at = pl.multiple_of(i * 32 + k * 16, 16)
            doubled[pl.ds(at, WT), :] = jnp.where(low, tile, swap)
            doubled[pl.ds(at + WT, WT), :] = jnp.where(low, swap, tile)
        return carry

    lax.fori_loop(0, message_ref.shape[0] // 16, pair, 0)


def assemble_tokens(win, edge_ref, own_ref, alt_ref, above_ref, below_ref, doubled, tokens):
    @pl.when(win == 0)
    def _():
        spread_message(above_ref, doubled)

    @pl.when(win == 1)
    def _():
        spread_message(below_ref, doubled)

    width = tokens.shape[1]
    own_low = row_half((WT, width)) == (win == 0)
    edge = edge_ref[win] == 1
    for slot, place in enumerate(SLOTS):
        rows = slice(slot * WT, slot * WT + WT)
        if place is None:
            tokens[rows, :] = jnp.zeros((WT, width), F32)
            continue
        h, w = place
        at = (h * SIDE + w) * WT
        own = turned(own_ref[0, h, w].astype(F32))
        other = jnp.where(edge, alt_ref[0, h, w].astype(F32), doubled[at : at + WT, :])
        tokens[rows, :] = jnp.where(own_low, own, other)


def pack_message(win, tokens, first, count, message_ref):
    def pair(i, carry):
        both = tokens[pl.ds(pl.multiple_of(first + i * 32, 16), 32), :]
        tiles = []
        for k in range(2):
            one, two = both[k * 16 : k * 16 + WT], both[k * 16 + WT : k * 16 + 16]
            low = row_half(one.shape)
            late = jnp.where(low, turned(one), two)
            early = jnp.where(low, one, turned(two))
            tiles.append(jnp.where(win == 0, late, early))
        message_ref[pl.ds(pl.multiple_of(i * 16, 16), 16), :] = jnp.concatenate(tiles, axis=0).astype(
            message_ref.dtype
        )
        return carry

    lax.fori_loop(0, count // 32, pair, 0)


def spread_table(source, outer, inner, out_ref, lane):
    width = inner * WT
    total = outer * width
    for ok in range(outer):
        for ik in range(inner):
            pieces = []
            for oq in range(outer):
                shift = (oq * width - (WIN_HW - 1 - ik) * WT) % 128
                piece = source[oq - ok + WIN_HW - 1]
                pieces.append(pltpu.roll(piece, shift, 1) if shift else piece)
            row = (ok * inner + ik) * WT
            for tile in range(up_to(total, 128) // 128):
                value = None
                for oq in range(outer):
                    begin, end = oq * width, (oq + 1) * width
                    if end <= tile * 128 or begin >= tile * 128 + 128:
                        continue
                    if value is None:
                        value = pieces[oq]
                    else:
                        value = jnp.where(lane >= begin - tile * 128, pieces[oq], value)
                out_ref[0, row : row + WT, tile * 128 : tile * 128 + 128] = value


def split3(values):
    parts = []
    for _ in range(3):
        part = values.astype(BF16)
        parts.append(part)
        values = values - part.astype(F32)
    return parts


def hot_times(tk):
    count = ACROSS * (2 * WT - 1)
    place = lax.broadcasted_iota(jnp.int32, (count, 128), 0)
    lane = lax.broadcasted_iota(jnp.int32, (count, 128), 1)
    tq = lane & (WT - 1)
    d = lax.shift_right_logical(lane, 3)
    return (((tq - tk + WT - 1) * ACROSS + d == place) & (d < ACROSS)).astype(BF16)


def lane_roll(tile, shift):
    shift = shift % 128
    return pltpu.roll(tile, shift, 1) if shift else tile


def lane_block(lane, d):
    return (lane >= d * WT) & (lane < d * WT + WT)


def bias_kernel(table_ref, b0_ref, b1_ref, b2_ref, b3_ref, strips):
    head = pl.program_id(0)

    @pl.when(head == 0)
    def _():
        parts = split3(table_ref[...] * LOG2E)
        for tk in range(WT):
            hot = hot_times(tk)
            strips[pl.ds(tk, table_ref.shape[0], stride=WT), :] = sum(nn(p, hot) for p in parts)

    lane = lax.broadcasted_iota(jnp.int32, (WT, 128), 1)
    base = pl.multiple_of(head * (ACROSS * WT), WT)
    by_rows = [strips[pl.ds(base + d * WT, WT), :] for d in range(ACROSS)]
    by_cols = [None] * ACROSS
    reach = BIAS_DIMS[1][0] - 1
    for d in range(WIN_HW - 1 - reach, WIN_HW + reach):
        by_cols[d] = sum(
            jnp.where(lane_block(lane, e), lane_roll(by_rows[e], (e - d) * WT), 0.0) for e in range(ACROSS)
        )
    for out_ref, source, (outer, inner) in zip(
        (b0_ref, b1_ref, b2_ref, b3_ref), (by_rows, by_cols, by_rows, by_rows), BIAS_DIMS
    ):
        spread_table(source, outer, inner, out_ref, lane)


def bias_shapes(heads):
    shapes = []
    for outer, inner in BIAS_DIMS:
        count = outer * inner * WT
        shapes.append((heads, count, up_to(count, 128)))
    return shapes


def make_bias(rel_table):
    heads = rel_table.shape[1]
    times = 2 * WT - 1
    cube = rel_table.T.reshape(heads, times, ACROSS, ACROSS)
    table = cube.transpose(0, 2, 1, 3).reshape(heads * ACROSS, times * ACROSS)
    shapes = bias_shapes(heads)
    return pl.pallas_call(
        bias_kernel,
        grid=(heads,),
        in_specs=[whole(table.shape)],
        out_specs=[pl.BlockSpec((1,) + s[1:], lambda h: (h, 0, 0)) for s in shapes],
        out_shape=[jax.ShapeDtypeStruct(s, F32) for s in shapes],
        scratch_shapes=[pltpu.VMEM((heads * ACROSS * WT, 128), F32)],
        compiler_params=pltpu.CompilerParams(vmem_limit_bytes=48 << 20),
        cost_estimate=cost(10),
        name="position_bias",
    )(table)


def fold_table(acc, outer, inner, totals, lane):
    width = inner * WT
    for ok in range(outer):
        for ik in range(inner):
            row = (ok * inner + ik) * WT
            for oq in range(outer):
                shift = (oq * width - (WIN_HW - 1 - ik) * WT) % 128
                begin, end = oq * width, (oq + 1) * width
                tile, lo = begin // 128, begin % 128
                last = (end - 1) // 128
                value = acc(row, tile)
                if last == tile:
                    value = jnp.where((lane >= lo) & (lane < lo + width), value, 0.0)
                else:
                    after = jnp.where(lane < end - last * 128, acc(row, last), 0.0)
                    value = jnp.where(lane >= lo, value, after)
                d = oq - ok + WIN_HW - 1
                back = pltpu.roll(value, (128 - shift) % 128, 1) if shift else value
                totals[d] = totals[d] + back


def qkv_kernel(
    tile,
    scale,
    edge_ref,
    own_ref,
    alt_ref,
    above_ref,
    below_ref,
    gain_ref,
    bias_ref,
    w_ref,
    wb_ref,
    x_ref,
    n_ref,
    q_ref,
    k_ref,
    v_ref,
    doubled,
    tokens,
):
    win, step = pl.program_id(0), pl.program_id(1)

    @pl.when(step == 0)
    def _():
        assemble_tokens(win, edge_ref, own_ref, alt_ref, above_ref, below_ref, doubled, tokens)

    x = tokens[pl.ds(pl.multiple_of(step * tile, 16), tile), :]
    x_ref[0] = x.astype(BF16)
    unit, _ = norm_stats(x)
    n_ref[0] = unit.astype(BF16)
    normed = (unit * gain_ref[...] + bias_ref[...]).astype(BF16)
    width = x.shape[1]
    q_ref[0] = ((nn(normed, w_ref[:, :width]) + wb_ref[:, :width]) * scale).astype(BF16)
    k_ref[0] = nn(normed, w_ref[:, width : 2 * width]).astype(BF16)
    v_ref[0] = (nn(normed, w_ref[:, 2 * width :]) + wb_ref[:, 2 * width :]).astype(BF16)


def cost(micros):
    return pl.CostEstimate(flops=int(micros * 1.1e9), bytes_accessed=1 << 20, transcendentals=0)


def norm_stats(values):
    centre = values - jnp.mean(values, axis=-1, keepdims=True)
    spread = jnp.mean(centre * centre, axis=-1, keepdims=True)
    inverse = lax.rsqrt(spread + EPS)
    return centre * inverse, inverse


def norm_back(scaled, unit, inverse):
    first = jnp.mean(scaled, axis=-1, keepdims=True)
    second = jnp.mean(scaled * unit, axis=-1, keepdims=True)
    return (scaled - first - unit * second) * inverse


def whole(shape):
    return pl.BlockSpec(shape, lambda *_: (0,) * len(shape))


def scalars():
    return pl.BlockSpec(memory_space=pltpu.SMEM)


def volume_specs(width):
    block = (1, SIDE, SIDE, WT, width)
    return [
        pl.BlockSpec(block, lambda w, *_: (w, 0, 0, 0, 0)),
        pl.BlockSpec(block, lambda w, *_: (1 - w, 0, 0, 0, 0)),
        whole((PLACES * SHIFT_T, width)),
        whole((PLACES * SHIFT_T, width)),
    ]


def tile_spec(tile, width):
    return pl.BlockSpec((1, tile, width), lambda w, j: (w, j, 0))


def make_qkv(edges, volume, above, below, gain, bias, w_qkv, qkv_bias, scale, tile=400):
    width = volume.shape[-1]
    out = jax.ShapeDtypeStruct((2, TOKENS, width), BF16)
    return pl.pallas_call(
        functools.partial(qkv_kernel, tile, scale),
        grid=(2, TOKENS // tile),
        in_specs=[scalars()]
        + volume_specs(width)
        + [whole((1, width)), whole((1, width)), whole(w_qkv.shape), whole((1, 3 * width))],
        out_specs=[tile_spec(tile, width)] * 5,
        out_shape=[out] * 5,
        scratch_shapes=[
            pltpu.VMEM((PLACES * WT, width), F32),
            pltpu.VMEM((TOKENS, width), F32),
        ],
        compiler_params=pltpu.CompilerParams(vmem_limit_bytes=60 << 20),
        cost_estimate=cost(17),
        name="norm1_qkv",
    )(edges, volume, volume, above, below, gain[None], bias[None], w_qkv, qkv_bias[None])


def head_rows(transposed, head, dim):
    rows, lanes = transposed.shape
    parts = []
    if head:
        parts.append(jnp.zeros((head * dim, lanes), transposed.dtype))
    parts.append(transposed[head * dim : head * dim + dim])
    if (head + 1) * dim < rows:
        parts.append(jnp.zeros((rows - (head + 1) * dim, lanes), transposed.dtype))
    return jnp.concatenate(parts, axis=0)


def attend_kernel(
    dim, q_ref, k_ref, v_ref, far_ref, b0, b1, b2, b3, e0_ref, e1_ref, e2_ref, o_ref, r_ref, *scores
):
    biases = (b0, b1, b2, b3)
    e_refs = (e0_ref, e1_ref, e2_ref)
    far = far_ref[0]
    per = 128 // dim
    ones = jnp.ones((16, RECT[0].rows), BF16)
    operands = {}

    def prepare(rect):
        if rect not in operands:
            queries = q_ref[0, rect.start : rect.start + rect.lanes, :].T
            values = v_ref[0, rect.start : rect.start + rect.rows, :].T
            operands[rect] = queries, k_ref[0, rect.start : rect.start + rect.rows, :], values, [], []
        return operands[rect]

    def score(rect, head, buffer):
        queries, keys, _, _, _ = prepare(rect)
        count, lanes = rect.count, rect.lanes
        raw = nn(keys, head_rows(queries, head, dim))[:count]
        raw = raw + biases[rect.table][head, :count, :lanes]
        buffer[:count, :lanes] = raw
        wide_far = wide(far, lanes)
        top = jnp.max(raw.reshape(count // 8, 8, lanes), axis=0) - wide_far
        return jnp.max(top, axis=0, keepdims=True) + wide_far

    def exponents(rect, head, buffer, top):
        count, rows, lanes = rect.count, rect.rows, rect.lanes
        exps = jnp.exp2(buffer[:count, :lanes].reshape(count // 8, 8, lanes) - top[None])
        exps = exps.reshape(count, lanes).astype(BF16)
        if rows > count:
            exps = jnp.concatenate([exps, jnp.zeros((rows - count, lanes), BF16)], axis=0)
        place = slice(rect.kind_row, rect.kind_row + rows), slice(head * lanes, head * lanes + lanes)
        e_refs[rect.kind][(0, 0) + place] = exps
        return exps

    def weigh(rect, head, exps):
        _, _, values, outs, scales = prepare(rect)
        rows, lanes, start = rect.rows, rect.lanes, rect.start
        lhs = jnp.concatenate([values[head * dim : head * dim + dim], ones[:, :rows]], axis=0)
        out = nn(lhs, exps)
        inverse = jnp.broadcast_to(1.0 / out[dim : dim + 1], (dim, lanes))
        outs.append(out[:dim] * inverse)
        scales.append(inverse)
        if len(outs) == per:
            o_ref[0, start : start + rows, :] = jnp.concatenate(outs, axis=0).T[:rows].astype(BF16)
            r_ref[0, start : start + rows, :] = jnp.concatenate(scales, axis=0).T[:rows]

    units = [(rect, head) for rect in RECT for head in range(per)]
    tops, exps = {}, {}
    for i in range(len(units) + 2):
        if i < len(units):
            tops[i] = score(*units[i], scores[i % len(scores)])
        if 0 <= i - 1 < len(units):
            exps[i - 1] = exponents(*units[i - 1], scores[(i - 1) % len(scores)], tops.pop(i - 1))
        if 0 <= i - 2:
            weigh(*units[i - 2], exps.pop(i - 2))


def head_group_specs(heads, per, biases):
    lane_tile = pl.BlockSpec((1, TOKENS, 128), lambda g, w: (w, 0, g))
    far = pl.BlockSpec((1, WT, 128), lambda g, w: (w, 0, 0))
    bias = [pl.BlockSpec((per,) + b[1:], lambda g, w: (g, 0, 0)) for b in biases]
    exps = [
        pl.BlockSpec((1, 1, KIND_ROWS[i], per * KIND_LANES[i]), lambda g, w: (w, g, 0, 0)) for i in range(3)
    ]
    return lane_tile, far, bias, exps


def exps_shapes(groups, per):
    return [jax.ShapeDtypeStruct((2, groups, KIND_ROWS[i], per * KIND_LANES[i]), BF16) for i in range(3)]


def attend(q, k, v, far, biases, dim):
    width = q.shape[-1]
    heads = width // dim
    per = 128 // dim
    groups = heads // per
    lane_tile, far_spec, bias_specs, exps_specs = head_group_specs(heads, per, [b.shape for b in biases])
    return pl.pallas_call(
        functools.partial(attend_kernel, dim),
        grid=(groups, 2),
        in_specs=[lane_tile] * 3 + [far_spec] + bias_specs,
        out_specs=exps_specs + [lane_tile, lane_tile],
        out_shape=exps_shapes(groups, per)
        + [jax.ShapeDtypeStruct((2, TOKENS, width), BF16), jax.ShapeDtypeStruct((2, TOKENS, width), F32)],
        scratch_shapes=[pltpu.VMEM((RECT[0].count, RECT[0].lanes), F32)] * 3,
        compiler_params=pltpu.CompilerParams(vmem_limit_bytes=60 << 20),
        cost_estimate=cost(55),
        name="attention",
    )(q, k, v, far, *biases)


def attend_back_kernel(
    dim,
    scale,
    q_ref,
    k_ref,
    v_ref,
    g_ref,
    o_ref,
    n_ref,
    e0_ref,
    e1_ref,
    e2_ref,
    d_ref,
    gw_ref,
    sums_ref,
    strips_ref,
    a0,
    a1,
    a2,
    a3,
    acc_w,
    *buffers,
):
    win = pl.program_id(0)
    accs = (a0, a1, a2, a3)
    e_refs = (e0_ref, e1_ref, e2_ref)
    grads, queries, outgrads, probs = buffers[:2], buffers[2:4], buffers[4:6], buffers[6:]
    per = 128 // dim
    lane = lax.broadcasted_iota(jnp.int32, (1, 128), 1)
    mine = [((lane >= h * dim) & (lane < h * dim + dim)).astype(BF16) for h in range(per)]

    @pl.when(win == 0)
    def _():
        for acc in accs:
            acc[...] = jnp.zeros_like(acc)
        acc_w[...] = jnp.zeros_like(acc_w)
        sums_ref[...] = jnp.zeros_like(sums_ref)

    operands = {}

    def prepare(index):
        if index not in operands:
            rect = RECT[index]
            rows, lanes, start = rect.rows, rect.lanes, rect.start
            out_grad = g_ref[0, start : start + rows, :]
            if lanes > rows:
                out_grad = jnp.concatenate([out_grad, jnp.zeros((lanes - rows, 128), BF16)], axis=0)
            query = q_ref[0, start : start + lanes, :]
            out_grad_t = out_grad.T
            out_t = o_ref[0, start : start + lanes, :].T
            keys_t = k_ref[0, start : start + rows, :].T
            product = out_grad_t.astype(F32) * out_t.astype(F32)
            for head in range(per):
                here = slice(head * lanes, head * lanes + lanes)
                queries[index % 2][here, :] = query * mine[head]
                outgrads[index % 2][here, :] = out_grad * mine[head]
            operands[index] = out_grad_t, keys_t, product, []
        return operands[index]

    def first(index, head, buffer):
        out_grad_t, _, product, _ = prepare(index)
        rect = RECT[index]
        values = v_ref[0, rect.start : rect.start + rect.rows, :]
        buffer[: rect.rows, : rect.lanes] = nn(values, head_rows(out_grad_t, head, dim))
        return jnp.sum(product[head * dim : head * dim + dim], axis=0, keepdims=True)

    def second(index, head, buffer, inner):
        rect = RECT[index]
        count, rows, lanes = rect.count, rect.rows, rect.lanes
        here = slice(head * lanes, head * lanes + lanes)
        exps = e_refs[rect.kind][0, 0, rect.kind_row : rect.kind_row + rows, here].astype(F32)
        score_grad = exps * (buffer[:rows, :lanes] - inner)
        accs[rect.table][head, :count, :lanes] += score_grad[:count]
        low = score_grad.astype(BF16)
        grads[index % 2][:rows, here] = low
        return low

    def third(index, head, low):
        _, keys_t, _, dqs = prepare(index)
        dqs.append(nn(keys_t[head * dim : head * dim + dim], low))
        if len(dqs) < per:
            return
        rect = RECT[index]
        rows, lanes, start = rect.rows, rect.lanes, rect.start
        dq = jnp.concatenate(dqs, axis=0) * scale
        d_ref[0, start : start + rows, :128] = dq.T[:rows].astype(BF16)
        dk = nn(grads[index % 2][:rows, : per * lanes], queries[index % 2][: per * lanes, :])
        d_ref[0, start : start + rows, 128:256] = (dk * LN2).astype(BF16)
        exps = e_refs[rect.kind][0, 0, rect.kind_row : rect.kind_row + rows, :]
        dv = nn(exps, outgrads[index % 2][: per * lanes, :])
        d_ref[0, start : start + rows, 256:] = dv.astype(BF16)

    units = [(index, head) for index in range(len(RECT)) for head in range(per)]
    inners, lows = {}, {}
    for i in range(len(units) + 2):
        if i < len(units):
            inners[i] = first(*units[i], probs[i % len(probs)])
        if 0 <= i - 1 < len(units):
            lows[i - 1] = second(*units[i - 1], probs[(i - 1) % len(probs)], inners.pop(i - 1))
        if 0 <= i - 2:
            third(*units[i - 2], lows.pop(i - 2))

    all_grads = d_ref[0]
    acc_w[...] += lax.dot_general(n_ref[0], all_grads, (((0,), (0,)), ((), ())), preferred_element_type=F32)
    sums_ref[...] += column_sums(all_grads.astype(F32))

    @pl.when(win == 1)
    def _():
        gw_ref[...] = acc_w[...].astype(BF16)
        lane8 = lax.broadcasted_iota(jnp.int32, (WT, 128), 1)
        for head in range(per):
            by_rows = [jnp.zeros((WT, 128), F32) for _ in range(ACROSS)]
            by_cols = [jnp.zeros((WT, 128), F32) for _ in range(ACROSS)]
            for acc, totals, (outer, inner) in zip(accs, (by_rows, by_cols, by_rows, by_rows), BIAS_DIMS):
                fold_table(
                    lambda row, tile: acc[head, row : row + WT, tile * 128 : tile * 128 + 128],
                    outer,
                    inner,
                    totals,
                    lane8,
                )
            for d in range(ACROSS):
                for e in range(ACROSS):
                    if abs(e - WIN_HW + 1) < BIAS_DIMS[1][0]:
                        turned_back = lane_roll(by_cols[e], (e - d) * WT)
                        by_rows[d] = by_rows[d] + jnp.where(lane_block(lane8, e), turned_back, 0.0)
                strips_ref[(head * ACROSS + d) * WT : (head * ACROSS + d + 1) * WT, :] = by_rows[d]


def attend_back(group, q, k, v, out_grad, out, unit, exps, dim):
    width = q.shape[-1]
    per = 128 // dim
    shapes = bias_shapes(per)
    lane_tile = pl.BlockSpec((1, TOKENS, 128), lambda w: (w, 0, group))
    exps_specs = [
        pl.BlockSpec((1, 1, KIND_ROWS[i], per * KIND_LANES[i]), lambda w: (w, group, 0, 0)) for i in range(3)
    ]
    strip = (per * ACROSS * WT, 128)
    most = per * RECT[0].lanes
    return pl.pallas_call(
        functools.partial(attend_back_kernel, dim, dim**-0.5),
        grid=(2,),
        in_specs=[lane_tile] * 5 + [pl.BlockSpec((1, TOKENS, width), lambda w: (w, 0, 0))] + exps_specs,
        out_specs=[
            pl.BlockSpec((1, TOKENS, 384), lambda w: (w, 0, 0)),
            whole((width, 384)),
            whole((8, 384)),
            whole(strip),
        ],
        out_shape=[
            jax.ShapeDtypeStruct((2, TOKENS, 384), BF16),
            jax.ShapeDtypeStruct((width, 384), BF16),
            jax.ShapeDtypeStruct((8, 384), F32),
            jax.ShapeDtypeStruct(strip, F32),
        ],
        scratch_shapes=[pltpu.VMEM(s, F32) for s in shapes]
        + [
            pltpu.VMEM((width, 384), F32),
        ]
        + [pltpu.VMEM((RECT[0].rows, most), BF16)] * 2
        + [pltpu.VMEM((most, 128), BF16)] * 4
        + [pltpu.VMEM((RECT[0].rows, RECT[0].lanes), F32)] * 3,
        compiler_params=pltpu.CompilerParams(vmem_limit_bytes=60 << 20),
        cost_estimate=cost(20),
        name="attention_back",
    )(q, k, v, out_grad, out, unit, *exps)


ERFC = (0.254829592, -0.284496736, 1.421413741, -1.453152027, 1.061405429)
ERFC_P = 0.3275911


def gelu_both(u):
    denominator = 1.0 + (ERFC_P * 0.5**0.5) * jnp.abs(u)
    t = pl.reciprocal(denominator, approx=True)
    t = t * (2.0 - denominator * t)
    bell = jnp.exp2((u * u) * (-0.5 * LOG2E))
    series = 0.5 * ERFC[4]
    for factor in ERFC[3::-1]:
        series = series * t + 0.5 * factor
    tail = series * t * bell
    area = jnp.where(u >= 0.0, 1.0 - tail, tail)
    return u * area, area + (u * (1.0 / np.sqrt(2.0 * np.pi))) * bell


def mlp_kernel(
    tile,
    steps,
    chunk,
    edge_ref,
    x_ref,
    att_ref,
    r_ref,
    own_ref,
    alt_ref,
    above_ref,
    below_ref,
    da_ref,
    dm_ref,
    wp_ref,
    pb_ref,
    g_ref,
    b_ref,
    w1_ref,
    b1_ref,
    w2_ref,
    b2_ref,
    mixed_ref,
    message_ref,
    mg_ref,
    og_ref,
    gw_ref,
    small_ref,
    fc1b_ref,
    doubled,
    tokens,
    acc_p,
    acc_1,
    acc_2,
    result,
    n2g,
    *buffers,
):
    hiddens, slopes = buffers[:2], buffers[2:]
    win, step = pl.program_id(0), pl.program_id(1)
    width = x_ref.shape[-1]

    @pl.when((win == 0) & (step == 0))
    def _():
        acc_p[...] = jnp.zeros_like(acc_p)
        acc_1[...] = jnp.zeros_like(acc_1)
        acc_2[...] = jnp.zeros_like(acc_2)
        small_ref[...] = jnp.zeros_like(small_ref)
        fc1b_ref[...] = jnp.zeros_like(fc1b_ref)

    @pl.when(step == 0)
    def _():
        assemble_tokens(win, edge_ref, own_ref, alt_ref, above_ref, below_ref, doubled, tokens)

    here = pl.ds(pl.multiple_of(step * tile, 16), tile)
    da, dm = da_ref[0], dm_ref[0]
    attended = att_ref[0]
    branch = nn(attended, wp_ref[...]) + pb_ref[...]
    middle = x_ref[0].astype(F32) + by_frame(branch, da)
    unit, inverse = norm_stats(middle)
    normed = (unit * g_ref[...] + b_ref[...]).astype(BF16)
    upstream = tokens[here, :]
    result_grad = by_frame(upstream, dm).astype(BF16)
    small_ref[0] += column_sums(result_grad.astype(F32))
    normed_t = normed.T
    result_grad_t = result_grad.T
    count = w1_ref.shape[1] // chunk
    lows = {}

    def widen(i):
        part = slice(i * chunk, i * chunk + chunk)
        hiddens[i % 2][...] = nn(normed, w1_ref[:, part])
        slopes[i % 2][...] = nt(result_grad, w2_ref[part, :])

    def activate(i):
        part = slice(i * chunk, i * chunk + chunk)
        active, slope = gelu_both(hiddens[i % 2][...] + b1_ref[:, part])
        hidden_grad = slopes[i % 2][...] * slope
        fc1b_ref[:, part] += column_sums(hidden_grad)
        lows[i] = active.astype(BF16), hidden_grad.astype(BF16)

    def narrow(i):
        part = slice(i * chunk, i * chunk + chunk)
        active, hidden_grad = lows.pop(i)
        forward = nn(active, w2_ref[part, :])
        backward = nt(hidden_grad, w1_ref[:, part])
        if i == 0:
            result[...] = forward
            n2g[...] = backward
        else:
            result[...] += forward
            n2g[...] += backward
        acc_2[:, part] += nn(result_grad_t, active)
        acc_1[:, part] += nn(normed_t, hidden_grad)

    for i in range(count + 2):
        if 0 <= i - 1 < count:
            activate(i - 1)
        if i < count:
            widen(i)
        if 0 <= i - 2:
            narrow(i - 2)
    mixed = middle + by_frame(result[...] + b2_ref[...], dm)
    mixed_ref[0] = mixed.astype(BF16)
    tokens[here, :] = mixed
    normed_grad = n2g[...]
    small_ref[1] += column_sums(normed_grad * unit)
    small_ref[2] += column_sums(normed_grad)
    middle_grad = upstream + norm_back(normed_grad * g_ref[...], unit, inverse)
    mg_ref[0] = middle_grad
    branch_grad = by_frame(middle_grad, da).astype(BF16)
    small_ref[3] += column_sums(branch_grad.astype(F32))
    acc_p[...] += nn(attended.T, branch_grad)
    out_grad = nt(branch_grad, wp_ref[...]).astype(BF16)
    og_ref[0] = (out_grad.astype(F32) * r_ref[0]).astype(BF16)

    @pl.when(step == steps - 1)
    def _():
        pack_message(win, tokens, 0, TOKENS, message_ref.at[0])

    @pl.when((win == 1) & (step == steps - 1))
    def _():
        blocks = acc_1.shape[1] // width
        for i in range(blocks):
            part = slice(i * width, i * width + width)
            gw_ref[part, :] = acc_1[:, part].astype(BF16)
            gw_ref[(blocks + i) * width : (blocks + i + 1) * width, :] = acc_2[:, part].T.astype(BF16)
        gw_ref[2 * blocks * width :, :] = acc_p[...].astype(BF16)


def mlp(
    edges, x, att, inverse, cot, above, below, drop_attn, drop_mlp, wp, pb, g, b, w1, b1, w2, b2, tile=400, chunk=256
):
    width, hidden = w1.shape
    steps = TOKENS // tile
    frames = pl.BlockSpec((1, WT, 128), lambda w, j: (w, 0, 0))
    return pl.pallas_call(
        functools.partial(mlp_kernel, tile, steps, chunk),
        grid=(2, steps),
        in_specs=[scalars(), tile_spec(tile, width), tile_spec(tile, width), tile_spec(tile, width)]
        + volume_specs(width)
        + [
            frames,
            frames,
            whole(wp.shape),
            whole((1, width)),
            whole((1, width)),
            whole((1, width)),
            whole(w1.shape),
            whole((1, hidden)),
            whole(w2.shape),
            whole((1, width)),
        ],
        out_specs=[
            tile_spec(tile, width),
            pl.BlockSpec((1, TOKENS // 2, width), lambda w, j: (w, 0, 0)),
            tile_spec(tile, width),
            tile_spec(tile, width),
            whole((2 * hidden + width, width)),
            whole((4, 8, width)),
            whole((8, hidden)),
        ],
        out_shape=[
            jax.ShapeDtypeStruct((2, TOKENS, width), BF16),
            jax.ShapeDtypeStruct((2, TOKENS // 2, width), BF16),
            jax.ShapeDtypeStruct((2, TOKENS, width), F32),
            jax.ShapeDtypeStruct((2, TOKENS, width), BF16),
            jax.ShapeDtypeStruct((2 * hidden + width, width), BF16),
            jax.ShapeDtypeStruct((4, 8, width), F32),
            jax.ShapeDtypeStruct((8, hidden), F32),
        ],
        scratch_shapes=[
            pltpu.VMEM((PLACES * WT, width), F32),
            pltpu.VMEM((TOKENS, width), F32),
            pltpu.VMEM((width, width), F32),
            pltpu.VMEM((width, hidden), F32),
            pltpu.VMEM((width, hidden), F32),
            pltpu.VMEM((tile, width), F32),
            pltpu.VMEM((tile, width), F32),
        ]
        + [pltpu.VMEM((tile, chunk), F32)] * 4,
        compiler_params=pltpu.CompilerParams(vmem_limit_bytes=63 << 20),
        cost_estimate=cost(100),
        name="mlp",
    )(
        edges,
        x,
        att,
        inverse,
        cot,
        cot,
        above,
        below,
        drop_attn,
        drop_mlp,
        wp,
        pb[None],
        g[None],
        b[None],
        w1,
        b1[None],
        w2,
        b2[None],
    )


def qkv_back_kernel(d0, d1, d2, d3, x_ref, mg_ref, w_ref, g_ref, out_ref, message_ref, tokens):
    win = pl.program_id(0)
    grads = jnp.concatenate([d[0] for d in (d0, d1, d2, d3)], axis=-1)
    normed_grad = nt(grads, w_ref[...])
    unit, inverse = norm_stats(x_ref[0].astype(F32))
    grad = mg_ref[0] + norm_back(normed_grad * g_ref[...], unit, inverse)
    out_ref[0] = grad
    tokens[...] = grad
    pack_message(win, tokens, 0, tokens.shape[0], message_ref.at[0])


def qkv_back(part, grads, x, middle_grad, w_groups, gain):
    width = x.shape[-1]
    rows = TOKENS // 2
    tile = pl.BlockSpec((1, rows, width), lambda w: (w, part, 0))
    grad = pl.BlockSpec((1, rows, 384), lambda w: (w, part, 0))

    def kernel(*refs):
        qkv_back_kernel(*refs)

    return pl.pallas_call(
        kernel,
        grid=(2,),
        in_specs=[grad] * 4 + [tile] * 2 + [whole(w_groups.shape), whole((1, width))],
        out_specs=[
            pl.BlockSpec((1, rows, width), lambda w: (w, 0, 0)),
            pl.BlockSpec((1, rows // 2, width), lambda w: (w, 0, 0)),
        ],
        out_shape=[
            jax.ShapeDtypeStruct((2, rows, width), F32),
            jax.ShapeDtypeStruct((2, rows // 2, width), BF16),
        ],
        scratch_shapes=[pltpu.VMEM((rows, width), F32)],
        compiler_params=pltpu.CompilerParams(vmem_limit_bytes=60 << 20),
        cost_estimate=cost(11),
        name="qkv_back",
    )(*grads, x, middle_grad, w_groups, gain[None])


def place_kernel(parts, edge_ref, *refs):
    vol = pl.program_id(0)
    owns, alts = refs[:parts], refs[parts : 2 * parts]
    belows, aboves = refs[2 * parts : 3 * parts], refs[3 * parts : 4 * parts]
    out_ref, doubled = refs[4 * parts :]
    size = TOKENS // parts
    edge = edge_ref[vol] == 1
    for part in range(parts):
        here = doubled.at[pl.ds(part * size, size)]

        @pl.when(jnp.logical_and(vol == 0, jnp.logical_not(edge)))
        def _():
            spread_message(belows[part], here)

        @pl.when(jnp.logical_and(vol == 1, jnp.logical_not(edge)))
        def _():
            spread_message(aboves[part], here)

        @pl.when(edge)
        def _():
            here[...] = alts[part][0].astype(F32)

    width = out_ref.shape[-1]
    low = row_half((WT, width)) == (vol == 0)
    for slot in range(0, len(SLOTS), 2):
        part, at = slot * WT // size, slot * WT % size
        both = owns[part][0, at : at + 2 * WT, :].astype(F32)
        for k in range(2):
            place = SLOTS[slot + k]
            if place is None:
                continue
            own = turned(both[k * WT : k * WT + WT])
            other = doubled[(slot + k) * WT : (slot + k + 1) * WT, :]
            out_ref[0, place[0], place[1]] = jnp.where(low, other, own).astype(out_ref.dtype)


def to_frames(edges, tokens, belows, aboves):
    parts = len(tokens)
    size = TOKENS // parts
    width = tokens[0].shape[-1]
    dtype = tokens[0].dtype
    lanes = 256
    own = pl.BlockSpec((1, size, lanes), lambda v, c, e: (v, 0, c))
    alt = pl.BlockSpec((1, size, lanes), lambda v, c, e: ((1 - v) * e[v], 0, c * e[v]))
    message = pl.BlockSpec((size // 2, lanes), lambda v, c, e: (0, c))
    return pl.pallas_call(
        functools.partial(place_kernel, parts),
        grid_spec=pltpu.PrefetchScalarGridSpec(
            num_scalar_prefetch=1,
            grid=(2, width // lanes),
            in_specs=[own] * parts + [alt] * parts + [message] * (2 * parts),
            out_specs=pl.BlockSpec((1, SIDE, SIDE, WT, lanes), lambda v, c, e: (v, 0, 0, 0, c)),
            scratch_shapes=[pltpu.VMEM((TOKENS, lanes), F32)],
        ),
        out_shape=jax.ShapeDtypeStruct((2, SIDE, SIDE, WT, width), dtype),
        compiler_params=pltpu.CompilerParams(vmem_limit_bytes=60 << 20),
        cost_estimate=cost(6),
        name="to_frames",
    )(edges, *tokens, *tokens, *belows, *aboves)


def tie(value, *after):
    return lax.optimization_barrier((value,) + after)[0]


def pick(array, index, axis=0):
    return lax.dynamic_index_in_dim(array, index, axis, keepdims=False)


def add_low(*values):
    return sum(v.astype(F32) for v in values).astype(BF16)


class Sum:
    def __init__(self, buffer):
        self.n = lax.axis_size("tm")
        self.size = lax.axis_size("dp")
        self.m = self.size // 2
        dp = lax.axis_index("dp")
        self.core, self.chip, self.plane = dp % 2, dp // 2, lax.axis_index("tm")
        rows, width = buffer.shape
        self.piece = (rows // (2 * self.m * self.n), width)
        self.whole = buffer.reshape((self.m, 2, self.n) + self.piece)

    def to_core(self, values):
        return lax.ppermute(values, "dp", [(i, i ^ 1) for i in range(self.size)])

    def to_chip(self, values, s):
        return lax.ppermute(values, "dp", [(i, i ^ (2 * s)) for i in range(self.size)])

    def to_plane(self, values, s):
        return lax.ppermute(values, "tm", [(i, i ^ s) for i in range(self.n)])

    def step0(self):
        self.got = self.to_core(pick(self.whole, 1 - self.core, 1))
        return self

    def step1(self):
        mine = pick(self.whole, self.core, 1)
        parts = [add_low(pick(mine, self.chip ^ s), pick(self.got, self.chip ^ s)) for s in range(self.m)]
        self.mine = parts[0]
        self.got = [self.to_chip(parts[s], s) for s in range(1, self.m)]
        return parts[-1]

    def step2(self):
        total = add_low(self.mine, *self.got)
        parts = [pick(total, self.plane ^ s) for s in range(self.n)]
        self.mine = parts[0]
        self.got = [self.to_plane(parts[s], s) for s in range(1, self.n)]
        return parts[-1]

    def step3(self):
        self.mine = add_low(self.mine, *self.got)
        return self.mine

    def gathered(self):
        return lax.all_gather(self.mine, ("dp", "tm"), tiled=True)

    def step3_back(self):
        self.step3()
        self.got = [self.to_plane(self.mine, s) for s in range(1, self.n)]
        return self.mine

    def step4_back(self):
        self.mine = jnp.stack([self.mine] + self.got)
        self.got = [self.to_chip(self.mine, s) for s in range(1, self.m)]
        return self.mine

    def step5_back(self):
        self.mine = jnp.stack([self.mine] + self.got)
        self.other = self.to_core(self.mine)
        return self.mine


EXTRA_TILES = 4
EXTRA_TABLE = 16


def pack_kernel(groups, *refs):
    pieces, strips, colsums = refs[:groups], refs[groups : 2 * groups], refs[2 * groups : 3 * groups]
    small_ref, fc1b_ref, out_ref, extra = refs[3 * groups :]
    width = pieces[0].shape[0]
    for g in range(groups):
        out_ref[g * width : (g + 1) * width, :] = pieces[g][...]
    extra[...] = jnp.zeros_like(extra)
    for g in range(groups):
        extra[g : g + 1, :] = jnp.sum(colsums[g][...], axis=0, keepdims=True)
    vectors = [jnp.sum(small_ref[i], axis=0, keepdims=True) for i in range(4)]
    vectors.append(jnp.sum(fc1b_ref[...], axis=0, keepdims=True))
    vectors = jnp.concatenate(vectors, axis=1)
    for t in range(vectors.shape[1] // 128):
        row, at = EXTRA_TILES + t // 3, t % 3 * 128
        extra[row : row + 1, at : at + 128] = vectors[:, t * 128 : t * 128 + 128]
    rows = strips[0].shape[0] // WT
    totals = [jnp.zeros((rows, ACROSS * (2 * WT - 1)), F32) for _ in range(groups)]
    for tk in range(WT):
        hot = hot_times(tk)
        for g in range(groups):
            for part in split3(strips[g][pl.ds(tk, rows, stride=WT), :]):
                totals[g] = totals[g] + nt(part, hot)
    for g in range(groups):
        at = EXTRA_TABLE + g * rows
        extra[at : at + rows, : totals[g].shape[1]] = totals[g]
    out_ref[groups * width :, :] = extra[...].astype(BF16)


def pack(pieces, strips, colsums, small, fc1b, unit_rows):
    groups = len(pieces)
    width, lanes = pieces[0].shape
    extras = EXTRA_TABLE + groups * strips[0].shape[0] // WT
    rows = up_to(groups * width + extras, unit_rows)
    return pl.pallas_call(
        functools.partial(pack_kernel, groups),
        out_shape=jax.ShapeDtypeStruct((rows, lanes), BF16),
        scratch_shapes=[pltpu.VMEM((rows - groups * width, lanes), F32)],
        compiler_params=pltpu.CompilerParams(vmem_limit_bytes=40 << 20),
        cost_estimate=cost(4),
        name="pack_sums",
    )(*pieces, *strips, *colsums, small, fc1b)


def finish_kernel(m, n, groups, ids_ref, mine_ref, other_ref, w_ref, gain_ref, bias_ref, *refs):
    gw_ref, lg_ref, lb_ref, qb_ref, vb_ref, s0, s1, s2, s3, fc1b_ref, table_ref, total = refs
    core, chip, plane = ids_ref[0], ids_ref[1], ids_ref[2]
    rows = mine_ref.shape[1]
    for c in range(m):
        for k in range(2):
            for z in range(n):
                at = (chip ^ c) * n + (plane ^ z)
                block = jnp.where(core == k, mine_ref[at].astype(F32), other_ref[at].astype(F32))
                first = ((c * 2 + k) * n + z) * rows
                total[first : first + rows, :] = block
    width = w_ref.shape[0]
    base = groups * width
    gain = gain_ref[...]
    bias = bias_ref[...]
    products = jnp.zeros((width, 128), F32)
    row = jnp.zeros((1, width), F32)
    for g in range(groups):
        part = total[g * width : (g + 1) * width, :]
        sums = total[base + g : base + g + 1, :]
        grad = gain * part + bias * sums
        for third in range(3):
            lanes = slice(third * 128, third * 128 + 128)
            at = third * width + g * 128
            gw_ref[:, at : at + 128] = grad[:, lanes]
            weight = w_ref[:, at : at + 128]
            products = products + weight.astype(F32) * part[:, lanes]
            for piece in split3(jnp.broadcast_to(sums[:, lanes], (8, 128))):
                row = row + nt(piece, weight)[:1]
        qb_ref[:, g * 128 : g * 128 + 128] = sums[:, :128]
        vb_ref[:, g * 128 : g * 128 + 128] = sums[:, 256:]
    lb_ref[...] = row
    ones = jnp.ones((8, 128), BF16)
    lg_ref[...] = sum(nt(ones, piece) for piece in split3(products))[:1]
    targets = [(ref, p) for ref in (s0, s1, s2, s3, fc1b_ref) for p in range(ref.shape[1] // 128)]
    for t, (ref, p) in enumerate(targets):
        at = base + EXTRA_TILES + t // 3
        ref[:, p * 128 : p * 128 + 128] = total[at : at + 1, t % 3 * 128 : t % 3 * 128 + 128]
    table_ref[...] = total[base + EXTRA_TABLE : base + EXTRA_TABLE + table_ref.shape[0], : table_ref.shape[1]]


def finish(sums, w_qkv, gain, bias, hidden, heads):
    width = w_qkv.shape[0]
    groups = width // 128
    rows, lanes = sums.piece
    count = sums.m * sums.n
    ids = jnp.stack([sums.core, sums.chip, sums.plane])
    vector = jax.ShapeDtypeStruct((1, width), F32)
    return pl.pallas_call(
        functools.partial(finish_kernel, sums.m, sums.n, groups),
        in_specs=[scalars()] + [pl.BlockSpec(memory_space=pltpu.VMEM)] * 5,
        out_specs=[pl.BlockSpec(memory_space=pltpu.VMEM)] * 11,
        out_shape=[jax.ShapeDtypeStruct(w_qkv.shape, F32)]
        + [vector] * 8
        + [
            jax.ShapeDtypeStruct((1, hidden), F32),
            jax.ShapeDtypeStruct((heads * ACROSS, ACROSS * (2 * WT - 1)), F32),
        ],
        scratch_shapes=[pltpu.VMEM((2 * count * rows, lanes), F32)],
        compiler_params=pltpu.CompilerParams(vmem_limit_bytes=60 << 20),
        cost_estimate=cost(5),
        name="finish",
    )(
        ids,
        sums.mine.reshape(count, rows, lanes),
        sums.other.reshape(count, rows, lanes),
        w_qkv,
        gain[:, None],
        bias[:, None],
    )


def widen_kernel(blocks, in_ref, fc1_ref, fc2_ref, proj_ref):
    step = pl.program_id(0)

    @pl.when(step < blocks)
    def _():
        fc1_ref[...] = in_ref[...].astype(F32)

    @pl.when(jnp.logical_and(step >= blocks, step < 2 * blocks))
    def _():
        fc2_ref[...] = in_ref[...].astype(F32)

    @pl.when(step == 2 * blocks)
    def _():
        proj_ref[...] = in_ref[...].astype(F32)


def widen_grads(buffer, hidden):
    width = buffer.shape[1]
    blocks = hidden // width
    block = (width, width)
    return pl.pallas_call(
        functools.partial(widen_kernel, blocks),
        grid=(2 * blocks + 1,),
        in_specs=[pl.BlockSpec(block, lambda i: (i, 0))],
        out_specs=[
            pl.BlockSpec(block, lambda i: (0, jnp.minimum(i, blocks - 1))),
            pl.BlockSpec(block, lambda i: (jnp.clip(i - blocks, 0, blocks - 1), 0)),
            pl.BlockSpec(block, lambda i: (0, 0)),
        ],
        out_shape=[
            jax.ShapeDtypeStruct((width, hidden), F32),
            jax.ShapeDtypeStruct((hidden, width), F32),
            jax.ShapeDtypeStruct(block, F32),
        ],
        compiler_params=pltpu.CompilerParams(vmem_limit_bytes=40 << 20),
        cost_estimate=cost(5),
        name="widen_grads",
    )(buffer)


def neighbours():
    count = lax.axis_size("tm")
    down = [(i, i - 1) for i in range(1, count)]
    up = [(i, i + 1) for i in range(count - 1)]
    return down, up


def fetch_halves(field):
    down, up = neighbours()
    width = field.shape[-1]
    above = lax.ppermute(field[0, :, :, :SHIFT_T].reshape(PLACES * SHIFT_T, width), "tm", down)
    below = lax.ppermute(field[1, :, :, SHIFT_T:].reshape(PLACES * SHIFT_T, width), "tm", up)
    return above, below


def send_back(message):
    down, up = neighbours()
    return lax.ppermute(message[0], "tm", up), lax.ppermute(message[1], "tm", down)


def frame_facts(segments, keep):
    count = lax.axis_size("tm")
    me = lax.axis_index("tm")
    own = 2 * SHIFT_T
    first = me * own
    t = jnp.arange(SHIFT_T)
    zero, one = jnp.zeros((SHIFT_T,), jnp.int32), jnp.ones((SHIFT_T,), jnp.int32)
    top, bottom = me == count - 1, me == 0
    frames = jnp.stack(
        [
            jnp.concatenate([first + SHIFT_T + t, jnp.where(top, first + SHIFT_T + t, first + own + t)]),
            jnp.concatenate([jnp.where(bottom, t, first - SHIFT_T + t), first + t]),
        ]
    )
    volumes = jnp.stack(
        [jnp.concatenate([zero, jnp.where(top, one, zero)]), jnp.concatenate([jnp.where(bottom, zero, one), one])]
    )
    pick_frame = (frames[:, :, None] == jnp.arange(segments.shape[1])).astype(jnp.int32)
    by_volume = jnp.sum(pick_frame[:, :, None, :] * segments[None, None], axis=-1)
    segment = jnp.where(volumes == 0, by_volume[..., 0], by_volume[..., 1])
    key = segment + 8 * (frames < SHIFT_T) + 16 * volumes
    apart = (key[:, :, None] != key[:, None, :]).astype(F32) * FAR
    far = jnp.tile(apart, (1, 1, 128 // WT))
    seg_hot = (segment[:, :, None] == jnp.arange(keep.shape[2])).astype(F32)
    kept = jnp.where(volumes[:, :, None, None] == 0, keep[0], keep[1]).astype(F32)
    drops = jnp.sum(seg_hot[:, :, None, :] * kept, axis=-1) / KEEP_RATE
    drops = jnp.broadcast_to(drops[..., None], drops.shape + (128,))
    return far, drops[:, :, 0], drops[:, :, 1]


def shards(
    volume,
    segments,
    keep,
    ln1_gain,
    ln1_bias,
    w_qkv,
    q_bias,
    v_bias,
    rel_table,
    w_proj,
    proj_bias,
    ln2_gain,
    ln2_bias,
    w_fc1,
    fc1_bias,
    w_fc2,
    fc2_bias,
    cotangent,
):
    width = volume.shape[-1]
    heads = rel_table.shape[1]
    dim = width // heads
    hidden = w_fc1.shape[1]
    groups = width // 128
    me = lax.axis_index("tm")
    top, bottom = me == lax.axis_size("tm") - 1, me == 0
    edges_in = jnp.stack([top, bottom]).astype(jnp.int32)
    edges_out = jnp.stack([bottom, top]).astype(jnp.int32)
    places = volume.transpose(0, 2, 3, 1, 4)
    cot = cotangent.transpose(0, 2, 3, 1, 4)
    above, below = fetch_halves(places)
    far, drop_attn, drop_mlp = frame_facts(segments, keep)
    biases = make_bias(rel_table)
    qkv_bias = jnp.concatenate([q_bias, jnp.zeros_like(q_bias), v_bias])
    w_groups = w_qkv.reshape(width, 3, groups, 128).transpose(0, 2, 1, 3).reshape(width, 3 * width)
    x, unit, q, k, v = make_qkv(
        edges_in, places, above, below, ln1_gain, ln1_bias, w_qkv, qkv_bias, dim**-0.5 * LOG2E
    )
    cot_above, cot_below = fetch_halves(tie(cot, q))
    *exps, att, inverse = attend(q, k, v, far, biases, dim)
    mixed, mixed_message, middle_grad, out_grad, g_mlp, small2, small_fc1 = mlp(
        edges_in,
        x,
        att,
        inverse,
        cot,
        cot_above,
        cot_below,
        drop_attn,
        drop_mlp,
        w_proj,
        proj_bias,
        ln2_gain,
        ln2_bias,
        w_fc1,
        fc1_bias,
        w_fc2,
        fc2_bias,
    )
    mixed_below, mixed_above = send_back(mixed_message)
    mlp_sum = Sum(g_mlp).step0()
    grads, pieces, sums, strips = [], [], [], []
    wait = mlp_sum.whole
    for group in range(groups):
        d, gw, colsum, strip = attend_back(group, q, k, v, tie(out_grad, wait), att, unit, exps, dim)
        grads.append(d)
        pieces.append(gw)
        sums.append(colsum)
        strips.append(strip)
        if group < 3:
            mlp_sum.got = lax.optimization_barrier((mlp_sum.got, d))[0]
            wait = (mlp_sum.step1, mlp_sum.step2, mlp_sum.step3)[group]()
    all_mlp = mlp_sum.gathered()
    unit_rows = 8 * lax.axis_size("dp") * lax.axis_size("tm")
    qkv_sum = Sum(pack(pieces, strips, sums, small2, small_fc1, unit_rows)).step0()
    grad0, message0 = qkv_back(0, grads, tie(x, qkv_sum.whole), middle_grad, w_groups, ln1_gain)
    below0, above0 = send_back(message0)
    qkv_sum.got = tie(qkv_sum.got, grad0)
    wait = qkv_sum.step1()
    grad1, message1 = qkv_back(1, grads, tie(x, wait, message0), middle_grad, w_groups, ln1_gain)
    below1, above1 = send_back(message1)
    qkv_sum.got = lax.optimization_barrier((qkv_sum.got, grad1))[0]
    wait = qkv_sum.step2()
    mixed_out = to_frames(edges_out, [tie(mixed, wait)], [mixed_below], [mixed_above])
    qkv_sum.got = lax.optimization_barrier((qkv_sum.got, mixed_out))[0]
    wait = qkv_sum.step3_back()
    g_fc1, g_fc2, g_proj = widen_grads(tie(all_mlp, wait), hidden)
    qkv_sum.got = lax.optimization_barrier((qkv_sum.got, g_fc1))[0]
    wait = qkv_sum.step4_back()
    volume_grad = to_frames(edges_out, [tie(grad0, wait), grad1], [below0, below1], [above0, above1])
    qkv_sum.got = lax.optimization_barrier((qkv_sum.got, volume_grad))[0]
    qkv_sum.step5_back()
    g_qkv, ln1_g, ln1_b, q_b, v_b, fc2_b, ln2_g, ln2_b, proj_b, fc1_b, table = finish(
        qkv_sum, w_qkv, ln1_gain, ln1_bias, hidden, heads
    )
    table = table.reshape(heads, ACROSS, 2 * WT - 1, ACROSS).transpose(0, 2, 1, 3).reshape(heads, -1).T
    return (
        mixed_out.transpose(0, 3, 1, 2, 4),
        volume_grad.transpose(0, 3, 1, 2, 4),
        ln1_g[0],
        ln1_b[0],
        g_qkv,
        q_b[0],
        v_b[0],
        table,
        g_proj,
        proj_b[0],
        ln2_g[0],
        ln2_b[0],
        g_fc1,
        fc1_b[0],
        g_fc2,
        fc2_b[0],
    )


def solution(mesh):
    split = P("dp", "tm", None, None, None)
    return jax.shard_map(
        shards,
        mesh=mesh,
        in_specs=(split, P("dp", None), P("dp", None, None)) + (P(),) * 14 + (split,),
        out_specs=(split, split) + (P(),) * 14,
        check_vma=False,
    )
```

```python
import functools

import jax
import jax.numpy as jnp
import numpy as np
from jax import lax
from jax.experimental import pallas as pl
from jax.experimental.pallas import tpu as pltpu
from jax.sharding import PartitionSpec as P

SIDE = 14
WT = 8
WIN_HW = 7
SHIFT_T = 4
SHIFT_HW = 3
EPS = 1e-05
KEEP_RATE = 0.75
PRECISE = lax.Precision.HIGHEST
LOG2E = 1.4426950408889634
LN2 = 0.6931471805599453
FAR = 1e30
F32 = jnp.float32
BF16 = jnp.bfloat16

SPANS = (
    (SHIFT_HW, WIN_HW),
    (SHIFT_HW + WIN_HW, SIDE - SHIFT_HW - WIN_HW),
    (0, SHIFT_HW),
)
ACROSS = 2 * WIN_HW - 1
RECTS = (
    (0, 0, True, 0),
    (1, 0, True, 0),
    (0, 1, False, 1),
    (2, 0, True, 0),
    (0, 2, False, 1),
    (2, 2, True, 3),
    (2, 1, True, 2),
    (1, 2, True, 3),
    (1, 1, True, 2),
)
BIAS_DIMS = ((7, 7), (4, 7), (4, 4), (4, 3))


def up_to(value, unit):
    return -(-value // unit) * unit


class Rect:
    pass


def plan_rects():
    rects, slots, start, lane_start = [], [], 0, 0
    class_rows = [0, 0, 0]
    for row_span, col_span, rows_outer, table in RECTS:
        r0, rn = SPANS[row_span]
        c0, cn = SPANS[col_span]
        rect = Rect()
        if rows_outer:
            places = [(r0 + a, c0 + b) for a in range(rn) for b in range(cn)]
        else:
            places = [(r0 + b, c0 + a) for a in range(cn) for b in range(rn)]
        rect.count = len(places) * WT
        rect.rows = up_to(rect.count, 16)
        rect.lanes = up_to(rect.count, 128)
        rect.start = start
        rect.table = table
        rect.kind = {512: 0, 256: 1, 128: 2}[rect.lanes]
        rect.kind_row = class_rows[rect.kind]
        class_rows[rect.kind] += rect.rows
        slots += places + [None] * ((rect.rows - rect.count) // WT)
        start += rect.rows
        rect.lane_start = lane_start
        lane_start += rect.lanes
        rects.append(rect)
    return rects, slots, class_rows


RECT, SLOTS, KIND_ROWS = plan_rects()
TOKENS = len(SLOTS) * WT
ALL_LANES = sum(rect.lanes for rect in RECT)
KIND_LANES = (512, 256, 128)
PLACES = SIDE * SIDE


def nn(a, b):
    return lax.dot_general(a, b, (((1,), (0,)), ((), ())), preferred_element_type=F32)


def nt(a, b):
    return lax.dot_general(a, b, (((1,), (1,)), ((), ())), preferred_element_type=F32)


def wide(pattern, width):
    return jnp.concatenate([pattern] * (width // pattern.shape[-1]), axis=-1)


def by_frame(values, pattern):
    rows, width = values.shape
    scaled = values.reshape(rows // WT, WT, width) * wide(pattern, width)[None]
    return scaled.reshape(rows, width)


def column_sums(values):
    rows, width = values.shape
    return jnp.sum(values.reshape(rows // 8, 8, width), axis=0)


def row_half(shape):
    return (lax.broadcasted_iota(jnp.int32, shape, 0) & (WT - 1)) < SHIFT_T


def turned(tile):
    return pltpu.roll(tile, SHIFT_T, 0)


def spread_message(message_ref, late, doubled):
    def pair(i, carry):
        both = message_ref[pl.ds(pl.multiple_of(i * 16, 16), 16), :].astype(F32)
        for k in range(2):
            tile = both[k * WT : k * WT + WT]
            at = pl.multiple_of(i * 32 + k * 16, 16)
            first, second = (turned(tile), tile) if late else (tile, turned(tile))
            doubled[pl.ds(at, WT), :] = first
            doubled[pl.ds(at + WT, WT), :] = second
        return carry

    lax.fori_loop(0, message_ref.shape[0] // 16, pair, 0)


def assemble_tokens(win, edge_ref, own_ref, alt_ref, above_ref, below_ref, doubled, tokens):
    edge = edge_ref[win] == 1
    inner = jnp.logical_not(edge)

    @pl.when(jnp.logical_and(inner, win == 0))
    def _():
        spread_message(above_ref, False, doubled)

    @pl.when(jnp.logical_and(inner, win == 1))
    def _():
        spread_message(below_ref, True, doubled)

    @pl.when(edge)
    def _():
        def row(h, carry):
            for w in range(SIDE):
                at = pl.multiple_of((h * SIDE + w) * WT, WT)
                doubled[pl.ds(at, WT), :] = turned(alt_ref[0, h, w].astype(F32))
            return carry

        lax.fori_loop(0, SIDE, row, 0)

    width = tokens.shape[1]
    from_other = row_half((WT, width)) == (win == 0)
    for slot, place in enumerate(SLOTS):
        rows = slice(slot * WT, slot * WT + WT)
        if place is None:
            tokens[rows, :] = jnp.zeros((WT, width), F32)
            continue
        h, w = place
        at = (h * SIDE + w) * WT
        tokens[rows, :] = jnp.where(from_other, doubled[at : at + WT, :], own_ref[0, h, w].astype(F32))


def pack_message(late, tokens, message_ref):
    def pair(i, carry):
        both = tokens[pl.ds(pl.multiple_of(i * 32, 32), 32), :]
        tiles = []
        for k in range(2):
            one, two = both[k * 16 : k * 16 + WT], both[k * 16 + WT : k * 16 + 16]
            low = row_half(one.shape)
            tiles.append(jnp.where(low, turned(one), two) if late else jnp.where(low, one, turned(two)))
        packed = jnp.concatenate(tiles, axis=0).astype(message_ref.dtype)
        message_ref[pl.ds(pl.multiple_of(i * 16, 16), 16), :] = packed
        return carry

    lax.fori_loop(0, tokens.shape[0] // 32, pair, 0)


def spread_table(source, outer, inner, out_ref, lane):
    width = inner * WT
    total = outer * width
    for ok in range(outer):
        for ik in range(inner):
            pieces = []
            for oq in range(outer):
                shift = (oq * width - (WIN_HW - 1 - ik) * WT) % 128
                piece = source[oq - ok + WIN_HW - 1]
                pieces.append(pltpu.roll(piece, shift, 1) if shift else piece)
            row = (ok * inner + ik) * WT
            for tile in range(up_to(total, 128) // 128):
                value = None
                for oq in range(outer):
                    begin, end = oq * width, (oq + 1) * width
                    if end <= tile * 128 or begin >= tile * 128 + 128:
                        continue
                    if value is None:
                        value = pieces[oq]
                    else:
                        value = jnp.where(lane >= begin - tile * 128, pieces[oq], value)
                out_ref[0, row : row + WT, tile * 128 : tile * 128 + 128] = value


def split3(values):
    parts = []
    for _ in range(3):
        part = values.astype(BF16)
        parts.append(part)
        values = values - part.astype(F32)
    return parts


def hot_times(tk):
    count = ACROSS * (2 * WT - 1)
    place = lax.broadcasted_iota(jnp.int32, (count, 128), 0)
    lane = lax.broadcasted_iota(jnp.int32, (count, 128), 1)
    tk = (tk + SHIFT_T) % WT
    tq = (lane + SHIFT_T) & (WT - 1)
    d = lax.shift_right_logical(lane, 3)
    return (((tq - tk + WT - 1) * ACROSS + d == place) & (d < ACROSS)).astype(BF16)


def lane_roll(tile, shift):
    shift = shift % 128
    return pltpu.roll(tile, shift, 1) if shift else tile


def lane_block(lane, d):
    return (lane >= d * WT) & (lane < d * WT + WT)


def bias_kernel(table_ref, b0_ref, b1_ref, b2_ref, b3_ref, strips):
    head = pl.program_id(0)

    @pl.when(head == 0)
    def _():
        parts = split3(table_ref[...] * LOG2E)
        for tk in range(WT):
            hot = hot_times(tk)
            strips[pl.ds(tk, table_ref.shape[0], stride=WT), :] = sum(nn(p, hot) for p in parts)

    lane = lax.broadcasted_iota(jnp.int32, (WT, 128), 1)
    base = pl.multiple_of(head * (ACROSS * WT), WT)
    by_rows = [strips[pl.ds(base + d * WT, WT), :] for d in range(ACROSS)]
    by_cols = [None] * ACROSS
    reach = BIAS_DIMS[1][0] - 1
    for d in range(WIN_HW - 1 - reach, WIN_HW + reach):
        by_cols[d] = sum(
            jnp.where(lane_block(lane, e), lane_roll(by_rows[e], (e - d) * WT), 0.0) for e in range(ACROSS)
        )
    for out_ref, source, (outer, inner) in zip(
        (b0_ref, b1_ref, b2_ref, b3_ref), (by_rows, by_cols, by_rows, by_rows), BIAS_DIMS
    ):
        spread_table(source, outer, inner, out_ref, lane)


def bias_shapes(heads):
    shapes = []
    for outer, inner in BIAS_DIMS:
        count = outer * inner * WT
        shapes.append((heads, count, up_to(count, 128)))
    return shapes


def make_bias(rel_table):
    heads = rel_table.shape[1]
    times = 2 * WT - 1
    cube = rel_table.T.reshape(heads, times, ACROSS, ACROSS)
    table = cube.transpose(0, 2, 1, 3).reshape(heads * ACROSS, times * ACROSS)
    shapes = bias_shapes(heads)
    return pl.pallas_call(
        bias_kernel,
        grid=(heads,),
        in_specs=[whole(table.shape)],
        out_specs=[pl.BlockSpec((1,) + s[1:], lambda h: (h, 0, 0)) for s in shapes],
        out_shape=[jax.ShapeDtypeStruct(s, F32) for s in shapes],
        scratch_shapes=[pltpu.VMEM((heads * ACROSS * WT, 128), F32)],
        compiler_params=pltpu.CompilerParams(vmem_limit_bytes=60 << 20),
        cost_estimate=cost(10),
        name="position_bias",
    )(table)


def fold_matrices():
    tiles = []
    for tile in range(4):
        tiles.append(np.zeros((WIN_HW * 128, 512), np.float32))
        for ik in range(WIN_HW):
            for lane in range(128):
                query = tile * 128 + lane
                oq, iq, frame = query // (WIN_HW * WT), query // WT % WIN_HW, query % WT
                if query < WIN_HW * WIN_HW * WT:
                    block = oq - tile * 128 // (WIN_HW * WT)
                    tiles[-1][ik * 128 + lane, block * 128 + (iq - ik + WIN_HW - 1) * WT + frame] = 1
    for outer, inner in BIAS_DIMS[2:]:
        tiles.append(np.zeros((inner * 128, 512), np.float32))
        for ik in range(inner):
            for lane in range(outer * inner * WT):
                oq, iq, frame = lane // (inner * WT), lane // WT % inner, lane % WT
                tiles[-1][ik * 128 + lane, oq * 128 + (iq - ik + WIN_HW - 1) * WT + frame] = 1
    return jnp.asarray(np.concatenate(tiles)).astype(BF16)


FOLD_ROWS = (4 * WIN_HW + BIAS_DIMS[2][1] + BIAS_DIMS[3][1]) * 128


def fold_tables(accs, per, hots):
    by_rows = [[jnp.zeros((WT, 128), F32) for _ in range(ACROSS)] for _ in range(per)]
    by_cols = [[jnp.zeros((WT, 128), F32) for _ in range(ACROSS)] for _ in range(per)]

    def left(table, tile):
        outer, inner = BIAS_DIMS[table]
        lanes = slice(tile * 128, tile * 128 + 128)
        rows = []
        for head in range(per):
            for ok in range(outer):
                at = [(ok * inner + ik) * WT for ik in range(inner)]
                rows.append(jnp.concatenate([accs[table][head, a : a + WT, lanes] for a in at], axis=1))
        return jnp.concatenate(rows, axis=0).astype(BF16)

    def add(totals, table, part, first, blocks):
        outer, _ = BIAS_DIMS[table]
        for head in range(per):
            for ok in range(outer):
                for block in range(blocks):
                    oq = first + block
                    if oq >= outer:
                        continue
                    row = (head * outer + ok) * WT
                    d = oq - ok + WIN_HW - 1
                    totals[head][d] = totals[head][d] + part[row : row + WT, block * 128 : block * 128 + 128]

    for tile in range(4):
        first = tile * 128 // (WIN_HW * WT)
        blocks = min(3, WIN_HW - first)
        tables = (0, 1) if tile < 2 else (0,)
        hot = hots[tile * WIN_HW * 128 : (tile + 1) * WIN_HW * 128, : blocks * 128]
        part = nn(jnp.concatenate([left(t, tile) for t in tables], axis=0), hot)
        split = per * BIAS_DIMS[0][0] * WT
        add(by_rows, 0, part[:split], first, blocks)
        if len(tables) > 1:
            add(by_cols, 1, part[split:], first, blocks)
    at = 4 * WIN_HW * 128
    for table in (2, 3):
        outer, inner = BIAS_DIMS[table]
        part = nn(left(table, 0), hots[at : at + inner * 128, :])
        at += inner * 128
        add(by_rows, table, part, 0, outer)
    return by_rows, by_cols


def qkv_kernel(
    tile,
    scale,
    edge_ref,
    own_ref,
    alt_ref,
    above_ref,
    below_ref,
    gain_ref,
    bias_ref,
    w_ref,
    wb_ref,
    x_ref,
    n_ref,
    q_ref,
    k_ref,
    v_ref,
    doubled,
    tokens,
):
    win, step = pl.program_id(0), pl.program_id(1)

    @pl.when(step == 0)
    def _():
        assemble_tokens(win, edge_ref, own_ref, alt_ref, above_ref, below_ref, doubled, tokens)

    x = tokens[pl.ds(pl.multiple_of(step * tile, 16), tile), :]
    x_ref[0] = x.astype(BF16)
    unit, _ = norm_stats(x)
    n_ref[0] = unit.astype(BF16)
    normed = (unit * gain_ref[...] + bias_ref[...]).astype(BF16)
    width = x.shape[1]
    put_groups(q_ref, ((nn(normed, w_ref[:, :width]) + wb_ref[:, :width]) * scale).astype(BF16))
    put_groups(k_ref, nn(normed, w_ref[:, width : 2 * width]).astype(BF16))
    put_groups(v_ref, (nn(normed, w_ref[:, 2 * width :]) + wb_ref[:, 2 * width :]).astype(BF16))


def put_groups(ref, values):
    for g in range(ref.shape[1]):
        ref[0, g] = values[:, g * 128 : g * 128 + 128]


def get_groups(ref):
    return jnp.concatenate([ref[0, g] for g in range(ref.shape[1])], axis=-1)


def group_spec(tile, width):
    return pl.BlockSpec((1, width // 128, tile, 128), lambda w, j: (w, 0, j, 0))


def group_shape(width):
    return jax.ShapeDtypeStruct((2, width // 128, TOKENS, 128), BF16)


def cost(micros):
    return pl.CostEstimate(flops=int(micros * 1.1e9), bytes_accessed=1 << 20, transcendentals=0)


def norm_stats(values):
    centre = values - jnp.mean(values, axis=-1, keepdims=True)
    spread = jnp.mean(centre * centre, axis=-1, keepdims=True)
    inverse = lax.rsqrt(spread + EPS)
    return centre * inverse, inverse


def norm_back(scaled, unit, inverse):
    first = jnp.mean(scaled, axis=-1, keepdims=True)
    second = jnp.mean(scaled * unit, axis=-1, keepdims=True)
    return (scaled - first - unit * second) * inverse


def whole(shape):
    return pl.BlockSpec(shape, lambda *_: (0,) * len(shape))


def scalars():
    return pl.BlockSpec(memory_space=pltpu.SMEM)


def volume_specs(width):
    block = (1, SIDE, SIDE, WT, width)
    return [
        pl.BlockSpec(block, lambda w, *_: (w, 0, 0, 0, 0)),
        pl.BlockSpec(block, lambda w, *_: (1 - w, 0, 0, 0, 0)),
        whole((PLACES * SHIFT_T, width)),
        whole((PLACES * SHIFT_T, width)),
    ]


def tile_spec(tile, width):
    return pl.BlockSpec((1, tile, width), lambda w, j: (w, j, 0))


def make_qkv(edges, volume, above, below, gain, bias, w_qkv, qkv_bias, scale, tile=400):
    width = volume.shape[-1]
    out = jax.ShapeDtypeStruct((2, TOKENS, width), BF16)
    return pl.pallas_call(
        functools.partial(qkv_kernel, tile, scale),
        grid=(2, TOKENS // tile),
        in_specs=[scalars()]
        + volume_specs(width)
        + [whole((1, width)), whole((1, width)), whole(w_qkv.shape), whole((1, 3 * width))],
        out_specs=[tile_spec(tile, width)] * 2 + [group_spec(tile, width)] * 3,
        out_shape=[out] * 2 + [group_shape(width)] * 3,
        scratch_shapes=[
            pltpu.VMEM((PLACES * WT, width), F32),
            pltpu.VMEM((TOKENS, width), F32),
        ],
        compiler_params=pltpu.CompilerParams(vmem_limit_bytes=60 << 20),
        cost_estimate=cost(17),
        name="norm1_qkv",
    )(edges, volume, volume, above, below, gain[None], bias[None], w_qkv, qkv_bias[None])


def head_rows(transposed, head, dim):
    rows, lanes = transposed.shape
    parts = []
    if head:
        parts.append(jnp.zeros((head * dim, lanes), transposed.dtype))
    parts.append(transposed[head * dim : head * dim + dim])
    if (head + 1) * dim < rows:
        parts.append(jnp.zeros((rows - (head + 1) * dim, lanes), transposed.dtype))
    return jnp.concatenate(parts, axis=0)


def attend_kernel(
    dim, q_ref, k_ref, v_ref, far_ref, b0, b1, b2, b3, e0_ref, e1_ref, e2_ref, o_ref, r_ref, *scores
):
    biases = (b0, b1, b2, b3)
    e_refs = (e0_ref, e1_ref, e2_ref)
    far = far_ref[0]
    per = 128 // dim
    ones = jnp.ones((16, RECT[0].rows), BF16)
    operands = {}

    def prepare(rect):
        if rect not in operands:
            queries = q_ref[0, 0, rect.start : rect.start + rect.lanes, :].T
            values = v_ref[0, 0, rect.start : rect.start + rect.rows, :].T
            operands[rect] = queries, k_ref[0, 0, rect.start : rect.start + rect.rows, :], values, []
        return operands[rect]

    def score(rect, head, buffer):
        queries, keys, _, _ = prepare(rect)
        count, lanes = rect.count, rect.lanes
        raw = nn(keys, head_rows(queries, head, dim))[:count]
        raw = raw + biases[rect.table][head, :count, :lanes]
        buffer[:count, :lanes] = raw
        wide_far = wide(far, lanes)
        top = jnp.max(raw.reshape(count // 8, 8, lanes), axis=0) - wide_far
        return jnp.max(top, axis=0, keepdims=True) + wide_far

    def exponents(rect, head, buffer, top):
        count, rows, lanes = rect.count, rect.rows, rect.lanes
        exps = jnp.exp2(buffer[:count, :lanes].reshape(count // 8, 8, lanes) - top[None])
        exps = exps.reshape(count, lanes).astype(BF16)
        if rows > count:
            exps = jnp.concatenate([exps, jnp.zeros((rows - count, lanes), BF16)], axis=0)
        place = slice(rect.kind_row, rect.kind_row + rows), slice(head * lanes, head * lanes + lanes)
        e_refs[rect.kind][(0, 0) + place] = exps
        return exps

    def weigh(rect, head, exps):
        _, _, values, outs = prepare(rect)
        rows, lanes, start = rect.rows, rect.lanes, rect.start
        lhs = jnp.concatenate([values[head * dim : head * dim + dim], ones[:, :rows]], axis=0)
        out = nn(lhs, exps)
        inverse = 1.0 / out[dim : dim + 1]
        outs.append(out[:dim] * inverse)
        r_ref[0, 0, head : head + 1, rect.lane_start : rect.lane_start + lanes] = inverse
        if len(outs) == per:
            o_ref[0, 0, start : start + rows, :] = jnp.concatenate(outs, axis=0).T[:rows].astype(BF16)

    units = [(rect, head) for rect in RECT for head in range(per)]
    tops, exps = {}, {}
    for i in range(len(units) + 2):
        if i < len(units):
            tops[i] = score(*units[i], scores[i % len(scores)])
        if 0 <= i - 1 < len(units):
            exps[i - 1] = exponents(*units[i - 1], scores[(i - 1) % len(scores)], tops.pop(i - 1))
        if 0 <= i - 2:
            weigh(*units[i - 2], exps.pop(i - 2))


def head_group_specs(heads, per, biases):
    lane_tile = pl.BlockSpec((1, 1, TOKENS, 128), lambda g, w: (w, g, 0, 0))
    far = pl.BlockSpec((1, WT, 128), lambda g, w: (w, 0, 0))
    bias = [pl.BlockSpec((per,) + b[1:], lambda g, w: (g, 0, 0)) for b in biases]
    exps = [
        pl.BlockSpec((1, 1, KIND_ROWS[i], per * KIND_LANES[i]), lambda g, w: (w, g, 0, 0)) for i in range(3)
    ]
    return lane_tile, far, bias, exps


def exps_shapes(groups, per):
    return [jax.ShapeDtypeStruct((2, groups, KIND_ROWS[i], per * KIND_LANES[i]), BF16) for i in range(3)]


def attend(q, k, v, far, biases, dim):
    groups = q.shape[1]
    per = 128 // dim
    heads = groups * per
    lane_tile, far_spec, bias_specs, exps_specs = head_group_specs(heads, per, [b.shape for b in biases])
    return pl.pallas_call(
        functools.partial(attend_kernel, dim),
        grid=(groups, 2),
        in_specs=[lane_tile] * 3 + [far_spec] + bias_specs,
        out_specs=exps_specs + [lane_tile, pl.BlockSpec((1, 1, per, ALL_LANES), lambda g, w: (w, g, 0, 0))],
        out_shape=exps_shapes(groups, per)
        + [group_shape(groups * 128), jax.ShapeDtypeStruct((2, groups, per, ALL_LANES), F32)],
        scratch_shapes=[pltpu.VMEM((RECT[0].count, RECT[0].lanes), F32)] * 3,
        compiler_params=pltpu.CompilerParams(vmem_limit_bytes=60 << 20),
        cost_estimate=cost(55),
        name="attention",
    )(q, k, v, far, *biases)


def attend_back_kernel(
    dim,
    scale,
    q_ref,
    k_ref,
    v_ref,
    g_ref,
    o_ref,
    r_ref,
    n_ref,
    hot_ref,
    e0_ref,
    e1_ref,
    e2_ref,
    d_ref,
    gw_ref,
    sums_ref,
    strips_ref,
    a0,
    a1,
    a2,
    a3,
    acc_w,
    hots,
    hot_sem,
    *buffers,
):
    win = pl.program_id(1)
    first_group = pl.program_id(0) == 0
    hot_copy = pltpu.make_async_copy(hot_ref, hots, hot_sem)
    accs = (a0, a1, a2, a3)
    e_refs = (e0_ref, e1_ref, e2_ref)
    grads, queries, outgrads, probs = buffers[:2], buffers[2:4], buffers[4:6], buffers[6:]
    per = 128 // dim
    lane = lax.broadcasted_iota(jnp.int32, (1, 128), 1)
    mine = [((lane >= h * dim) & (lane < h * dim + dim)).astype(BF16) for h in range(per)]

    @pl.when(win == 0)
    def _():
        acc_w[...] = jnp.zeros_like(acc_w)
        sums_ref[...] = jnp.zeros_like(sums_ref)

    @pl.when(jnp.logical_and(first_group, win == 0))
    def _():
        hot_copy.start()

    operands, parity = {}, {}

    def prepare(index):
        if index not in operands:
            parity[index] = len(parity) % 2
            rect = RECT[index]
            rows, lanes, start = rect.rows, rect.lanes, rect.start
            out_grad = g_ref[0, 0, start : start + rows, :]
            if lanes > rows:
                out_grad = jnp.concatenate([out_grad, jnp.zeros((lanes - rows, 128), BF16)], axis=0)
            query = q_ref[0, 0, start : start + lanes, :]
            inverse = r_ref[0, 0, :, rect.lane_start : rect.lane_start + lanes]
            inverse = [jnp.broadcast_to(inverse[h : h + 1], (dim, lanes)) for h in range(per)]
            out_grad_t = (out_grad.T.astype(F32) * jnp.concatenate(inverse, axis=0)).astype(BF16)
            out_grad = out_grad_t.T
            out_t = o_ref[0, 0, start : start + lanes, :].T
            keys_t = k_ref[0, 0, start : start + rows, :].T
            product = out_grad_t.astype(F32) * out_t.astype(F32)
            for head in range(per):
                here = slice(head * lanes, head * lanes + lanes)
                queries[parity[index]][here, :] = query * mine[head]
                outgrads[parity[index]][here, :] = out_grad * mine[head]
            operands[index] = out_grad_t, keys_t, product, []
        return operands[index]

    def first(index, head, buffer):
        out_grad_t, _, product, _ = prepare(index)
        rect = RECT[index]
        values = v_ref[0, 0, rect.start : rect.start + rect.rows, :]
        buffer[: rect.rows, : rect.lanes] = nn(values, head_rows(out_grad_t, head, dim))
        return jnp.sum(product[head * dim : head * dim + dim], axis=0, keepdims=True)

    def second(index, head, buffer, inner):
        rect = RECT[index]
        count, rows, lanes = rect.count, rect.rows, rect.lanes
        here = slice(head * lanes, head * lanes + lanes)
        exps = e_refs[rect.kind][0, 0, rect.kind_row : rect.kind_row + rows, here].astype(F32)
        score_grad = exps * (buffer[:rows, :lanes] - inner)
        acc = accs[rect.table]
        total = score_grad[:count] + acc[head, :count, :lanes]
        if (count, lanes) == acc.shape[1:]:
            total = jnp.where(win == 0, score_grad[:count], total)
        acc[head, :count, :lanes] = total
        low = score_grad.astype(BF16)
        grads[parity[index]][:rows, here] = low
        return low

    def third(index, head, low):
        _, keys_t, _, dqs = prepare(index)
        dqs.append(nn(keys_t[head * dim : head * dim + dim], low))
        if len(dqs) < per:
            return
        rect = RECT[index]
        rows, lanes, start = rect.rows, rect.lanes, rect.start
        dq = jnp.concatenate(dqs, axis=0) * scale
        d_ref[0, start : start + rows, :128] = dq.T[:rows].astype(BF16)
        dk = nn(grads[parity[index]][:rows, : per * lanes], queries[parity[index]][: per * lanes, :])
        d_ref[0, start : start + rows, 128:256] = (dk * LN2).astype(BF16)
        exps = e_refs[rect.kind][0, 0, rect.kind_row : rect.kind_row + rows, :]
        dv = nn(exps, outgrads[parity[index]][: per * lanes, :])
        d_ref[0, start : start + rows, 256:] = dv.astype(BF16)

    order = sorted(range(len(RECT)), key=lambda i: (RECT[i].kind, -RECT[i].count))
    units = [(index, head) for index in order for head in range(per)]
    inners, lows = {}, {}
    for i in range(len(units) + 2):
        if i < len(units):
            inners[i] = first(*units[i], probs[i % len(probs)])
        if 0 <= i - 1 < len(units):
            lows[i - 1] = second(*units[i - 1], probs[(i - 1) % len(probs)], inners.pop(i - 1))
        if 0 <= i - 2:
            third(*units[i - 2], lows.pop(i - 2))

    all_grads = d_ref[0]
    acc_w[...] += lax.dot_general(n_ref[0], all_grads, (((0,), (0,)), ((), ())), preferred_element_type=F32)
    sums_ref[...] += column_sums(all_grads.astype(F32))

    @pl.when(win == 1)
    def _():
        gw_ref[...] = acc_w[...].astype(BF16)
        lane8 = lax.broadcasted_iota(jnp.int32, (WT, 128), 1)

        @pl.when(first_group)
        def _():
            hot_copy.wait()

        all_rows, all_cols = fold_tables(accs, per, hots)
        for head in range(per):
            by_rows, by_cols = all_rows[head], all_cols[head]
            for d in range(ACROSS):
                for e in range(ACROSS):
                    if abs(e - WIN_HW + 1) < BIAS_DIMS[1][0]:
                        turned_back = lane_roll(by_cols[e], (e - d) * WT)
                        by_rows[d] = by_rows[d] + jnp.where(lane_block(lane8, e), turned_back, 0.0)
                strips_ref[(head * ACROSS + d) * WT : (head * ACROSS + d + 1) * WT, :] = by_rows[d]


def attend_back(first, groups, q, k, v, out_grad, out, inverse, unit, exps, dim):
    width = q.shape[1] * 128
    per = 128 // dim
    shapes = bias_shapes(per)
    lane_tile = pl.BlockSpec((1, 1, TOKENS, 128), lambda g, w: (w, first + g, 0, 0))
    exps_specs = [
        pl.BlockSpec((1, 1, KIND_ROWS[i], per * KIND_LANES[i]), lambda g, w: (w, first + g, 0, 0))
        for i in range(3)
    ]
    strip = (per * ACROSS * WT, 128)
    most = per * RECT[0].lanes
    return pl.pallas_call(
        functools.partial(attend_back_kernel, dim, dim**-0.5),
        grid=(groups, 2),
        in_specs=[lane_tile] * 5
        + [
            pl.BlockSpec((1, 1, per, ALL_LANES), lambda g, w: (w, first + g, 0, 0)),
            pl.BlockSpec((1, TOKENS, width), lambda g, w: (w, 0, 0)),
            pl.BlockSpec(memory_space=pl.ANY),
        ]
        + exps_specs,
        out_specs=[
            pl.BlockSpec((1, TOKENS, 384), lambda g, w: (w, 0, g)),
            pl.BlockSpec((width, 384), lambda g, w: (g, 0)),
            pl.BlockSpec((8, 384), lambda g, w: (g, 0)),
            pl.BlockSpec(strip, lambda g, w: (g, 0)),
        ],
        out_shape=[
            jax.ShapeDtypeStruct((2, TOKENS, groups * 384), BF16),
            jax.ShapeDtypeStruct((groups * width, 384), BF16),
            jax.ShapeDtypeStruct((groups * 8, 384), F32),
            jax.ShapeDtypeStruct((groups * strip[0], 128), F32),
        ],
        scratch_shapes=[pltpu.VMEM(s, F32) for s in shapes]
        + [
            pltpu.VMEM((width, 384), F32),
            pltpu.VMEM((FOLD_ROWS, 512), BF16),
            pltpu.SemaphoreType.DMA,
        ]
        + [pltpu.VMEM((RECT[0].rows, most), BF16)] * 2
        + [pltpu.VMEM((most, 128), BF16)] * 4
        + [pltpu.VMEM((RECT[0].rows, RECT[0].lanes), F32)] * 3,
        compiler_params=pltpu.CompilerParams(vmem_limit_bytes=60 << 20),
        cost_estimate=cost(18 * groups),
        name="attention_back",
    )(q, k, v, out_grad, out, inverse, unit, fold_matrices(), *exps)


ERFC = (0.254829592, -0.284496736, 1.421413741, -1.453152027, 1.061405429)
ERFC_P = 0.3275911


def gelu_both(u):
    denominator = 1.0 + (ERFC_P * 0.5**0.5) * jnp.abs(u)
    t = pl.reciprocal(denominator, approx=True)
    t = t * (2.0 - denominator * t)
    bell = jnp.exp2((u * u) * (-0.5 * LOG2E))
    series = 0.5 * ERFC[4]
    for factor in ERFC[3::-1]:
        series = series * t + 0.5 * factor
    tail = series * t * bell
    area = jnp.where(u >= 0.0, 1.0 - tail, tail)
    return u * area, area + (u * (1.0 / np.sqrt(2.0 * np.pi))) * bell


def mlp_kernel(
    tile,
    steps,
    chunk,
    parts,
    planes,
    edge_ref,
    x_ref,
    att_ref,
    own_ref,
    alt_ref,
    above_ref,
    below_ref,
    da_ref,
    dm_ref,
    wp_ref,
    pb_ref,
    g_ref,
    b_ref,
    w1_ref,
    b1_ref,
    w2_ref,
    b2_ref,
    mixed_ref,
    up_ref,
    down_ref,
    mg_ref,
    og_ref,
    mine_ref,
    theirs_ref,
    small_ref,
    fc1b_ref,
    doubled,
    tokens,
    acc_p,
    acc_1,
    acc_2,
    result,
    n2g,
    *buffers,
):
    hiddens, slopes = buffers[:2], buffers[2:]
    win, step = pl.program_id(0), pl.program_id(1)
    width = x_ref.shape[-1]

    @pl.when((win == 0) & (step == 0))
    def _():
        acc_p[...] = jnp.zeros_like(acc_p)
        acc_1[...] = jnp.zeros_like(acc_1)
        acc_2[...] = jnp.zeros_like(acc_2)
        small_ref[...] = jnp.zeros_like(small_ref)
        fc1b_ref[...] = jnp.zeros_like(fc1b_ref)

    @pl.when(step == 0)
    def _():
        assemble_tokens(win, edge_ref, own_ref, alt_ref, above_ref, below_ref, doubled, tokens)

    here = pl.ds(pl.multiple_of(step * tile, 16), tile)
    da, dm = da_ref[0], dm_ref[0]
    attended = get_groups(att_ref)
    branch = nn(attended, wp_ref[...]) + pb_ref[...]
    middle = x_ref[0].astype(F32) + by_frame(branch, da)
    unit, inverse = norm_stats(middle)
    normed = (unit * g_ref[...] + b_ref[...]).astype(BF16)
    upstream = tokens[here, :]
    result_grad = by_frame(upstream, dm).astype(BF16)
    small_ref[0] += column_sums(result_grad.astype(F32))
    normed_t = normed.T
    result_grad_t = result_grad.T
    count = w1_ref.shape[1] // chunk
    lows = {}

    def widen(i):
        part = slice(i * chunk, i * chunk + chunk)
        hiddens[i % 2][...] = nn(normed, w1_ref[:, part])
        slopes[i % 2][...] = nt(result_grad, w2_ref[part, :])

    def activate(i):
        part = slice(i * chunk, i * chunk + chunk)
        active, slope = gelu_both(hiddens[i % 2][...] + b1_ref[:, part])
        hidden_grad = slopes[i % 2][...] * slope
        fc1b_ref[:, part] += column_sums(hidden_grad)
        lows[i] = active.astype(BF16), hidden_grad.astype(BF16)

    def narrow(i):
        part = slice(i * chunk, i * chunk + chunk)
        active, hidden_grad = lows.pop(i)
        forward = nn(active, w2_ref[part, :])
        backward = nt(hidden_grad, w1_ref[:, part])
        if i == 0:
            result[...] = forward
            n2g[...] = backward
        else:
            result[...] += forward
            n2g[...] += backward
        acc_2[:, part] += nn(result_grad_t, active)
        acc_1[:, part] += nn(normed_t, hidden_grad)

    for i in range(count + 2):
        if 0 <= i - 1 < count:
            activate(i - 1)
        if i < count:
            widen(i)
        if 0 <= i - 2:
            narrow(i - 2)
    mixed = middle + by_frame(result[...] + b2_ref[...], dm)
    mixed_ref[0] = mixed.astype(BF16)
    tokens[here, :] = mixed
    normed_grad = n2g[...]
    small_ref[1] += column_sums(normed_grad * unit)
    small_ref[2] += column_sums(normed_grad)
    middle_grad = upstream + norm_back(normed_grad * g_ref[...], unit, inverse)
    mg_ref[0] = middle_grad
    branch_grad = by_frame(middle_grad, da).astype(BF16)
    small_ref[3] += column_sums(branch_grad.astype(F32))
    acc_p[...] += nn(attended.T, branch_grad)
    put_groups(og_ref, nt(branch_grad, wp_ref[...]).astype(BF16))

    for late, message_ref in enumerate((up_ref, down_ref)):

        @pl.when((win == late) & (step == steps - 1))
        def _():
            pack_message(late, tokens, message_ref)

    @pl.when((win == 1) & (step == steps - 1))
    def _():
        blocks = acc_1.shape[1] // width
        piece = 2 * mine_ref.shape[0] // parts
        for core in range(2):

            @pl.when(edge_ref[2] == core)
            def _():
                for i in range(2 * blocks + 1):
                    part = slice(i % blocks * width, i % blocks * width + width)
                    if i < blocks:
                        block = acc_1[:, part]
                    elif i < 2 * blocks:
                        block = acc_2[:, part].T
                    else:
                        block = acc_p[...]
                    block = block.astype(BF16)
                    for row in range(0, width, 16):
                        at, within = divmod(i * width + row, piece)
                        chip, plane = divmod(at, 2 * planes)
                        owner, plane = divmod(plane, planes)
                        to = (chip * planes + plane) * piece + within
                        ref = mine_ref if owner == core else theirs_ref
                        ref[to : to + 16, :] = block[row : row + 16]


def mlp(
    parts, planes, edges, x, att, cot, above, below, drop_attn, drop_mlp, wp, pb, g, b, w1, b1, w2, b2, tile=400, chunk=256
):
    width, hidden = w1.shape
    steps = TOKENS // tile
    half = (up_to(2 * hidden + width, 16 * parts) // 2, width)
    frames = pl.BlockSpec((1, WT, 128), lambda w, j: (w, 0, 0))
    return pl.pallas_call(
        functools.partial(mlp_kernel, tile, steps, chunk, parts, planes),
        grid=(2, steps),
        in_specs=[scalars(), tile_spec(tile, width), group_spec(tile, width)]
        + volume_specs(width)
        + [
            frames,
            frames,
            whole(wp.shape),
            whole((1, width)),
            whole((1, width)),
            whole((1, width)),
            whole(w1.shape),
            whole((1, hidden)),
            whole(w2.shape),
            whole((1, width)),
        ],
        out_specs=[
            tile_spec(tile, width),
            whole((TOKENS // 2, width)),
            whole((TOKENS // 2, width)),
            tile_spec(tile, width),
            group_spec(tile, width),
            whole(half),
            whole(half),
            whole((4, 8, width)),
            whole((8, hidden)),
        ],
        out_shape=[
            jax.ShapeDtypeStruct((2, TOKENS, width), BF16),
            jax.ShapeDtypeStruct((TOKENS // 2, width), BF16),
            jax.ShapeDtypeStruct((TOKENS // 2, width), BF16),
            jax.ShapeDtypeStruct((2, TOKENS, width), F32),
            group_shape(width),
            jax.ShapeDtypeStruct(half, BF16),
            jax.ShapeDtypeStruct(half, BF16),
            jax.ShapeDtypeStruct((4, 8, width), F32),
            jax.ShapeDtypeStruct((8, hidden), F32),
        ],
        scratch_shapes=[
            pltpu.VMEM((PLACES * WT, width), F32),
            pltpu.VMEM((TOKENS, width), F32),
            pltpu.VMEM((width, width), F32),
            pltpu.VMEM((width, hidden), F32),
            pltpu.VMEM((width, hidden), F32),
            pltpu.VMEM((tile, width), F32),
            pltpu.VMEM((tile, width), F32),
        ]
        + [pltpu.VMEM((tile, chunk), F32)] * 4,
        compiler_params=pltpu.CompilerParams(vmem_limit_bytes=62 << 20),
        cost_estimate=cost(100),
        name="mlp",
    )(
        edges,
        x,
        att,
        cot,
        cot,
        above,
        below,
        drop_attn,
        drop_mlp,
        wp,
        pb[None],
        g[None],
        b[None],
        w1,
        b1[None],
        w2,
        b2[None],
    )


def qkv_back_kernel(late, count, tile, *refs):
    grads = refs[:count]
    x_ref, mg_ref, w_ref, g_ref = refs[count : count + 4]
    out_ref, message_ref, tokens = refs[-3:]
    products = {}

    def multiply(i):
        here = slice(i * tile, i * tile + tile)
        groups = [d[0, here, at : at + 384] for d in grads for at in range(0, d.shape[-1], 384)]
        thirds = [g[:, third * 128 : third * 128 + 128] for third in range(3) for g in groups]
        products[i] = nt(jnp.concatenate(thirds, axis=-1), w_ref[...])

    def norm(i):
        here = slice(i * tile, i * tile + tile)
        unit, inverse = norm_stats(x_ref[0, here, :].astype(F32))
        grad = mg_ref[0, here, :] + norm_back(products.pop(i) * g_ref[...], unit, inverse)
        out_ref[0, here, :] = grad
        tokens[here, :] = grad

    steps = tokens.shape[0] // tile
    for i in range(steps + 1):
        if i < steps:
            multiply(i)
        if i:
            norm(i - 1)
    pack_message(late, tokens, message_ref)


def qkv_back(win, grads, x, middle_grad, w_qkv, gain, previous=None):
    width = x.shape[-1]
    rows = TOKENS // 2
    tile = pl.BlockSpec((1, rows, width), lambda j: (win, j, 0))
    passed = [] if previous is None else [previous]
    return pl.pallas_call(
        functools.partial(qkv_back_kernel, win == 1, len(grads), 400),
        grid=(2,),
        in_specs=[pl.BlockSpec((1, rows, g.shape[-1]), lambda j: (win, j, 0)) for g in grads]
        + [tile] * 2
        + [whole(w_qkv.shape), whole((1, width))]
        + [pl.BlockSpec(memory_space=pl.ANY) for _ in passed],
        out_specs=[tile, pl.BlockSpec((rows // 2, width), lambda j: (j, 0))],
        out_shape=[
            jax.ShapeDtypeStruct((2, TOKENS, width), F32),
            jax.ShapeDtypeStruct((rows, width), BF16),
        ],
        scratch_shapes=[pltpu.VMEM((rows, width), F32)],
        input_output_aliases={len(grads) + 4: 0} if passed else {},
        compiler_params=pltpu.CompilerParams(vmem_limit_bytes=60 << 20),
        cost_estimate=cost(9),
        name="qkv_back",
    )(*grads, x, middle_grad, w_qkv, gain[None], *passed)


def place_kernel(edge_ref, own_ref, up_ref, down_ref, below_ref, above_ref, out_ref, doubled):
    vol = pl.program_id(0)
    edge = edge_ref[vol] == 1
    inner = jnp.logical_not(edge)
    for late, received, sent in ((False, below_ref, down_ref), (True, above_ref, up_ref)):
        mine = vol == int(late)

        @pl.when(jnp.logical_and(mine, inner))
        def _():
            spread_message(received, late, doubled)

        @pl.when(jnp.logical_and(mine, edge))
        def _():
            spread_message(sent, late, doubled)

    width = out_ref.shape[-1]
    from_other = row_half((WT, width)) == (vol == 0)
    for slot in range(0, len(SLOTS), 2):
        both = own_ref[0, slot * WT : slot * WT + 2 * WT, :].astype(F32)
        for k in range(2):
            place = SLOTS[slot + k]
            if place is None:
                continue
            other = doubled[(slot + k) * WT : (slot + k + 1) * WT, :]
            value = jnp.where(from_other, other, both[k * WT : k * WT + WT])
            out_ref[0, place[0], place[1]] = value.astype(out_ref.dtype)


def to_frames(edges, tokens, up, down, below, above):
    width = tokens.shape[-1]
    return pl.pallas_call(
        place_kernel,
        grid=(2,),
        in_specs=[scalars(), pl.BlockSpec((1, TOKENS, width), lambda v: (v, 0, 0))] + [whole(up.shape)] * 4,
        out_specs=pl.BlockSpec((1, SIDE, SIDE, WT, width), lambda v: (v, 0, 0, 0, 0)),
        out_shape=jax.ShapeDtypeStruct((2, SIDE, SIDE, WT, width), tokens.dtype),
        scratch_shapes=[pltpu.VMEM((TOKENS, width), F32)],
        compiler_params=pltpu.CompilerParams(vmem_limit_bytes=28 << 20),
        cost_estimate=cost(5),
        name="to_frames",
    )(edges, tokens, up, down, below, above)


def tie(value, *after):
    return lax.optimization_barrier((value,) + after)[0]


def pick(array, index, axis=0):
    return lax.dynamic_index_in_dim(array, index, axis, keepdims=False)


def add_low(*values):
    return sum(v.astype(F32) for v in values).astype(BF16)


class Sum:
    def __init__(self, buffer=None, mine=None, theirs=None):
        self.n = lax.axis_size("tm")
        self.size = lax.axis_size("dp")
        self.m = self.size // 2
        dp = lax.axis_index("dp")
        self.core, self.chip, self.plane = dp % 2, dp // 2, lax.axis_index("tm")
        if buffer is not None:
            rows, width = buffer.shape
            whole = buffer.reshape(self.m, 2, self.n, rows // (2 * self.m * self.n), width)
            mine, theirs = pick(whole, self.core, 1), pick(whole, 1 - self.core, 1)
        else:
            rows, width = mine.shape
            shape = (self.m, self.n, rows // (self.m * self.n), width)
            mine, theirs = mine.reshape(shape), theirs.reshape(shape)
        self.piece = mine.shape[2:]
        self.mine, self.theirs = mine, theirs

    def to_core(self, values):
        return lax.ppermute(values, "dp", [(i, i ^ 1) for i in range(self.size)])

    def to_chip(self, values, s):
        return lax.ppermute(values, "dp", [(i, i ^ (2 * s)) for i in range(self.size)])

    def to_plane(self, values, s):
        return lax.ppermute(values, "tm", [(i, i ^ s) for i in range(self.n)])

    def step0(self):
        self.got = self.to_core(self.theirs)
        return self

    def step1(self):
        parts = [add_low(pick(self.mine, self.chip ^ s), pick(self.got, self.chip ^ s)) for s in range(self.m)]
        self.mine = parts[0]
        self.got = [self.to_chip(parts[s], s) for s in range(1, self.m)]
        return parts[-1]

    def step2(self):
        total = add_low(self.mine, *self.got)
        parts = [pick(total, self.plane ^ s) for s in range(self.n)]
        self.mine = parts[0]
        self.got = [self.to_plane(parts[s], s) for s in range(1, self.n)]
        return parts[-1]

    def step3(self):
        self.mine = add_low(self.mine, *self.got)
        self.got = []
        return self.mine

    def gathered(self):
        return lax.all_gather(self.mine, ("dp", "tm"), tiled=True)

    def step3_back(self):
        self.step3()
        self.got = [self.to_plane(self.mine, s) for s in range(1, self.n)]
        return self.mine

    def step4_back(self):
        self.mine = jnp.stack([self.mine] + self.got)
        self.got = [self.to_chip(self.mine, s) for s in range(1, self.m)]
        return self.mine

    def step5_back(self):
        self.mine = jnp.stack([self.mine] + self.got)
        self.other = self.to_core(self.mine)
        return self.mine


EXTRA_TILES = 4
EXTRA_TABLE = 16


def pack_kernel(calls, width, *refs):
    pieces, strips, colsums = refs[:calls], refs[calls : 2 * calls], refs[2 * calls : 3 * calls]
    small_ref, fc1b_ref, out_ref, extra = refs[3 * calls :]
    extra[...] = jnp.zeros_like(extra)
    group, at = 0, 0
    for c in range(calls):
        rows = pieces[c].shape[0]
        out_ref[at : at + rows, :] = pieces[c][...]
        at += rows
        for g in range(rows // width):
            extra[group : group + 1, :] = jnp.sum(colsums[c][g * 8 : g * 8 + 8, :], axis=0, keepdims=True)
            group += 1
    vectors = [jnp.sum(small_ref[i], axis=0, keepdims=True) for i in range(4)]
    vectors.append(jnp.sum(fc1b_ref[...], axis=0, keepdims=True))
    vectors = jnp.concatenate(vectors, axis=1)
    for t in range(vectors.shape[1] // 128):
        row, lanes = EXTRA_TILES + t // 3, t % 3 * 128
        extra[row : row + 1, lanes : lanes + 128] = vectors[:, t * 128 : t * 128 + 128]
    counts = [s.shape[0] // WT for s in strips]
    totals = [jnp.zeros((rows, ACROSS * (2 * WT - 1)), F32) for rows in counts]
    for tk in range(WT):
        hot = hot_times(tk)
        for c in range(calls):
            for part in split3(strips[c][pl.ds(tk, counts[c], stride=WT), :]):
                totals[c] = totals[c] + nt(part, hot)
    row = EXTRA_TABLE
    for c in range(calls):
        extra[row : row + counts[c], : totals[c].shape[1]] = totals[c]
        row += counts[c]
    out_ref[at:, :] = extra[...].astype(BF16)


def pack(pieces, strips, colsums, small, fc1b, unit_rows):
    width, lanes = small.shape[-1], pieces[0].shape[1]
    main = sum(p.shape[0] for p in pieces)
    rows = up_to(main + EXTRA_TABLE + sum(s.shape[0] for s in strips) // WT, unit_rows)
    return pl.pallas_call(
        functools.partial(pack_kernel, len(pieces), width),
        out_shape=jax.ShapeDtypeStruct((rows, lanes), BF16),
        scratch_shapes=[pltpu.VMEM((rows - main, lanes), F32)],
        compiler_params=pltpu.CompilerParams(vmem_limit_bytes=60 << 20),
        cost_estimate=cost(4),
        name="pack_sums",
    )(*pieces, *strips, *colsums, small, fc1b)


def finish_kernel(m, n, groups, ids_ref, mine_ref, other_ref, w_ref, gain_ref, bias_ref, *refs):
    gw_ref, lg_ref, lb_ref, qb_ref, vb_ref, s0, s1, s2, s3, fc1b_ref, table_ref, total, sorted_rows = refs
    core, chip, plane = ids_ref[0], ids_ref[1], ids_ref[2]
    rows = mine_ref.shape[1]
    for c in range(m):
        for k in range(2):
            for z in range(n):
                at = (chip ^ c) * n + (plane ^ z)
                block = jnp.where(core == k, mine_ref[at].astype(F32), other_ref[at].astype(F32))
                first = ((c * 2 + k) * n + z) * rows
                total[first : first + rows, :] = block
    width = w_ref.shape[0]
    base = groups * width
    gain = gain_ref[...]
    bias = bias_ref[...]
    products = jnp.zeros((width, 128), F32)
    row = jnp.zeros((1, width), F32)
    for g in range(groups):
        part = total[g * width : (g + 1) * width, :]
        sums = total[base + g : base + g + 1, :]
        grad = gain * part + bias * sums
        for third in range(3):
            lanes = slice(third * 128, third * 128 + 128)
            at = third * width + g * 128
            gw_ref[:, at : at + 128] = grad[:, lanes]
            weight = w_ref[:, at : at + 128]
            products = products + weight.astype(F32) * part[:, lanes]
            for piece in split3(jnp.broadcast_to(sums[:, lanes], (8, 128))):
                row = row + nt(piece, weight)[:1]
        qb_ref[:, g * 128 : g * 128 + 128] = sums[:, :128]
        vb_ref[:, g * 128 : g * 128 + 128] = sums[:, 256:]
    lb_ref[...] = row
    ones = jnp.ones((8, 128), BF16)
    lg_ref[...] = sum(nt(ones, piece) for piece in split3(products))[:1]
    targets = [(ref, p) for ref in (s0, s1, s2, s3, fc1b_ref) for p in range(ref.shape[1] // 128)]
    for t, (ref, p) in enumerate(targets):
        at = base + EXTRA_TILES + t // 3
        ref[:, p * 128 : p * 128 + 128] = total[at : at + 1, t % 3 * 128 : t % 3 * 128 + 128]
    heads, entries = table_ref.shape
    times = 2 * WT - 1
    lane = lax.broadcasted_iota(jnp.int32, (heads, 128), 1)
    tiles = [None] * (up_to(entries, 128) // 128)
    for part in range(up_to(ACROSS * times, 128) // 128):
        sorted_rows[...] = total[base + EXTRA_TABLE :, part * 128 : part * 128 + 128]
        for dh in range(ACROSS):
            source = sorted_rows[pl.ds(dh, heads, stride=ACROSS), :]
            for dt in range(times):
                begin, end = max(dt * ACROSS, part * 128), min((dt + 1) * ACROSS, part * 128 + 128)
                if begin >= end:
                    continue
                move = dt * ACROSS * ACROSS + dh * ACROSS - dt * ACROSS
                rolled = lane_roll(source, move)
                for tile in range((begin + move) // 128, (end - 1 + move) // 128 + 1):
                    here = lane + tile * 128
                    value = jnp.where((here >= begin + move) & (here < end + move), rolled, 0.0)
                    tiles[tile] = value if tiles[tile] is None else tiles[tile] + value
    for tile, value in enumerate(tiles):
        stop = min(128, entries - tile * 128)
        table_ref[:, tile * 128 : tile * 128 + stop] = value[:, :stop]


def finish(sums, w_qkv, gain, bias, hidden, heads):
    width = w_qkv.shape[0]
    groups = width // 128
    rows, lanes = sums.piece
    count = sums.m * sums.n
    ids = jnp.stack([sums.core, sums.chip, sums.plane])
    vector = jax.ShapeDtypeStruct((1, width), F32)
    return pl.pallas_call(
        functools.partial(finish_kernel, sums.m, sums.n, groups),
        in_specs=[scalars()] + [pl.BlockSpec(memory_space=pltpu.VMEM)] * 5,
        out_specs=[pl.BlockSpec(memory_space=pltpu.VMEM)] * 11,
        out_shape=[jax.ShapeDtypeStruct(w_qkv.shape, F32)]
        + [vector] * 8
        + [
            jax.ShapeDtypeStruct((1, hidden), F32),
            jax.ShapeDtypeStruct((heads, ACROSS * ACROSS * (2 * WT - 1)), F32),
        ],
        scratch_shapes=[
            pltpu.VMEM((2 * count * rows, lanes), F32),
            pltpu.VMEM((2 * count * rows - groups * width - EXTRA_TABLE, 128), F32),
        ],
        compiler_params=pltpu.CompilerParams(vmem_limit_bytes=32 << 20),
        cost_estimate=cost(5),
        name="finish",
    )(
        ids,
        sums.mine.reshape(count, rows, lanes),
        sums.other.reshape(count, rows, lanes),
        w_qkv,
        gain[:, None],
        bias[:, None],
    )


def widen_kernel(blocks, in_ref, fc1_ref, fc2_ref, proj_ref):
    step = pl.program_id(0)

    @pl.when(step < blocks)
    def _():
        fc1_ref[...] = in_ref[...].astype(F32)

    @pl.when(jnp.logical_and(step >= blocks, step < 2 * blocks))
    def _():
        fc2_ref[...] = in_ref[...].astype(F32)

    @pl.when(step == 2 * blocks)
    def _():
        proj_ref[...] = in_ref[...].astype(F32)


def widen_grads(buffer, hidden):
    width = buffer.shape[1]
    blocks = hidden // width
    block = (width, width)
    return pl.pallas_call(
        functools.partial(widen_kernel, blocks),
        grid=(2 * blocks + 1,),
        in_specs=[pl.BlockSpec(block, lambda i: (i, 0))],
        out_specs=[
            pl.BlockSpec(block, lambda i: (0, jnp.minimum(i, blocks - 1))),
            pl.BlockSpec(block, lambda i: (jnp.clip(i - blocks, 0, blocks - 1), 0)),
            pl.BlockSpec(block, lambda i: (0, 0)),
        ],
        out_shape=[
            jax.ShapeDtypeStruct((width, hidden), F32),
            jax.ShapeDtypeStruct((hidden, width), F32),
            jax.ShapeDtypeStruct(block, F32),
        ],
        compiler_params=pltpu.CompilerParams(vmem_limit_bytes=14 << 20),
        cost_estimate=cost(5),
        name="widen_grads",
    )(buffer)


def neighbours():
    count = lax.axis_size("tm")
    down = [(i, i - 1) for i in range(1, count)]
    up = [(i, i + 1) for i in range(count - 1)]
    return down, up


def fetch_halves(field):
    down, up = neighbours()
    width = field.shape[-1]
    above = lax.ppermute(field[0, :, :, :SHIFT_T].reshape(PLACES * SHIFT_T, width), "tm", down)
    below = lax.ppermute(field[1, :, :, SHIFT_T:].reshape(PLACES * SHIFT_T, width), "tm", up)
    return above, below


def send_up(message):
    return lax.ppermute(message, "tm", neighbours()[1])


def send_down(message):
    return lax.ppermute(message, "tm", neighbours()[0])


def frame_facts(segments, keep):
    count = lax.axis_size("tm")
    me = lax.axis_index("tm")
    own = 2 * SHIFT_T
    first = me * own
    t = jnp.arange(SHIFT_T)
    zero, one = jnp.zeros((SHIFT_T,), jnp.int32), jnp.ones((SHIFT_T,), jnp.int32)
    top, bottom = me == count - 1, me == 0
    frames = jnp.stack(
        [
            jnp.concatenate([jnp.where(top, first + SHIFT_T + t, first + own + t), first + SHIFT_T + t]),
            jnp.concatenate([first + t, jnp.where(bottom, t, first - SHIFT_T + t)]),
        ]
    )
    volumes = jnp.stack(
        [jnp.concatenate([jnp.where(top, one, zero), zero]), jnp.concatenate([one, jnp.where(bottom, zero, one)])]
    )
    pick_frame = (frames[:, :, None] == jnp.arange(segments.shape[1])).astype(jnp.int32)
    by_volume = jnp.sum(pick_frame[:, :, None, :] * segments[None, None], axis=-1)
    segment = jnp.where(volumes == 0, by_volume[..., 0], by_volume[..., 1])
    key = segment + 8 * (frames < SHIFT_T) + 16 * volumes
    apart = (key[:, :, None] != key[:, None, :]).astype(F32) * FAR
    far = jnp.tile(apart, (1, 1, 128 // WT))
    seg_hot = (segment[:, :, None] == jnp.arange(keep.shape[2])).astype(F32)
    kept = jnp.where(volumes[:, :, None, None] == 0, keep[0], keep[1]).astype(F32)
    drops = jnp.sum(seg_hot[:, :, None, :] * kept, axis=-1) / KEEP_RATE
    drops = jnp.broadcast_to(drops[..., None], drops.shape + (128,))
    return far, drops[:, :, 0], drops[:, :, 1]


def shards(
    volume,
    segments,
    keep,
    ln1_gain,
    ln1_bias,
    w_qkv,
    q_bias,
    v_bias,
    rel_table,
    w_proj,
    proj_bias,
    ln2_gain,
    ln2_bias,
    w_fc1,
    fc1_bias,
    w_fc2,
    fc2_bias,
    cotangent,
):
    width = volume.shape[-1]
    heads = rel_table.shape[1]
    dim = width // heads
    hidden = w_fc1.shape[1]
    groups = width // 128
    me = lax.axis_index("tm")
    top, bottom = me == lax.axis_size("tm") - 1, me == 0
    planes = lax.axis_size("tm")
    parts = lax.axis_size("dp") * planes
    edges_in = jnp.stack([top, bottom, lax.axis_index("dp") % 2]).astype(jnp.int32)
    edges_out = jnp.stack([bottom, top]).astype(jnp.int32)
    places = volume.transpose(0, 2, 3, 1, 4)
    cot = cotangent.transpose(0, 2, 3, 1, 4)
    above, below = fetch_halves(places)
    far, drop_attn, drop_mlp = frame_facts(segments, keep)
    biases = make_bias(rel_table)
    qkv_bias = jnp.concatenate([q_bias, jnp.zeros_like(q_bias), v_bias])
    x, unit, q, k, v = make_qkv(
        edges_in, places, above, below, ln1_gain, ln1_bias, w_qkv, qkv_bias, dim**-0.5 * LOG2E
    )
    cot_above, cot_below = fetch_halves(tie(cot, q))
    *exps, att, inverse = attend(q, k, v, far, biases, dim)
    mixed, mixed_up, mixed_down, middle_grad, out_grad, g_mine, g_theirs, small2, small_fc1 = mlp(
        parts,
        planes,
        edges_in,
        x,
        att,
        cot,
        cot_above,
        cot_below,
        drop_attn,
        drop_mlp,
        w_proj,
        proj_bias,
        ln2_gain,
        ln2_bias,
        w_fc1,
        fc1_bias,
        w_fc2,
        fc2_bias,
    )
    mixed_below, mixed_above = send_up(mixed_up), send_down(mixed_down)
    mlp_sum = Sum(mine=g_mine, theirs=g_theirs).step0()
    grads, pieces, sums, strips = [], [], [], []
    first = 0
    for many, step in ((2, mlp_sum.step1), (1, mlp_sum.step2), (1, mlp_sum.step3)):
        wait = step()
        d, gw, colsum, strip = attend_back(first, many, q, k, v, tie(out_grad, wait), att, inverse, unit, exps, dim)
        first += many
        grads.append(d)
        pieces.append(gw)
        sums.append(colsum)
        strips.append(strip)
        mlp_sum.got = lax.optimization_barrier((mlp_sum.got, d))[0]
    all_mlp = mlp_sum.gathered()
    unit_rows = 8 * lax.axis_size("dp") * lax.axis_size("tm")
    qkv_sum = Sum(pack(pieces, strips, sums, small2, small_fc1, unit_rows)).step0()
    grad0, grad_up = qkv_back(0, grads, tie(x, qkv_sum.theirs), middle_grad, w_qkv, ln1_gain)
    below = send_up(grad_up)
    qkv_sum.got = tie(qkv_sum.got, grad0)
    wait = qkv_sum.step1()
    grad, grad_down = qkv_back(1, grads, tie(x, wait, grad_up), middle_grad, w_qkv, ln1_gain, grad0)
    above = send_down(grad_down)
    qkv_sum.got = lax.optimization_barrier((qkv_sum.got, grad))[0]
    wait = qkv_sum.step2()
    mixed_out = to_frames(edges_out, tie(mixed, wait), mixed_up, mixed_down, mixed_below, mixed_above)
    g_fc1, g_fc2, g_proj = widen_grads(tie(all_mlp, mixed_out), hidden)
    qkv_sum.got = lax.optimization_barrier((qkv_sum.got, g_fc1))[0]
    qkv_sum.step3_back()
    wait = qkv_sum.step4_back()
    volume_grad = to_frames(edges_out, tie(grad, wait), grad_up, grad_down, below, above)
    qkv_sum.got = lax.optimization_barrier((qkv_sum.got, volume_grad))[0]
    qkv_sum.step5_back()
    g_qkv, ln1_g, ln1_b, q_b, v_b, fc2_b, ln2_g, ln2_b, proj_b, fc1_b, table = finish(
        qkv_sum, w_qkv, ln1_gain, ln1_bias, hidden, heads
    )
    return (
        mixed_out.transpose(0, 3, 1, 2, 4),
        volume_grad.transpose(0, 3, 1, 2, 4),
        ln1_g[0],
        ln1_b[0],
        g_qkv,
        q_b[0],
        v_b[0],
        table.T,
        g_proj,
        proj_b[0],
        ln2_g[0],
        ln2_b[0],
        g_fc1,
        fc1_b[0],
        g_fc2,
        fc2_b[0],
    )


def solution(mesh):
    split = P("dp", "tm", None, None, None)
    return jax.shard_map(
        shards,
        mesh=mesh,
        in_specs=(split, P("dp", None), P("dp", None, None)) + (P(),) * 14 + (split,),
        out_specs=(split, split) + (P(),) * 14,
        check_vma=False,
    )
```

```python
import functools

import jax
import jax.numpy as jnp
import numpy as np
from jax import lax
from jax.experimental import pallas as pl
from jax.experimental.pallas import tpu as pltpu
from jax.sharding import PartitionSpec as P

SIDE = 14
WT = 8
WIN_HW = 7
SHIFT_T = 4
SHIFT_HW = 3
EPS = 1e-05
KEEP_RATE = 0.75
PRECISE = lax.Precision.HIGHEST
LOG2E = 1.4426950408889634
LN2 = 0.6931471805599453
FAR = 1e30
F32 = jnp.float32
BF16 = jnp.bfloat16

SPANS = (
    (SHIFT_HW, WIN_HW),
    (SHIFT_HW + WIN_HW, SIDE - SHIFT_HW - WIN_HW),
    (0, SHIFT_HW),
)
ACROSS = 2 * WIN_HW - 1
RECTS = (
    (0, 0, True, 0),
    (1, 0, True, 0),
    (0, 1, False, 1),
    (2, 0, True, 0),
    (0, 2, False, 1),
    (2, 2, True, 3),
    (2, 1, True, 2),
    (1, 2, True, 3),
    (1, 1, True, 2),
)
BIAS_DIMS = ((7, 7), (4, 7), (4, 4), (4, 3))


def up_to(value, unit):
    return -(-value // unit) * unit


class Rect:
    pass


def plan_rects():
    rects, slots, start, lane_start = [], [], 0, 0
    class_rows = [0, 0, 0]
    for row_span, col_span, rows_outer, table in RECTS:
        r0, rn = SPANS[row_span]
        c0, cn = SPANS[col_span]
        rect = Rect()
        if rows_outer:
            places = [(r0 + a, c0 + b) for a in range(rn) for b in range(cn)]
        else:
            places = [(r0 + b, c0 + a) for a in range(cn) for b in range(rn)]
        rect.count = len(places) * WT
        rect.rows = up_to(rect.count, 16)
        rect.lanes = up_to(rect.count, 128)
        rect.start = start
        rect.table = table
        rect.kind = {512: 0, 256: 1, 128: 2}[rect.lanes]
        rect.kind_row = class_rows[rect.kind]
        class_rows[rect.kind] += rect.rows
        slots += places + [None] * ((rect.rows - rect.count) // WT)
        start += rect.rows
        rect.lane_start = lane_start
        lane_start += rect.lanes
        rects.append(rect)
    return rects, slots, class_rows


RECT, SLOTS, KIND_ROWS = plan_rects()
TOKENS = len(SLOTS) * WT
ALL_LANES = sum(rect.lanes for rect in RECT)
KIND_LANES = (512, 256, 128)
PLACES = SIDE * SIDE


def nn(a, b):
    return lax.dot_general(a, b, (((1,), (0,)), ((), ())), preferred_element_type=F32)


def nt(a, b):
    return lax.dot_general(a, b, (((1,), (1,)), ((), ())), preferred_element_type=F32)


def wide(pattern, width):
    return jnp.concatenate([pattern] * (width // pattern.shape[-1]), axis=-1)


def by_frame(values, pattern):
    rows, width = values.shape
    scaled = values.reshape(rows // WT, WT, width) * wide(pattern, width)[None]
    return scaled.reshape(rows, width)


def column_sums(values):
    rows, width = values.shape
    return jnp.sum(values.reshape(rows // 8, 8, width), axis=0)


def row_half(shape):
    return (lax.broadcasted_iota(jnp.int32, shape, 0) & (WT - 1)) < SHIFT_T


def turned(tile):
    return pltpu.roll(tile, SHIFT_T, 0)


def spread_message(message_ref, late, doubled):
    def pair(i, carry):
        both = message_ref[pl.ds(pl.multiple_of(i * 16, 16), 16), :].astype(F32)
        for k in range(2):
            tile = both[k * WT : k * WT + WT]
            at = pl.multiple_of(i * 32 + k * 16, 16)
            first, second = (turned(tile), tile) if late else (tile, turned(tile))
            doubled[pl.ds(at, WT), :] = first
            doubled[pl.ds(at + WT, WT), :] = second
        return carry

    lax.fori_loop(0, message_ref.shape[0] // 16, pair, 0)


def assemble_tokens(win, edge_ref, own_ref, alt_ref, above_ref, below_ref, doubled, tokens):
    edge = edge_ref[win] == 1
    inner = jnp.logical_not(edge)

    @pl.when(jnp.logical_and(inner, win == 0))
    def _():
        spread_message(above_ref, False, doubled)

    @pl.when(jnp.logical_and(inner, win == 1))
    def _():
        spread_message(below_ref, True, doubled)

    @pl.when(edge)
    def _():
        def row(h, carry):
            for w in range(SIDE):
                at = pl.multiple_of((h * SIDE + w) * WT, WT)
                doubled[pl.ds(at, WT), :] = turned(alt_ref[0, h, w].astype(F32))
            return carry

        lax.fori_loop(0, SIDE, row, 0)

    width = tokens.shape[1]
    from_other = row_half((WT, width)) == (win == 0)
    for slot, place in enumerate(SLOTS):
        rows = slice(slot * WT, slot * WT + WT)
        if place is None:
            tokens[rows, :] = jnp.zeros((WT, width), F32)
            continue
        h, w = place
        at = (h * SIDE + w) * WT
        tokens[rows, :] = jnp.where(from_other, doubled[at : at + WT, :], own_ref[0, h, w].astype(F32))


def pack_message(late, tokens, message_ref):
    def pair(i, carry):
        both = tokens[pl.ds(pl.multiple_of(i * 32, 32), 32), :]
        tiles = []
        for k in range(2):
            one, two = both[k * 16 : k * 16 + WT], both[k * 16 + WT : k * 16 + 16]
            low = row_half(one.shape)
            tiles.append(jnp.where(low, turned(one), two) if late else jnp.where(low, one, turned(two)))
        packed = jnp.concatenate(tiles, axis=0).astype(message_ref.dtype)
        message_ref[pl.ds(pl.multiple_of(i * 16, 16), 16), :] = packed
        return carry

    lax.fori_loop(0, tokens.shape[0] // 32, pair, 0)


def spread_table(source, outer, inner, out_ref, lane):
    width = inner * WT
    total = outer * width
    for ok in range(outer):
        for ik in range(inner):
            pieces = []
            for oq in range(outer):
                shift = (oq * width - (WIN_HW - 1 - ik) * WT) % 128
                piece = source[oq - ok + WIN_HW - 1]
                pieces.append(pltpu.roll(piece, shift, 1) if shift else piece)
            row = (ok * inner + ik) * WT
            for tile in range(up_to(total, 128) // 128):
                value = None
                for oq in range(outer):
                    begin, end = oq * width, (oq + 1) * width
                    if end <= tile * 128 or begin >= tile * 128 + 128:
                        continue
                    if value is None:
                        value = pieces[oq]
                    else:
                        value = jnp.where(lane >= begin - tile * 128, pieces[oq], value)
                out_ref[0, row : row + WT, tile * 128 : tile * 128 + 128] = value


def split3(values):
    parts = []
    for _ in range(3):
        part = values.astype(BF16)
        parts.append(part)
        values = values - part.astype(F32)
    return parts


def hot_times(tk):
    count = ACROSS * (2 * WT - 1)
    place = lax.broadcasted_iota(jnp.int32, (count, 128), 0)
    lane = lax.broadcasted_iota(jnp.int32, (count, 128), 1)
    tk = (tk + SHIFT_T) % WT
    tq = (lane + SHIFT_T) & (WT - 1)
    d = lax.shift_right_logical(lane, 3)
    return (((tq - tk + WT - 1) * ACROSS + d == place) & (d < ACROSS)).astype(BF16)


def lane_roll(tile, shift):
    shift = shift % 128
    return pltpu.roll(tile, shift, 1) if shift else tile


def lane_block(lane, d):
    return (lane >= d * WT) & (lane < d * WT + WT)


def bias_kernel(table_ref, b0_ref, b1_ref, b2_ref, b3_ref, strips):
    head = pl.program_id(0)

    @pl.when(head == 0)
    def _():
        parts = split3(table_ref[...] * LOG2E)
        for tk in range(WT):
            hot = hot_times(tk)
            strips[pl.ds(tk, table_ref.shape[0], stride=WT), :] = sum(nn(p, hot) for p in parts)

    lane = lax.broadcasted_iota(jnp.int32, (WT, 128), 1)
    base = pl.multiple_of(head * (ACROSS * WT), WT)
    by_rows = [strips[pl.ds(base + d * WT, WT), :] for d in range(ACROSS)]
    by_cols = [None] * ACROSS
    reach = BIAS_DIMS[1][0] - 1
    for d in range(WIN_HW - 1 - reach, WIN_HW + reach):
        by_cols[d] = sum(
            jnp.where(lane_block(lane, e), lane_roll(by_rows[e], (e - d) * WT), 0.0) for e in range(ACROSS)
        )
    for out_ref, source, (outer, inner) in zip(
        (b0_ref, b1_ref, b2_ref, b3_ref), (by_rows, by_cols, by_rows, by_rows), BIAS_DIMS
    ):
        spread_table(source, outer, inner, out_ref, lane)


def bias_shapes(heads):
    shapes = []
    for outer, inner in BIAS_DIMS:
        count = outer * inner * WT
        shapes.append((heads, count, up_to(count, 128)))
    return shapes


def make_bias(rel_table):
    heads = rel_table.shape[1]
    times = 2 * WT - 1
    cube = rel_table.T.reshape(heads, times, ACROSS, ACROSS)
    table = cube.transpose(0, 2, 1, 3).reshape(heads * ACROSS, times * ACROSS)
    shapes = bias_shapes(heads)
    return pl.pallas_call(
        bias_kernel,
        grid=(heads,),
        in_specs=[whole(table.shape)],
        out_specs=[pl.BlockSpec((1,) + s[1:], lambda h: (h, 0, 0)) for s in shapes],
        out_shape=[jax.ShapeDtypeStruct(s, F32) for s in shapes],
        scratch_shapes=[pltpu.VMEM((heads * ACROSS * WT, 128), F32)],
        compiler_params=pltpu.CompilerParams(vmem_limit_bytes=60 << 20),
        cost_estimate=cost(10),
        name="position_bias",
    )(table)


def fold_matrices():
    tiles = []
    for tile in range(4):
        tiles.append(np.zeros((WIN_HW * 128, 512), np.float32))
        for ik in range(WIN_HW):
            for lane in range(128):
                query = tile * 128 + lane
                oq, iq, frame = query // (WIN_HW * WT), query // WT % WIN_HW, query % WT
                if query < WIN_HW * WIN_HW * WT:
                    block = oq - tile * 128 // (WIN_HW * WT)
                    tiles[-1][ik * 128 + lane, block * 128 + (iq - ik + WIN_HW - 1) * WT + frame] = 1
    for outer, inner in BIAS_DIMS[2:]:
        tiles.append(np.zeros((inner * 128, 512), np.float32))
        for ik in range(inner):
            for lane in range(outer * inner * WT):
                oq, iq, frame = lane // (inner * WT), lane // WT % inner, lane % WT
                tiles[-1][ik * 128 + lane, oq * 128 + (iq - ik + WIN_HW - 1) * WT + frame] = 1
    return jnp.asarray(np.concatenate(tiles)).astype(BF16)


FOLD_ROWS = (4 * WIN_HW + BIAS_DIMS[2][1] + BIAS_DIMS[3][1]) * 128


def fold_tables(accs, per, hots):
    by_rows = [[jnp.zeros((WT, 128), F32) for _ in range(ACROSS)] for _ in range(per)]
    by_cols = [[jnp.zeros((WT, 128), F32) for _ in range(ACROSS)] for _ in range(per)]

    def left(table, tile):
        outer, inner = BIAS_DIMS[table]
        lanes = slice(tile * 128, tile * 128 + 128)
        rows = []
        for head in range(per):
            for ok in range(outer):
                at = [(ok * inner + ik) * WT for ik in range(inner)]
                rows.append(jnp.concatenate([accs[table][head, a : a + WT, lanes] for a in at], axis=1))
        return jnp.concatenate(rows, axis=0).astype(BF16)

    def add(totals, table, part, first, blocks):
        outer, _ = BIAS_DIMS[table]
        for head in range(per):
            for ok in range(outer):
                for block in range(blocks):
                    oq = first + block
                    if oq >= outer:
                        continue
                    row = (head * outer + ok) * WT
                    d = oq - ok + WIN_HW - 1
                    totals[head][d] = totals[head][d] + part[row : row + WT, block * 128 : block * 128 + 128]

    for tile in range(4):
        first = tile * 128 // (WIN_HW * WT)
        blocks = min(3, WIN_HW - first)
        tables = (0, 1) if tile < 2 else (0,)
        hot = hots[tile * WIN_HW * 128 : (tile + 1) * WIN_HW * 128, : blocks * 128]
        part = nn(jnp.concatenate([left(t, tile) for t in tables], axis=0), hot)
        split = per * BIAS_DIMS[0][0] * WT
        add(by_rows, 0, part[:split], first, blocks)
        if len(tables) > 1:
            add(by_cols, 1, part[split:], first, blocks)
    at = 4 * WIN_HW * 128
    for table in (2, 3):
        outer, inner = BIAS_DIMS[table]
        part = nn(left(table, 0), hots[at : at + inner * 128, :])
        at += inner * 128
        add(by_rows, table, part, 0, outer)
    return by_rows, by_cols


def qkv_kernel(
    tile,
    scale,
    edge_ref,
    own_ref,
    alt_ref,
    above_ref,
    below_ref,
    gain_ref,
    bias_ref,
    w_ref,
    wb_ref,
    x_ref,
    n_ref,
    q_ref,
    k_ref,
    v_ref,
    doubled,
    tokens,
):
    win, step = pl.program_id(0), pl.program_id(1)

    @pl.when(step == 0)
    def _():
        assemble_tokens(win, edge_ref, own_ref, alt_ref, above_ref, below_ref, doubled, tokens)

    x = tokens[pl.ds(pl.multiple_of(step * tile, 16), tile), :]
    x_ref[0] = x.astype(BF16)
    unit, _ = norm_stats(x)
    n_ref[0] = unit.astype(BF16)
    normed = (unit * gain_ref[...] + bias_ref[...]).astype(BF16)
    width = x.shape[1]
    put_groups(q_ref, ((nn(normed, w_ref[:, :width]) + wb_ref[:, :width]) * scale).astype(BF16))
    put_groups(k_ref, nn(normed, w_ref[:, width : 2 * width]).astype(BF16))
    put_groups(v_ref, (nn(normed, w_ref[:, 2 * width :]) + wb_ref[:, 2 * width :]).astype(BF16))


def put_groups(ref, values):
    for g in range(ref.shape[1]):
        ref[0, g] = values[:, g * 128 : g * 128 + 128]


def get_groups(ref):
    return jnp.concatenate([ref[0, g] for g in range(ref.shape[1])], axis=-1)


def group_spec(tile, width):
    return pl.BlockSpec((1, width // 128, tile, 128), lambda w, j: (w, 0, j, 0))


def group_shape(width):
    return jax.ShapeDtypeStruct((2, width // 128, TOKENS, 128), BF16)


def cost(micros):
    return pl.CostEstimate(flops=int(micros * 1.1e9), bytes_accessed=1 << 20, transcendentals=0)


def norm_stats(values):
    centre = values - jnp.mean(values, axis=-1, keepdims=True)
    spread = jnp.mean(centre * centre, axis=-1, keepdims=True)
    inverse = lax.rsqrt(spread + EPS)
    return centre * inverse, inverse


def norm_back(scaled, unit, inverse):
    first = jnp.mean(scaled, axis=-1, keepdims=True)
    second = jnp.mean(scaled * unit, axis=-1, keepdims=True)
    return (scaled - first - unit * second) * inverse


def whole(shape):
    return pl.BlockSpec(shape, lambda *_: (0,) * len(shape))


def scalars():
    return pl.BlockSpec(memory_space=pltpu.SMEM)


def volume_specs(width):
    block = (1, SIDE, SIDE, WT, width)
    return [
        pl.BlockSpec(block, lambda w, *_: (w, 0, 0, 0, 0)),
        pl.BlockSpec(block, lambda w, *_: (1 - w, 0, 0, 0, 0)),
        whole((PLACES * SHIFT_T, width)),
        whole((PLACES * SHIFT_T, width)),
    ]


def tile_spec(tile, width):
    return pl.BlockSpec((1, tile, width), lambda w, j: (w, j, 0))


def make_qkv(edges, volume, above, below, gain, bias, w_qkv, qkv_bias, scale, tile=400):
    width = volume.shape[-1]
    out = jax.ShapeDtypeStruct((2, TOKENS, width), BF16)
    return pl.pallas_call(
        functools.partial(qkv_kernel, tile, scale),
        grid=(2, TOKENS // tile),
        in_specs=[scalars()]
        + volume_specs(width)
        + [whole((1, width)), whole((1, width)), whole(w_qkv.shape), whole((1, 3 * width))],
        out_specs=[tile_spec(tile, width)] * 2 + [group_spec(tile, width)] * 3,
        out_shape=[out] * 2 + [group_shape(width)] * 3,
        scratch_shapes=[
            pltpu.VMEM((PLACES * WT, width), F32),
            pltpu.VMEM((TOKENS, width), F32),
        ],
        compiler_params=pltpu.CompilerParams(vmem_limit_bytes=60 << 20),
        cost_estimate=cost(17),
        name="norm1_qkv",
    )(edges, volume, volume, above, below, gain[None], bias[None], w_qkv, qkv_bias[None])


def head_rows(transposed, head, dim):
    rows, lanes = transposed.shape
    parts = []
    if head:
        parts.append(jnp.zeros((head * dim, lanes), transposed.dtype))
    parts.append(transposed[head * dim : head * dim + dim])
    if (head + 1) * dim < rows:
        parts.append(jnp.zeros((rows - (head + 1) * dim, lanes), transposed.dtype))
    return jnp.concatenate(parts, axis=0)


def attend_kernel(
    dim, q_ref, k_ref, v_ref, far_ref, b0, b1, b2, b3, e0_ref, e1_ref, e2_ref, o_ref, r_ref, *scores
):
    biases = (b0, b1, b2, b3)
    e_refs = (e0_ref, e1_ref, e2_ref)
    far = far_ref[0]
    per = 128 // dim
    ones = jnp.ones((16, RECT[0].rows), BF16)
    operands = {}

    def prepare(rect):
        if rect not in operands:
            queries = q_ref[0, 0, rect.start : rect.start + rect.lanes, :].T
            values = v_ref[0, 0, rect.start : rect.start + rect.rows, :].T
            operands[rect] = queries, k_ref[0, 0, rect.start : rect.start + rect.rows, :], values, []
        return operands[rect]

    def score(rect, head, buffer):
        queries, keys, _, _ = prepare(rect)
        count, lanes = rect.count, rect.lanes
        raw = nn(keys, head_rows(queries, head, dim))[:count]
        raw = raw + biases[rect.table][head, :count, :lanes]
        buffer[:count, :lanes] = raw
        wide_far = wide(far, lanes)
        top = jnp.max(raw.reshape(count // 8, 8, lanes), axis=0) - wide_far
        return jnp.max(top, axis=0, keepdims=True) + wide_far

    def exponents(rect, head, buffer, top):
        count, rows, lanes = rect.count, rect.rows, rect.lanes
        exps = jnp.exp2(buffer[:count, :lanes].reshape(count // 8, 8, lanes) - top[None])
        exps = exps.reshape(count, lanes).astype(BF16)
        if rows > count:
            exps = jnp.concatenate([exps, jnp.zeros((rows - count, lanes), BF16)], axis=0)
        place = slice(rect.kind_row, rect.kind_row + rows), slice(head * lanes, head * lanes + lanes)
        e_refs[rect.kind][(0, 0) + place] = exps
        return exps

    def weigh(rect, head, exps):
        _, _, values, outs = prepare(rect)
        rows, lanes, start = rect.rows, rect.lanes, rect.start
        lhs = jnp.concatenate([values[head * dim : head * dim + dim], ones[:, :rows]], axis=0)
        out = nn(lhs, exps)
        inverse = 1.0 / out[dim : dim + 1]
        outs.append(out[:dim] * inverse)
        r_ref[0, 0, head : head + 1, rect.lane_start : rect.lane_start + lanes] = inverse
        if len(outs) == per:
            o_ref[0, 0, start : start + rows, :] = jnp.concatenate(outs, axis=0).T[:rows].astype(BF16)

    units = [(rect, head) for rect in RECT for head in range(per)]
    tops, exps = {}, {}
    for i in range(len(units) + 2):
        if i < len(units):
            tops[i] = score(*units[i], scores[i % len(scores)])
        if 0 <= i - 1 < len(units):
            exps[i - 1] = exponents(*units[i - 1], scores[(i - 1) % len(scores)], tops.pop(i - 1))
        if 0 <= i - 2:
            weigh(*units[i - 2], exps.pop(i - 2))


def head_group_specs(heads, per, biases):
    lane_tile = pl.BlockSpec((1, 1, TOKENS, 128), lambda g, w: (w, g, 0, 0))
    far = pl.BlockSpec((1, WT, 128), lambda g, w: (w, 0, 0))
    bias = [pl.BlockSpec((per,) + b[1:], lambda g, w: (g, 0, 0)) for b in biases]
    exps = [
        pl.BlockSpec((1, 1, KIND_ROWS[i], per * KIND_LANES[i]), lambda g, w: (w, g, 0, 0)) for i in range(3)
    ]
    return lane_tile, far, bias, exps


def exps_shapes(groups, per):
    return [jax.ShapeDtypeStruct((2, groups, KIND_ROWS[i], per * KIND_LANES[i]), BF16) for i in range(3)]


def attend(q, k, v, far, biases, dim):
    groups = q.shape[1]
    per = 128 // dim
    heads = groups * per
    lane_tile, far_spec, bias_specs, exps_specs = head_group_specs(heads, per, [b.shape for b in biases])
    return pl.pallas_call(
        functools.partial(attend_kernel, dim),
        grid=(groups, 2),
        in_specs=[lane_tile] * 3 + [far_spec] + bias_specs,
        out_specs=exps_specs + [lane_tile, pl.BlockSpec((1, 1, per, ALL_LANES), lambda g, w: (w, g, 0, 0))],
        out_shape=exps_shapes(groups, per)
        + [group_shape(groups * 128), jax.ShapeDtypeStruct((2, groups, per, ALL_LANES), F32)],
        scratch_shapes=[pltpu.VMEM((RECT[0].count, RECT[0].lanes), F32)] * 3,
        compiler_params=pltpu.CompilerParams(vmem_limit_bytes=60 << 20),
        cost_estimate=cost(55),
        name="attention",
    )(q, k, v, far, *biases)


def attend_back_kernel(
    dim,
    scale,
    q_ref,
    k_ref,
    v_ref,
    g_ref,
    o_ref,
    r_ref,
    n_ref,
    hot_ref,
    e0_ref,
    e1_ref,
    e2_ref,
    d_ref,
    gw_ref,
    sums_ref,
    strips_ref,
    a0,
    a1,
    a2,
    a3,
    acc_w,
    hots,
    hot_sem,
    *buffers,
):
    win = pl.program_id(1)
    first_group = pl.program_id(0) == 0
    hot_copy = pltpu.make_async_copy(hot_ref, hots, hot_sem)
    accs = (a0, a1, a2, a3)
    e_refs = (e0_ref, e1_ref, e2_ref)
    grads, queries, outgrads, probs = buffers[:2], buffers[2:4], buffers[4:6], buffers[6:]
    per = 128 // dim
    lane = lax.broadcasted_iota(jnp.int32, (1, 128), 1)
    mine = [((lane >= h * dim) & (lane < h * dim + dim)).astype(BF16) for h in range(per)]

    @pl.when(win == 0)
    def _():
        acc_w[...] = jnp.zeros_like(acc_w)
        sums_ref[...] = jnp.zeros_like(sums_ref)

    @pl.when(jnp.logical_and(first_group, win == 0))
    def _():
        hot_copy.start()

    operands, parity = {}, {}

    def prepare(index):
        if index not in operands:
            parity[index] = len(parity) % 2
            rect = RECT[index]
            rows, lanes, start = rect.rows, rect.lanes, rect.start
            out_grad = g_ref[0, 0, start : start + rows, :]
            if lanes > rows:
                out_grad = jnp.concatenate([out_grad, jnp.zeros((lanes - rows, 128), BF16)], axis=0)
            query = q_ref[0, 0, start : start + lanes, :]
            inverse = r_ref[0, 0, :, rect.lane_start : rect.lane_start + lanes]
            inverse = [jnp.broadcast_to(inverse[h : h + 1], (dim, lanes)) for h in range(per)]
            out_grad_t = (out_grad.T.astype(F32) * jnp.concatenate(inverse, axis=0)).astype(BF16)
            out_grad = out_grad_t.T
            out_t = o_ref[0, 0, start : start + lanes, :].T
            keys_t = k_ref[0, 0, start : start + rows, :].T
            product = out_grad_t.astype(F32) * out_t.astype(F32)
            for head in range(per):
                here = slice(head * lanes, head * lanes + lanes)
                queries[parity[index]][here, :] = query * mine[head]
                outgrads[parity[index]][here, :] = out_grad * mine[head]
            operands[index] = out_grad_t, keys_t, product, []
        return operands[index]

    def first(index, head, buffer):
        out_grad_t, _, product, _ = prepare(index)
        rect = RECT[index]
        values = v_ref[0, 0, rect.start : rect.start + rect.rows, :]
        buffer[: rect.rows, : rect.lanes] = nn(values, head_rows(out_grad_t, head, dim))
        return jnp.sum(product[head * dim : head * dim + dim], axis=0, keepdims=True)

    def second(index, head, buffer, inner):
        rect = RECT[index]
        count, rows, lanes = rect.count, rect.rows, rect.lanes
        here = slice(head * lanes, head * lanes + lanes)
        exps = e_refs[rect.kind][0, 0, rect.kind_row : rect.kind_row + rows, here].astype(F32)
        score_grad = exps * (buffer[:rows, :lanes] - inner)
        acc = accs[rect.table]
        total = score_grad[:count] + acc[head, :count, :lanes]
        if (count, lanes) == acc.shape[1:]:
            total = jnp.where(win == 0, score_grad[:count], total)
        acc[head, :count, :lanes] = total
        low = score_grad.astype(BF16)
        grads[parity[index]][:rows, here] = low
        return low

    def third(index, head, low):
        _, keys_t, _, dqs = prepare(index)
        dqs.append(nn(keys_t[head * dim : head * dim + dim], low))
        if len(dqs) < per:
            return
        rect = RECT[index]
        rows, lanes, start = rect.rows, rect.lanes, rect.start
        dq = jnp.concatenate(dqs, axis=0) * scale
        d_ref[0, start : start + rows, :128] = dq.T[:rows].astype(BF16)
        dk = nn(grads[parity[index]][:rows, : per * lanes], queries[parity[index]][: per * lanes, :])
        d_ref[0, start : start + rows, 128:256] = (dk * LN2).astype(BF16)
        exps = e_refs[rect.kind][0, 0, rect.kind_row : rect.kind_row + rows, :]
        dv = nn(exps, outgrads[parity[index]][: per * lanes, :])
        d_ref[0, start : start + rows, 256:] = dv.astype(BF16)

    order = sorted(range(len(RECT)), key=lambda i: (RECT[i].kind, -RECT[i].count))
    units = [(index, head) for index in order for head in range(per)]
    inners, lows = {}, {}
    for i in range(len(units) + 2):
        if i < len(units):
            inners[i] = first(*units[i], probs[i % len(probs)])
        if 0 <= i - 1 < len(units):
            lows[i - 1] = second(*units[i - 1], probs[(i - 1) % len(probs)], inners.pop(i - 1))
        if 0 <= i - 2:
            third(*units[i - 2], lows.pop(i - 2))

    all_grads = d_ref[0]
    acc_w[...] += lax.dot_general(n_ref[0], all_grads, (((0,), (0,)), ((), ())), preferred_element_type=F32)
    sums_ref[...] += column_sums(all_grads.astype(F32))

    @pl.when(win == 1)
    def _():
        gw_ref[...] = acc_w[...].astype(BF16)
        lane8 = lax.broadcasted_iota(jnp.int32, (WT, 128), 1)

        @pl.when(first_group)
        def _():
            hot_copy.wait()

        all_rows, all_cols = fold_tables(accs, per, hots)
        for head in range(per):
            by_rows, by_cols = all_rows[head], all_cols[head]
            for d in range(ACROSS):
                for e in range(ACROSS):
                    if abs(e - WIN_HW + 1) < BIAS_DIMS[1][0]:
                        turned_back = lane_roll(by_cols[e], (e - d) * WT)
                        by_rows[d] = by_rows[d] + jnp.where(lane_block(lane8, e), turned_back, 0.0)
                strips_ref[(head * ACROSS + d) * WT : (head * ACROSS + d + 1) * WT, :] = by_rows[d]


def attend_back(first, groups, q, k, v, out_grad, out, inverse, unit, exps, dim):
    width = q.shape[1] * 128
    per = 128 // dim
    shapes = bias_shapes(per)
    lane_tile = pl.BlockSpec((1, 1, TOKENS, 128), lambda g, w: (w, first + g, 0, 0))
    exps_specs = [
        pl.BlockSpec((1, 1, KIND_ROWS[i], per * KIND_LANES[i]), lambda g, w: (w, first + g, 0, 0))
        for i in range(3)
    ]
    strip = (per * ACROSS * WT, 128)
    most = per * RECT[0].lanes
    return pl.pallas_call(
        functools.partial(attend_back_kernel, dim, dim**-0.5),
        grid=(groups, 2),
        in_specs=[lane_tile] * 5
        + [
            pl.BlockSpec((1, 1, per, ALL_LANES), lambda g, w: (w, first + g, 0, 0)),
            pl.BlockSpec((1, TOKENS, width), lambda g, w: (w, 0, 0)),
            pl.BlockSpec(memory_space=pl.ANY),
        ]
        + exps_specs,
        out_specs=[
            pl.BlockSpec((1, TOKENS, 384), lambda g, w: (w, 0, g)),
            pl.BlockSpec((width, 384), lambda g, w: (g, 0)),
            pl.BlockSpec((8, 384), lambda g, w: (g, 0)),
            pl.BlockSpec(strip, lambda g, w: (g, 0)),
        ],
        out_shape=[
            jax.ShapeDtypeStruct((2, TOKENS, groups * 384), BF16),
            jax.ShapeDtypeStruct((groups * width, 384), BF16),
            jax.ShapeDtypeStruct((groups * 8, 384), F32),
            jax.ShapeDtypeStruct((groups * strip[0], 128), F32),
        ],
        scratch_shapes=[pltpu.VMEM(s, F32) for s in shapes]
        + [
            pltpu.VMEM((width, 384), F32),
            pltpu.VMEM((FOLD_ROWS, 512), BF16),
            pltpu.SemaphoreType.DMA,
        ]
        + [pltpu.VMEM((RECT[0].rows, most), BF16)] * 2
        + [pltpu.VMEM((most, 128), BF16)] * 4
        + [pltpu.VMEM((RECT[0].rows, RECT[0].lanes), F32)] * 3,
        compiler_params=pltpu.CompilerParams(vmem_limit_bytes=60 << 20),
        cost_estimate=cost(18 * groups),
        name="attention_back",
    )(q, k, v, out_grad, out, inverse, unit, fold_matrices(), *exps)


ERFC = (0.254829592, -0.284496736, 1.421413741, -1.453152027, 1.061405429)
ERFC_P = 0.3275911


def gelu_both(u):
    denominator = 1.0 + (ERFC_P * 0.5**0.5) * jnp.abs(u)
    t = pl.reciprocal(denominator, approx=True)
    bell = jnp.exp2((u * u) * (-0.5 * LOG2E))
    series = 0.5 * ERFC[4]
    for factor in ERFC[3::-1]:
        series = series * t + 0.5 * factor
    tail = series * t * bell
    area = jnp.where(u >= 0.0, 1.0 - tail, tail)
    return u * area, area + (u * (1.0 / np.sqrt(2.0 * np.pi))) * bell


def mlp_kernel(
    tile,
    steps,
    chunk,
    parts,
    planes,
    edge_ref,
    x_ref,
    att_ref,
    own_ref,
    alt_ref,
    above_ref,
    below_ref,
    da_ref,
    dm_ref,
    wp_ref,
    pb_ref,
    g_ref,
    b_ref,
    w1_ref,
    b1_ref,
    w2_ref,
    b2_ref,
    mixed_ref,
    up_ref,
    down_ref,
    mg_ref,
    og_ref,
    mine_ref,
    theirs_ref,
    small_ref,
    fc1b_ref,
    doubled,
    tokens,
    acc_p,
    acc_1,
    acc_2,
    result,
    n2g,
    *buffers,
):
    hiddens, slopes = buffers[:2], buffers[2:]
    win, step = pl.program_id(0), pl.program_id(1)
    width = x_ref.shape[-1]

    @pl.when((win == 0) & (step == 0))
    def _():
        acc_p[...] = jnp.zeros_like(acc_p)
        acc_1[...] = jnp.zeros_like(acc_1)
        acc_2[...] = jnp.zeros_like(acc_2)
        small_ref[...] = jnp.zeros_like(small_ref)
        fc1b_ref[...] = jnp.zeros_like(fc1b_ref)

    @pl.when(step == 0)
    def _():
        assemble_tokens(win, edge_ref, own_ref, alt_ref, above_ref, below_ref, doubled, tokens)

    here = pl.ds(pl.multiple_of(step * tile, 16), tile)
    da, dm = da_ref[0], dm_ref[0]
    attended = get_groups(att_ref)
    branch = nn(attended, wp_ref[...]) + pb_ref[...]
    middle = x_ref[0].astype(F32) + by_frame(branch, da)
    unit, inverse = norm_stats(middle)
    normed = (unit * g_ref[...] + b_ref[...]).astype(BF16)
    upstream = tokens[here, :]
    result_grad = by_frame(upstream, dm).astype(BF16)
    small_ref[0] += column_sums(result_grad.astype(F32))
    normed_t = normed.T
    result_grad_t = result_grad.T
    count = w1_ref.shape[1] // chunk
    lows = {}

    def widen(i):
        part = slice(i * chunk, i * chunk + chunk)
        hiddens[i % 2][...] = nn(normed, w1_ref[:, part])
        slopes[i % 2][...] = nt(result_grad, w2_ref[part, :])

    def activate(i):
        part = slice(i * chunk, i * chunk + chunk)
        active, slope = gelu_both(hiddens[i % 2][...] + b1_ref[:, part])
        hidden_grad = slopes[i % 2][...] * slope
        fc1b_ref[:, part] += column_sums(hidden_grad)
        lows[i] = active.astype(BF16), hidden_grad.astype(BF16)

    def narrow(i):
        part = slice(i * chunk, i * chunk + chunk)
        active, hidden_grad = lows.pop(i)
        forward = nn(active, w2_ref[part, :])
        backward = nt(hidden_grad, w1_ref[:, part])
        if i == 0:
            result[...] = forward
            n2g[...] = backward
        else:
            result[...] += forward
            n2g[...] += backward
        acc_2[:, part] += nn(result_grad_t, active)
        acc_1[:, part] += nn(normed_t, hidden_grad)

    for i in range(count + 2):
        if 0 <= i - 1 < count:
            activate(i - 1)
        if i < count:
            widen(i)
        if 0 <= i - 2:
            narrow(i - 2)
    mixed = middle + by_frame(result[...] + b2_ref[...], dm)
    mixed_ref[0] = mixed.astype(BF16)
    tokens[here, :] = mixed
    normed_grad = n2g[...]
    small_ref[1] += column_sums(normed_grad * unit)
    small_ref[2] += column_sums(normed_grad)
    middle_grad = upstream + norm_back(normed_grad * g_ref[...], unit, inverse)
    mg_ref[0] = middle_grad
    branch_grad = by_frame(middle_grad, da).astype(BF16)
    small_ref[3] += column_sums(branch_grad.astype(F32))
    acc_p[...] += nn(attended.T, branch_grad)
    put_groups(og_ref, nt(branch_grad, wp_ref[...]).astype(BF16))

    for late, message_ref in enumerate((up_ref, down_ref)):

        @pl.when((win == late) & (step == steps - 1))
        def _():
            pack_message(late, tokens, message_ref)

    @pl.when((win == 1) & (step == steps - 1))
    def _():
        blocks = acc_1.shape[1] // width
        piece = 2 * mine_ref.shape[0] // parts
        for core in range(2):

            @pl.when(edge_ref[2] == core)
            def _():
                for i in range(2 * blocks + 1):
                    part = slice(i % blocks * width, i % blocks * width + width)
                    if i < blocks:
                        block = acc_1[:, part]
                    elif i < 2 * blocks:
                        block = acc_2[:, part].T
                    else:
                        block = acc_p[...]
                    block = block.astype(BF16)
                    for row in range(0, width, 16):
                        at, within = divmod(i * width + row, piece)
                        chip, plane = divmod(at, 2 * planes)
                        owner, plane = divmod(plane, planes)
                        to = (chip * planes + plane) * piece + within
                        ref = mine_ref if owner == core else theirs_ref
                        ref[to : to + 16, :] = block[row : row + 16]


def mlp(
    parts, planes, edges, x, att, cot, above, below, drop_attn, drop_mlp, wp, pb, g, b, w1, b1, w2, b2, tile=400, chunk=256
):
    width, hidden = w1.shape
    steps = TOKENS // tile
    half = (up_to(2 * hidden + width, 16 * parts) // 2, width)
    frames = pl.BlockSpec((1, WT, 128), lambda w, j: (w, 0, 0))
    return pl.pallas_call(
        functools.partial(mlp_kernel, tile, steps, chunk, parts, planes),
        grid=(2, steps),
        in_specs=[scalars(), tile_spec(tile, width), group_spec(tile, width)]
        + volume_specs(width)
        + [
            frames,
            frames,
            whole(wp.shape),
            whole((1, width)),
            whole((1, width)),
            whole((1, width)),
            whole(w1.shape),
            whole((1, hidden)),
            whole(w2.shape),
            whole((1, width)),
        ],
        out_specs=[
            tile_spec(tile, width),
            whole((TOKENS // 2, width)),
            whole((TOKENS // 2, width)),
            tile_spec(tile, width),
            group_spec(tile, width),
            whole(half),
            whole(half),
            whole((4, 8, width)),
            whole((8, hidden)),
        ],
        out_shape=[
            jax.ShapeDtypeStruct((2, TOKENS, width), BF16),
            jax.ShapeDtypeStruct((TOKENS // 2, width), BF16),
            jax.ShapeDtypeStruct((TOKENS // 2, width), BF16),
            jax.ShapeDtypeStruct((2, TOKENS, width), F32),
            group_shape(width),
            jax.ShapeDtypeStruct(half, BF16),
            jax.ShapeDtypeStruct(half, BF16),
            jax.ShapeDtypeStruct((4, 8, width), F32),
            jax.ShapeDtypeStruct((8, hidden), F32),
        ],
        scratch_shapes=[
            pltpu.VMEM((PLACES * WT, width), F32),
            pltpu.VMEM((TOKENS, width), F32),
            pltpu.VMEM((width, width), F32),
            pltpu.VMEM((width, hidden), F32),
            pltpu.VMEM((width, hidden), F32),
            pltpu.VMEM((tile, width), F32),
            pltpu.VMEM((tile, width), F32),
        ]
        + [pltpu.VMEM((tile, chunk), F32)] * 4,
        compiler_params=pltpu.CompilerParams(vmem_limit_bytes=62 << 20),
        cost_estimate=cost(100),
        name="mlp",
    )(
        edges,
        x,
        att,
        cot,
        cot,
        above,
        below,
        drop_attn,
        drop_mlp,
        wp,
        pb[None],
        g[None],
        b[None],
        w1,
        b1[None],
        w2,
        b2[None],
    )


def qkv_back_kernel(late, count, tile, *refs):
    grads = refs[:count]
    x_ref, mg_ref, w_ref, g_ref = refs[count : count + 4]
    out_ref, message_ref, tokens = refs[-3:]
    products = {}

    def multiply(i):
        here = slice(i * tile, i * tile + tile)
        groups = [d[0, here, at : at + 384] for d in grads for at in range(0, d.shape[-1], 384)]
        thirds = [g[:, third * 128 : third * 128 + 128] for third in range(3) for g in groups]
        products[i] = nt(jnp.concatenate(thirds, axis=-1), w_ref[...])

    def norm(i):
        here = slice(i * tile, i * tile + tile)
        unit, inverse = norm_stats(x_ref[0, here, :].astype(F32))
        grad = mg_ref[0, here, :] + norm_back(products.pop(i) * g_ref[...], unit, inverse)
        out_ref[0, here, :] = grad
        tokens[here, :] = grad

    steps = tokens.shape[0] // tile
    for i in range(steps + 1):
        if i < steps:
            multiply(i)
        if i:
            norm(i - 1)
    pack_message(late, tokens, message_ref)


def qkv_back(win, grads, x, middle_grad, w_qkv, gain, previous=None):
    width = x.shape[-1]
    rows = TOKENS // 2
    tile = pl.BlockSpec((1, rows, width), lambda j: (win, j, 0))
    passed = [] if previous is None else [previous]
    return pl.pallas_call(
        functools.partial(qkv_back_kernel, win == 1, len(grads), 400),
        grid=(2,),
        in_specs=[pl.BlockSpec((1, rows, g.shape[-1]), lambda j: (win, j, 0)) for g in grads]
        + [tile] * 2
        + [whole(w_qkv.shape), whole((1, width))]
        + [pl.BlockSpec(memory_space=pl.ANY) for _ in passed],
        out_specs=[tile, pl.BlockSpec((rows // 2, width), lambda j: (j, 0))],
        out_shape=[
            jax.ShapeDtypeStruct((2, TOKENS, width), F32),
            jax.ShapeDtypeStruct((rows, width), BF16),
        ],
        scratch_shapes=[pltpu.VMEM((rows, width), F32)],
        input_output_aliases={len(grads) + 4: 0} if passed else {},
        compiler_params=pltpu.CompilerParams(vmem_limit_bytes=44 << 20),
        cost_estimate=cost(9),
        name="qkv_back",
    )(*grads, x, middle_grad, w_qkv, gain[None], *passed)


def place_kernel(edge_ref, own_ref, up_ref, down_ref, below_ref, above_ref, out_ref, doubled):
    vol = pl.program_id(0)
    edge = edge_ref[vol] == 1
    inner = jnp.logical_not(edge)
    for late, received, sent in ((False, below_ref, down_ref), (True, above_ref, up_ref)):
        mine = vol == int(late)

        @pl.when(jnp.logical_and(mine, inner))
        def _():
            spread_message(received, late, doubled)

        @pl.when(jnp.logical_and(mine, edge))
        def _():
            spread_message(sent, late, doubled)

    width = out_ref.shape[-1]
    from_other = row_half((WT, width)) == (vol == 0)
    for slot in range(0, len(SLOTS), 2):
        both = own_ref[0, slot * WT : slot * WT + 2 * WT, :].astype(F32)
        for k in range(2):
            place = SLOTS[slot + k]
            if place is None:
                continue
            other = doubled[(slot + k) * WT : (slot + k + 1) * WT, :]
            value = jnp.where(from_other, other, both[k * WT : k * WT + WT])
            out_ref[0, place[0], place[1]] = value.astype(out_ref.dtype)


def to_frames(edges, tokens, up, down, below, above):
    width = tokens.shape[-1]
    return pl.pallas_call(
        place_kernel,
        grid=(2,),
        in_specs=[scalars(), pl.BlockSpec((1, TOKENS, width), lambda v: (v, 0, 0))] + [whole(up.shape)] * 4,
        out_specs=pl.BlockSpec((1, SIDE, SIDE, WT, width), lambda v: (v, 0, 0, 0, 0)),
        out_shape=jax.ShapeDtypeStruct((2, SIDE, SIDE, WT, width), tokens.dtype),
        scratch_shapes=[pltpu.VMEM((TOKENS, width), F32)],
        compiler_params=pltpu.CompilerParams(vmem_limit_bytes=28 << 20),
        cost_estimate=cost(5),
        name="to_frames",
    )(edges, tokens, up, down, below, above)


def tie(value, *after):
    return lax.optimization_barrier((value,) + after)[0]


def pick(array, index, axis=0):
    return lax.dynamic_index_in_dim(array, index, axis, keepdims=False)


def add_low(*values):
    return sum(v.astype(F32) for v in values).astype(BF16)


class Sum:
    def __init__(self, buffer=None, mine=None, theirs=None):
        self.n = lax.axis_size("tm")
        self.size = lax.axis_size("dp")
        self.m = self.size // 2
        dp = lax.axis_index("dp")
        self.core, self.chip, self.plane = dp % 2, dp // 2, lax.axis_index("tm")
        if buffer is not None:
            rows, width = buffer.shape
            whole = buffer.reshape(self.m, 2, self.n, rows // (2 * self.m * self.n), width)
            mine, theirs = pick(whole, self.core, 1), pick(whole, 1 - self.core, 1)
        else:
            rows, width = mine.shape
            shape = (self.m, self.n, rows // (self.m * self.n), width)
            mine, theirs = mine.reshape(shape), theirs.reshape(shape)
        self.piece = mine.shape[2:]
        self.mine, self.theirs = mine, theirs

    def to_core(self, values):
        return lax.ppermute(values, "dp", [(i, i ^ 1) for i in range(self.size)])

    def to_chip(self, values, s):
        return lax.ppermute(values, "dp", [(i, i ^ (2 * s)) for i in range(self.size)])

    def to_plane(self, values, s):
        return lax.ppermute(values, "tm", [(i, i ^ s) for i in range(self.n)])

    def step0(self):
        self.got = self.to_core(self.theirs)
        return self

    def step1(self):
        parts = [add_low(pick(self.mine, self.chip ^ s), pick(self.got, self.chip ^ s)) for s in range(self.m)]
        self.mine = parts[0]
        self.got = [self.to_chip(parts[s], s) for s in range(1, self.m)]
        return parts[-1]

    def step2(self):
        total = add_low(self.mine, *self.got)
        parts = [pick(total, self.plane ^ s) for s in range(self.n)]
        self.mine = parts[0]
        self.got = [self.to_plane(parts[s], s) for s in range(1, self.n)]
        return parts[-1]

    def step3(self):
        self.mine = add_low(self.mine, *self.got)
        self.got = []
        return self.mine

    def gathered(self):
        return lax.all_gather(self.mine, ("dp", "tm"), tiled=True)

    def step3_back(self):
        self.step3()
        self.got = [self.to_plane(self.mine, s) for s in range(1, self.n)]
        return self.mine

    def step4_back(self):
        self.mine = jnp.stack([self.mine] + self.got)
        self.got = [self.to_chip(self.mine, s) for s in range(1, self.m)]
        return self.mine

    def step5_back(self):
        self.mine = jnp.stack([self.mine] + self.got)
        self.other = self.to_core(self.mine)
        return self.mine


EXTRA_TILES = 4
EXTRA_TABLE = 16


def pack_kernel(calls, width, *refs):
    pieces, strips, colsums = refs[:calls], refs[calls : 2 * calls], refs[2 * calls : 3 * calls]
    small_ref, fc1b_ref, out_ref, extra = refs[3 * calls :]
    extra[...] = jnp.zeros_like(extra)
    group, at = 0, 0
    for c in range(calls):
        rows = pieces[c].shape[0]
        out_ref[at : at + rows, :] = pieces[c][...]
        at += rows
        for g in range(rows // width):
            extra[group : group + 1, :] = jnp.sum(colsums[c][g * 8 : g * 8 + 8, :], axis=0, keepdims=True)
            group += 1
    vectors = [jnp.sum(small_ref[i], axis=0, keepdims=True) for i in range(4)]
    vectors.append(jnp.sum(fc1b_ref[...], axis=0, keepdims=True))
    vectors = jnp.concatenate(vectors, axis=1)
    for t in range(vectors.shape[1] // 128):
        row, lanes = EXTRA_TILES + t // 3, t % 3 * 128
        extra[row : row + 1, lanes : lanes + 128] = vectors[:, t * 128 : t * 128 + 128]
    counts = [s.shape[0] // WT for s in strips]
    totals = [jnp.zeros((rows, ACROSS * (2 * WT - 1)), F32) for rows in counts]
    for tk in range(WT):
        hot = hot_times(tk)
        for c in range(calls):
            for part in split3(strips[c][pl.ds(tk, counts[c], stride=WT), :]):
                totals[c] = totals[c] + nt(part, hot)
    row = EXTRA_TABLE
    for c in range(calls):
        extra[row : row + counts[c], : totals[c].shape[1]] = totals[c]
        row += counts[c]
    out_ref[at:, :] = extra[...].astype(BF16)


def pack(pieces, strips, colsums, small, fc1b, unit_rows):
    width, lanes = small.shape[-1], pieces[0].shape[1]
    main = sum(p.shape[0] for p in pieces)
    rows = up_to(main + EXTRA_TABLE + sum(s.shape[0] for s in strips) // WT, unit_rows)
    return pl.pallas_call(
        functools.partial(pack_kernel, len(pieces), width),
        out_shape=jax.ShapeDtypeStruct((rows, lanes), BF16),
        scratch_shapes=[pltpu.VMEM((rows - main, lanes), F32)],
        compiler_params=pltpu.CompilerParams(vmem_limit_bytes=60 << 20),
        cost_estimate=cost(4),
        name="pack_sums",
    )(*pieces, *strips, *colsums, small, fc1b)


def finish_kernel(m, n, groups, ids_ref, mine_ref, other_ref, w_ref, gain_ref, bias_ref, *refs):
    gw_ref, lg_ref, lb_ref, qb_ref, vb_ref, s0, s1, s2, s3, fc1b_ref, table_ref, total, sorted_rows = refs
    core, chip, plane = ids_ref[0], ids_ref[1], ids_ref[2]
    rows = mine_ref.shape[1]
    for c in range(m):
        for k in range(2):
            for z in range(n):
                at = (chip ^ c) * n + (plane ^ z)
                block = jnp.where(core == k, mine_ref[at].astype(F32), other_ref[at].astype(F32))
                first = ((c * 2 + k) * n + z) * rows
                total[first : first + rows, :] = block
    width = w_ref.shape[0]
    base = groups * width
    gain = gain_ref[...]
    bias = bias_ref[...]
    products = jnp.zeros((width, 128), F32)
    row = jnp.zeros((1, width), F32)
    for g in range(groups):
        part = total[g * width : (g + 1) * width, :]
        sums = total[base + g : base + g + 1, :]
        grad = gain * part + bias * sums
        for third in range(3):
            lanes = slice(third * 128, third * 128 + 128)
            at = third * width + g * 128
            gw_ref[:, at : at + 128] = grad[:, lanes]
            weight = w_ref[:, at : at + 128]
            products = products + weight.astype(F32) * part[:, lanes]
            for piece in split3(jnp.broadcast_to(sums[:, lanes], (8, 128))):
                row = row + nt(piece, weight)[:1]
        qb_ref[:, g * 128 : g * 128 + 128] = sums[:, :128]
        vb_ref[:, g * 128 : g * 128 + 128] = sums[:, 256:]
    lb_ref[...] = row
    ones = jnp.ones((8, 128), BF16)
    lg_ref[...] = sum(nt(ones, piece) for piece in split3(products))[:1]
    targets = [(ref, p) for ref in (s0, s1, s2, s3, fc1b_ref) for p in range(ref.shape[1] // 128)]
    for t, (ref, p) in enumerate(targets):
        at = base + EXTRA_TILES + t // 3
        ref[:, p * 128 : p * 128 + 128] = total[at : at + 1, t % 3 * 128 : t % 3 * 128 + 128]
    heads, entries = table_ref.shape
    times = 2 * WT - 1
    lane = lax.broadcasted_iota(jnp.int32, (heads, 128), 1)
    tiles = [None] * (up_to(entries, 128) // 128)
    for part in range(up_to(ACROSS * times, 128) // 128):
        sorted_rows[...] = total[base + EXTRA_TABLE :, part * 128 : part * 128 + 128]
        for dh in range(ACROSS):
            source = sorted_rows[pl.ds(dh, heads, stride=ACROSS), :]
            for dt in range(times):
                begin, end = max(dt * ACROSS, part * 128), min((dt + 1) * ACROSS, part * 128 + 128)
                if begin >= end:
                    continue
                move = dt * ACROSS * ACROSS + dh * ACROSS - dt * ACROSS
                rolled = lane_roll(source, move)
                for tile in range((begin + move) // 128, (end - 1 + move) // 128 + 1):
                    here = lane + tile * 128
                    value = jnp.where((here >= begin + move) & (here < end + move), rolled, 0.0)
                    tiles[tile] = value if tiles[tile] is None else tiles[tile] + value
    for tile, value in enumerate(tiles):
        stop = min(128, entries - tile * 128)
        table_ref[:, tile * 128 : tile * 128 + stop] = value[:, :stop]


def finish(sums, w_qkv, gain, bias, hidden, heads):
    width = w_qkv.shape[0]
    groups = width // 128
    rows, lanes = sums.piece
    count = sums.m * sums.n
    ids = jnp.stack([sums.core, sums.chip, sums.plane])
    vector = jax.ShapeDtypeStruct((1, width), F32)
    return pl.pallas_call(
        functools.partial(finish_kernel, sums.m, sums.n, groups),
        in_specs=[scalars()] + [pl.BlockSpec(memory_space=pltpu.VMEM)] * 5,
        out_specs=[pl.BlockSpec(memory_space=pltpu.VMEM)] * 11,
        out_shape=[jax.ShapeDtypeStruct(w_qkv.shape, F32)]
        + [vector] * 8
        + [
            jax.ShapeDtypeStruct((1, hidden), F32),
            jax.ShapeDtypeStruct((heads, ACROSS * ACROSS * (2 * WT - 1)), F32),
        ],
        scratch_shapes=[
            pltpu.VMEM((2 * count * rows, lanes), F32),
            pltpu.VMEM((2 * count * rows - groups * width - EXTRA_TABLE, 128), F32),
        ],
        compiler_params=pltpu.CompilerParams(vmem_limit_bytes=32 << 20),
        cost_estimate=cost(5),
        name="finish",
    )(
        ids,
        sums.mine.reshape(count, rows, lanes),
        sums.other.reshape(count, rows, lanes),
        w_qkv,
        gain[:, None],
        bias[:, None],
    )


def widen_kernel(blocks, in_ref, fc1_ref, fc2_ref, proj_ref):
    step = pl.program_id(0)

    @pl.when(step < blocks)
    def _():
        fc1_ref[...] = in_ref[...].astype(F32)

    @pl.when(jnp.logical_and(step >= blocks, step < 2 * blocks))
    def _():
        fc2_ref[...] = in_ref[...].astype(F32)

    @pl.when(step == 2 * blocks)
    def _():
        proj_ref[...] = in_ref[...].astype(F32)


def widen_grads(buffer, hidden):
    width = buffer.shape[1]
    blocks = hidden // width
    block = (width, width)
    return pl.pallas_call(
        functools.partial(widen_kernel, blocks),
        grid=(2 * blocks + 1,),
        in_specs=[pl.BlockSpec(block, lambda i: (i, 0))],
        out_specs=[
            pl.BlockSpec(block, lambda i: (0, jnp.minimum(i, blocks - 1))),
            pl.BlockSpec(block, lambda i: (jnp.clip(i - blocks, 0, blocks - 1), 0)),
            pl.BlockSpec(block, lambda i: (0, 0)),
        ],
        out_shape=[
            jax.ShapeDtypeStruct((width, hidden), F32),
            jax.ShapeDtypeStruct((hidden, width), F32),
            jax.ShapeDtypeStruct(block, F32),
        ],
        compiler_params=pltpu.CompilerParams(vmem_limit_bytes=14 << 20),
        cost_estimate=cost(5),
        name="widen_grads",
    )(buffer)


def neighbours():
    count = lax.axis_size("tm")
    down = [(i, i - 1) for i in range(1, count)]
    up = [(i, i + 1) for i in range(count - 1)]
    return down, up


def fetch_halves(field):
    down, up = neighbours()
    width = field.shape[-1]
    above = lax.ppermute(field[0, :, :, :SHIFT_T].reshape(PLACES * SHIFT_T, width), "tm", down)
    below = lax.ppermute(field[1, :, :, SHIFT_T:].reshape(PLACES * SHIFT_T, width), "tm", up)
    return above, below


def send_up(message):
    return lax.ppermute(message, "tm", neighbours()[1])


def send_down(message):
    return lax.ppermute(message, "tm", neighbours()[0])


def frame_facts(segments, keep):
    count = lax.axis_size("tm")
    me = lax.axis_index("tm")
    own = 2 * SHIFT_T
    first = me * own
    t = jnp.arange(SHIFT_T)
    zero, one = jnp.zeros((SHIFT_T,), jnp.int32), jnp.ones((SHIFT_T,), jnp.int32)
    top, bottom = me == count - 1, me == 0
    frames = jnp.stack(
        [
            jnp.concatenate([jnp.where(top, first + SHIFT_T + t, first + own + t), first + SHIFT_T + t]),
            jnp.concatenate([first + t, jnp.where(bottom, t, first - SHIFT_T + t)]),
        ]
    )
    volumes = jnp.stack(
        [jnp.concatenate([jnp.where(top, one, zero), zero]), jnp.concatenate([one, jnp.where(bottom, zero, one)])]
    )
    pick_frame = (frames[:, :, None] == jnp.arange(segments.shape[1])).astype(jnp.int32)
    by_volume = jnp.sum(pick_frame[:, :, None, :] * segments[None, None], axis=-1)
    segment = jnp.where(volumes == 0, by_volume[..., 0], by_volume[..., 1])
    key = segment + 8 * (frames < SHIFT_T) + 16 * volumes
    apart = (key[:, :, None] != key[:, None, :]).astype(F32) * FAR
    far = jnp.tile(apart, (1, 1, 128 // WT))
    seg_hot = (segment[:, :, None] == jnp.arange(keep.shape[2])).astype(F32)
    kept = jnp.where(volumes[:, :, None, None] == 0, keep[0], keep[1]).astype(F32)
    drops = jnp.sum(seg_hot[:, :, None, :] * kept, axis=-1) / KEEP_RATE
    drops = jnp.broadcast_to(drops[..., None], drops.shape + (128,))
    return far, drops[:, :, 0], drops[:, :, 1]


def shards(
    volume,
    segments,
    keep,
    ln1_gain,
    ln1_bias,
    w_qkv,
    q_bias,
    v_bias,
    rel_table,
    w_proj,
    proj_bias,
    ln2_gain,
    ln2_bias,
    w_fc1,
    fc1_bias,
    w_fc2,
    fc2_bias,
    cotangent,
):
    width = volume.shape[-1]
    heads = rel_table.shape[1]
    dim = width // heads
    hidden = w_fc1.shape[1]
    groups = width // 128
    me = lax.axis_index("tm")
    top, bottom = me == lax.axis_size("tm") - 1, me == 0
    planes = lax.axis_size("tm")
    parts = lax.axis_size("dp") * planes
    edges_in = jnp.stack([top, bottom, lax.axis_index("dp") % 2]).astype(jnp.int32)
    edges_out = jnp.stack([bottom, top]).astype(jnp.int32)
    places = volume.transpose(0, 2, 3, 1, 4)
    cot = cotangent.transpose(0, 2, 3, 1, 4)
    above, below = fetch_halves(places)
    far, drop_attn, drop_mlp = frame_facts(segments, keep)
    biases = make_bias(rel_table)
    qkv_bias = jnp.concatenate([q_bias, jnp.zeros_like(q_bias), v_bias])
    x, unit, q, k, v = make_qkv(
        edges_in, places, above, below, ln1_gain, ln1_bias, w_qkv, qkv_bias, dim**-0.5 * LOG2E
    )
    cot_above, cot_below = fetch_halves(tie(cot, q))
    *exps, att, inverse = attend(q, k, v, far, biases, dim)
    mixed, mixed_up, mixed_down, middle_grad, out_grad, g_mine, g_theirs, small2, small_fc1 = mlp(
        parts,
        planes,
        edges_in,
        x,
        att,
        cot,
        cot_above,
        cot_below,
        drop_attn,
        drop_mlp,
        w_proj,
        proj_bias,
        ln2_gain,
        ln2_bias,
        w_fc1,
        fc1_bias,
        w_fc2,
        fc2_bias,
    )
    mixed_below, mixed_above = send_up(mixed_up), send_down(mixed_down)
    mlp_sum = Sum(mine=g_mine, theirs=g_theirs).step0()
    grads, pieces, sums, strips = [], [], [], []
    first = 0
    for many, step in ((2, mlp_sum.step1), (1, mlp_sum.step2), (1, mlp_sum.step3)):
        wait = step()
        d, gw, colsum, strip = attend_back(first, many, q, k, v, tie(out_grad, wait), att, inverse, unit, exps, dim)
        first += many
        grads.append(d)
        pieces.append(gw)
        sums.append(colsum)
        strips.append(strip)
        mlp_sum.got = lax.optimization_barrier((mlp_sum.got, d))[0]
    all_mlp = mlp_sum.gathered()
    unit_rows = 8 * lax.axis_size("dp") * lax.axis_size("tm")
    qkv_sum = Sum(pack(pieces, strips, sums, small2, small_fc1, unit_rows)).step0()
    grad0, grad_up = qkv_back(0, grads, tie(x, qkv_sum.theirs), middle_grad, w_qkv, ln1_gain)
    below = send_up(grad_up)
    qkv_sum.got = tie(qkv_sum.got, grad0)
    wait = qkv_sum.step1()
    grad, grad_down = qkv_back(1, grads, tie(x, wait, grad_up), middle_grad, w_qkv, ln1_gain, grad0)
    above = send_down(grad_down)
    qkv_sum.got = lax.optimization_barrier((qkv_sum.got, grad))[0]
    wait = qkv_sum.step2()
    mixed_out = to_frames(edges_out, tie(mixed, wait), mixed_up, mixed_down, mixed_below, mixed_above)
    g_fc1, g_fc2, g_proj = widen_grads(tie(all_mlp, mixed_out), hidden)
    qkv_sum.got = lax.optimization_barrier((qkv_sum.got, g_fc1))[0]
    qkv_sum.step3_back()
    wait = qkv_sum.step4_back()
    volume_grad = to_frames(edges_out, tie(grad, wait), grad_up, grad_down, below, above)
    qkv_sum.got = lax.optimization_barrier((qkv_sum.got, volume_grad))[0]
    qkv_sum.step5_back()
    g_qkv, ln1_g, ln1_b, q_b, v_b, fc2_b, ln2_g, ln2_b, proj_b, fc1_b, table = finish(
        qkv_sum, w_qkv, ln1_gain, ln1_bias, hidden, heads
    )
    return (
        mixed_out.transpose(0, 3, 1, 2, 4),
        volume_grad.transpose(0, 3, 1, 2, 4),
        ln1_g[0],
        ln1_b[0],
        g_qkv,
        q_b[0],
        v_b[0],
        table.T,
        g_proj,
        proj_b[0],
        ln2_g[0],
        ln2_b[0],
        g_fc1,
        fc1_b[0],
        g_fc2,
        fc2_b[0],
    )


def solution(mesh):
    split = P("dp", "tm", None, None, None)
    return jax.shard_map(
        shards,
        mesh=mesh,
        in_specs=(split, P("dp", None), P("dp", None, None)) + (P(),) * 14 + (split,),
        out_specs=(split, split) + (P(),) * 14,
        check_vma=False,
    )
```

```python
import functools

import jax
import jax.numpy as jnp
import numpy as np
from jax import lax
from jax.experimental import pallas as pl
from jax.experimental.pallas import tpu as pltpu
from jax.sharding import PartitionSpec as P

SIDE = 14
WT = 8
WIN_HW = 7
SHIFT_T = 4
SHIFT_HW = 3
EPS = 1e-05
KEEP_RATE = 0.75
PRECISE = lax.Precision.HIGHEST
LOG2E = 1.4426950408889634
LN2 = 0.6931471805599453
FAR = 1e30
F32 = jnp.float32
BF16 = jnp.bfloat16

SPANS = (
    (SHIFT_HW, WIN_HW),
    (SHIFT_HW + WIN_HW, SIDE - SHIFT_HW - WIN_HW),
    (0, SHIFT_HW),
)
ACROSS = 2 * WIN_HW - 1
RECTS = (
    (0, 0, True, 0),
    (1, 0, True, 0),
    (0, 1, False, 1),
    (2, 0, True, 0),
    (0, 2, False, 1),
    (2, 2, True, 3),
    (2, 1, True, 2),
    (1, 2, True, 3),
    (1, 1, True, 2),
)
BIAS_DIMS = ((7, 7), (4, 7), (4, 4), (4, 3))


def up_to(value, unit):
    return -(-value // unit) * unit


class Rect:
    pass


def plan_rects():
    rects, slots, start, lane_start = [], [], 0, 0
    class_rows = [0, 0, 0]
    for row_span, col_span, rows_outer, table in RECTS:
        r0, rn = SPANS[row_span]
        c0, cn = SPANS[col_span]
        rect = Rect()
        if rows_outer:
            places = [(r0 + a, c0 + b) for a in range(rn) for b in range(cn)]
        else:
            places = [(r0 + b, c0 + a) for a in range(cn) for b in range(rn)]
        rect.count = len(places) * WT
        rect.rows = up_to(rect.count, 16)
        rect.lanes = up_to(rect.count, 128)
        rect.start = start
        rect.table = table
        rect.kind = {512: 0, 256: 1, 128: 2}[rect.lanes]
        rect.kind_row = class_rows[rect.kind]
        class_rows[rect.kind] += rect.rows
        slots += places + [None] * ((rect.rows - rect.count) // WT)
        start += rect.rows
        rect.lane_start = lane_start
        lane_start += rect.lanes
        rects.append(rect)
    return rects, slots, class_rows


RECT, SLOTS, KIND_ROWS = plan_rects()
TOKENS = len(SLOTS) * WT
ALL_LANES = sum(rect.lanes for rect in RECT)
KIND_LANES = (512, 256, 128)
PLACES = SIDE * SIDE


def nn(a, b):
    return lax.dot_general(a, b, (((1,), (0,)), ((), ())), preferred_element_type=F32)


def nt(a, b):
    return lax.dot_general(a, b, (((1,), (1,)), ((), ())), preferred_element_type=F32)


def wide(pattern, width):
    return jnp.concatenate([pattern] * (width // pattern.shape[-1]), axis=-1)


def by_frame(values, pattern):
    rows, width = values.shape
    scaled = values.reshape(rows // WT, WT, width) * wide(pattern, width)[None]
    return scaled.reshape(rows, width)


def column_sums(values):
    rows, width = values.shape
    return jnp.sum(values.reshape(rows // 8, 8, width), axis=0)


def row_half(shape):
    return (lax.broadcasted_iota(jnp.int32, shape, 0) & (WT - 1)) < SHIFT_T


def turned(tile):
    return pltpu.roll(tile, SHIFT_T, 0)


def spread_message(message_ref, late, doubled):
    def pair(i, carry):
        both = message_ref[pl.ds(pl.multiple_of(i * 16, 16), 16), :].astype(F32)
        for k in range(2):
            tile = both[k * WT : k * WT + WT]
            at = pl.multiple_of(i * 32 + k * 16, 16)
            first, second = (turned(tile), tile) if late else (tile, turned(tile))
            doubled[pl.ds(at, WT), :] = first
            doubled[pl.ds(at + WT, WT), :] = second
        return carry

    lax.fori_loop(0, message_ref.shape[0] // 16, pair, 0)


def assemble_tokens(win, edge_ref, own_ref, alt_ref, above_ref, below_ref, doubled, tokens):
    edge = edge_ref[win] == 1
    inner = jnp.logical_not(edge)

    @pl.when(jnp.logical_and(inner, win == 0))
    def _():
        spread_message(above_ref, False, doubled)

    @pl.when(jnp.logical_and(inner, win == 1))
    def _():
        spread_message(below_ref, True, doubled)

    @pl.when(edge)
    def _():
        def row(h, carry):
            for w in range(SIDE):
                at = pl.multiple_of((h * SIDE + w) * WT, WT)
                doubled[pl.ds(at, WT), :] = turned(alt_ref[0, h, w].astype(F32))
            return carry

        lax.fori_loop(0, SIDE, row, 0)

    width = tokens.shape[1]
    from_other = row_half((WT, width)) == (win == 0)
    for slot, place in enumerate(SLOTS):
        rows = slice(slot * WT, slot * WT + WT)
        if place is None:
            tokens[rows, :] = jnp.zeros((WT, width), F32)
            continue
        h, w = place
        at = (h * SIDE + w) * WT
        tokens[rows, :] = jnp.where(from_other, doubled[at : at + WT, :], own_ref[0, h, w].astype(F32))


def pack_message(late, tokens, message_ref):
    def pair(i, carry):
        both = tokens[pl.ds(pl.multiple_of(i * 32, 32), 32), :]
        tiles = []
        for k in range(2):
            one, two = both[k * 16 : k * 16 + WT], both[k * 16 + WT : k * 16 + 16]
            low = row_half(one.shape)
            tiles.append(jnp.where(low, turned(one), two) if late else jnp.where(low, one, turned(two)))
        packed = jnp.concatenate(tiles, axis=0).astype(message_ref.dtype)
        message_ref[pl.ds(pl.multiple_of(i * 16, 16), 16), :] = packed
        return carry

    lax.fori_loop(0, tokens.shape[0] // 32, pair, 0)


def spread_table(source, outer, inner, out_ref, lane):
    width = inner * WT
    total = outer * width
    for ok in range(outer):
        for ik in range(inner):
            pieces = []
            for oq in range(outer):
                shift = (oq * width - (WIN_HW - 1 - ik) * WT) % 128
                piece = source[oq - ok + WIN_HW - 1]
                pieces.append(pltpu.roll(piece, shift, 1) if shift else piece)
            row = (ok * inner + ik) * WT
            for tile in range(up_to(total, 128) // 128):
                value = None
                for oq in range(outer):
                    begin, end = oq * width, (oq + 1) * width
                    if end <= tile * 128 or begin >= tile * 128 + 128:
                        continue
                    if value is None:
                        value = pieces[oq]
                    else:
                        value = jnp.where(lane >= begin - tile * 128, pieces[oq], value)
                out_ref[0, row : row + WT, tile * 128 : tile * 128 + 128] = value


def split3(values):
    parts = []
    for _ in range(3):
        part = values.astype(BF16)
        parts.append(part)
        values = values - part.astype(F32)
    return parts


def hot_times(tk):
    count = ACROSS * (2 * WT - 1)
    place = lax.broadcasted_iota(jnp.int32, (count, 128), 0)
    lane = lax.broadcasted_iota(jnp.int32, (count, 128), 1)
    tk = (tk + SHIFT_T) % WT
    tq = (lane + SHIFT_T) & (WT - 1)
    d = lax.shift_right_logical(lane, 3)
    return (((tq - tk + WT - 1) * ACROSS + d == place) & (d < ACROSS)).astype(BF16)


def lane_roll(tile, shift):
    shift = shift % 128
    return pltpu.roll(tile, shift, 1) if shift else tile


def lane_block(lane, d):
    return (lane >= d * WT) & (lane < d * WT + WT)


def bias_kernel(table_ref, b0_ref, b1_ref, b2_ref, b3_ref, strips):
    head = pl.program_id(0)

    @pl.when(head == 0)
    def _():
        parts = split3(table_ref[...] * LOG2E)
        for tk in range(WT):
            hot = hot_times(tk)
            strips[pl.ds(tk, table_ref.shape[0], stride=WT), :] = sum(nn(p, hot) for p in parts)

    lane = lax.broadcasted_iota(jnp.int32, (WT, 128), 1)
    base = pl.multiple_of(head * (ACROSS * WT), WT)
    by_rows = [strips[pl.ds(base + d * WT, WT), :] for d in range(ACROSS)]
    by_cols = [None] * ACROSS
    reach = BIAS_DIMS[1][0] - 1
    for d in range(WIN_HW - 1 - reach, WIN_HW + reach):
        by_cols[d] = sum(
            jnp.where(lane_block(lane, e), lane_roll(by_rows[e], (e - d) * WT), 0.0) for e in range(ACROSS)
        )
    for out_ref, source, (outer, inner) in zip(
        (b0_ref, b1_ref, b2_ref, b3_ref), (by_rows, by_cols, by_rows, by_rows), BIAS_DIMS
    ):
        spread_table(source, outer, inner, out_ref, lane)


def bias_shapes(heads):
    shapes = []
    for outer, inner in BIAS_DIMS:
        count = outer * inner * WT
        shapes.append((heads, count, up_to(count, 128)))
    return shapes


def make_bias(rel_table):
    heads = rel_table.shape[1]
    times = 2 * WT - 1
    cube = rel_table.T.reshape(heads, times, ACROSS, ACROSS)
    table = cube.transpose(0, 2, 1, 3).reshape(heads * ACROSS, times * ACROSS)
    shapes = bias_shapes(heads)
    return pl.pallas_call(
        bias_kernel,
        grid=(heads,),
        in_specs=[whole(table.shape)],
        out_specs=[pl.BlockSpec((1,) + s[1:], lambda h: (h, 0, 0)) for s in shapes],
        out_shape=[jax.ShapeDtypeStruct(s, F32) for s in shapes],
        scratch_shapes=[pltpu.VMEM((heads * ACROSS * WT, 128), F32)],
        compiler_params=pltpu.CompilerParams(vmem_limit_bytes=60 << 20),
        cost_estimate=cost(10),
        name="position_bias",
    )(table)


def fold_matrices():
    tiles = []
    for tile in range(4):
        tiles.append(np.zeros((WIN_HW * 128, 512), np.float32))
        for ik in range(WIN_HW):
            for lane in range(128):
                query = tile * 128 + lane
                oq, iq, frame = query // (WIN_HW * WT), query // WT % WIN_HW, query % WT
                if query < WIN_HW * WIN_HW * WT:
                    block = oq - tile * 128 // (WIN_HW * WT)
                    tiles[-1][ik * 128 + lane, block * 128 + (iq - ik + WIN_HW - 1) * WT + frame] = 1
    for outer, inner in BIAS_DIMS[2:]:
        tiles.append(np.zeros((inner * 128, 512), np.float32))
        for ik in range(inner):
            for lane in range(outer * inner * WT):
                oq, iq, frame = lane // (inner * WT), lane // WT % inner, lane % WT
                tiles[-1][ik * 128 + lane, oq * 128 + (iq - ik + WIN_HW - 1) * WT + frame] = 1
    return jnp.asarray(np.concatenate(tiles)).astype(BF16)


FOLD_ROWS = (4 * WIN_HW + BIAS_DIMS[2][1] + BIAS_DIMS[3][1]) * 128


def fold_tables(accs, per, hots):
    by_rows = [[jnp.zeros((WT, 128), F32) for _ in range(ACROSS)] for _ in range(per)]
    by_cols = [[jnp.zeros((WT, 128), F32) for _ in range(ACROSS)] for _ in range(per)]

    def left(table, tile):
        outer, inner = BIAS_DIMS[table]
        lanes = slice(tile * 128, tile * 128 + 128)
        rows = []
        for head in range(per):
            for ok in range(outer):
                at = [(ok * inner + ik) * WT for ik in range(inner)]
                rows.append(jnp.concatenate([accs[table][head, a : a + WT, lanes] for a in at], axis=1))
        return jnp.concatenate(rows, axis=0).astype(BF16)

    def add(totals, table, part, first, blocks):
        outer, _ = BIAS_DIMS[table]
        for head in range(per):
            for ok in range(outer):
                for block in range(blocks):
                    oq = first + block
                    if oq >= outer:
                        continue
                    row = (head * outer + ok) * WT
                    d = oq - ok + WIN_HW - 1
                    totals[head][d] = totals[head][d] + part[row : row + WT, block * 128 : block * 128 + 128]

    for tile in range(4):
        first = tile * 128 // (WIN_HW * WT)
        blocks = min(3, WIN_HW - first)
        tables = (0, 1) if tile < 2 else (0,)
        hot = hots[tile * WIN_HW * 128 : (tile + 1) * WIN_HW * 128, : blocks * 128]
        part = nn(jnp.concatenate([left(t, tile) for t in tables], axis=0), hot)
        split = per * BIAS_DIMS[0][0] * WT
        add(by_rows, 0, part[:split], first, blocks)
        if len(tables) > 1:
            add(by_cols, 1, part[split:], first, blocks)
    at = 4 * WIN_HW * 128
    for table in (2, 3):
        outer, inner = BIAS_DIMS[table]
        part = nn(left(table, 0), hots[at : at + inner * 128, :])
        at += inner * 128
        add(by_rows, table, part, 0, outer)
    return by_rows, by_cols


def qkv_kernel(
    tile,
    scale,
    edge_ref,
    own_ref,
    alt_ref,
    above_ref,
    below_ref,
    gain_ref,
    bias_ref,
    w_ref,
    wb_ref,
    x_ref,
    n_ref,
    q_ref,
    k_ref,
    v_ref,
    doubled,
    tokens,
):
    win, step = pl.program_id(0), pl.program_id(1)

    @pl.when(step == 0)
    def _():
        assemble_tokens(win, edge_ref, own_ref, alt_ref, above_ref, below_ref, doubled, tokens)

    x = tokens[pl.ds(pl.multiple_of(step * tile, 16), tile), :]
    x_ref[0] = x.astype(BF16)
    unit, _ = norm_stats(x)
    n_ref[0] = unit.astype(BF16)
    normed = (unit * gain_ref[...] + bias_ref[...]).astype(BF16)
    width = x.shape[1]
    put_groups(q_ref, ((nn(normed, w_ref[:, :width]) + wb_ref[:, :width]) * scale).astype(BF16))
    put_groups(k_ref, nn(normed, w_ref[:, width : 2 * width]).astype(BF16))
    put_groups(v_ref, (nn(normed, w_ref[:, 2 * width :]) + wb_ref[:, 2 * width :]).astype(BF16))


def put_groups(ref, values):
    for g in range(ref.shape[1]):
        ref[0, g] = values[:, g * 128 : g * 128 + 128]


def get_groups(ref):
    return jnp.concatenate([ref[0, g] for g in range(ref.shape[1])], axis=-1)


def group_spec(tile, width):
    return pl.BlockSpec((1, width // 128, tile, 128), lambda w, j: (w, 0, j, 0))


def group_shape(width):
    return jax.ShapeDtypeStruct((2, width // 128, TOKENS, 128), BF16)


def cost(micros):
    return pl.CostEstimate(flops=int(micros * 1.1e9), bytes_accessed=1 << 20, transcendentals=0)


def norm_stats(values):
    centre = values - jnp.mean(values, axis=-1, keepdims=True)
    spread = jnp.mean(centre * centre, axis=-1, keepdims=True)
    inverse = lax.rsqrt(spread + EPS)
    return centre * inverse, inverse


def norm_back(scaled, unit, inverse):
    first = jnp.mean(scaled, axis=-1, keepdims=True)
    second = jnp.mean(scaled * unit, axis=-1, keepdims=True)
    return (scaled - first - unit * second) * inverse


def whole(shape):
    return pl.BlockSpec(shape, lambda *_: (0,) * len(shape))


def scalars():
    return pl.BlockSpec(memory_space=pltpu.SMEM)


def volume_specs(width):
    block = (1, SIDE, SIDE, WT, width)
    return [
        pl.BlockSpec(block, lambda w, *_: (w, 0, 0, 0, 0)),
        pl.BlockSpec(block, lambda w, *_: (1 - w, 0, 0, 0, 0)),
        whole((PLACES * SHIFT_T, width)),
        whole((PLACES * SHIFT_T, width)),
    ]


def tile_spec(tile, width):
    return pl.BlockSpec((1, tile, width), lambda w, j: (w, j, 0))


def make_qkv(edges, volume, above, below, gain, bias, w_qkv, qkv_bias, scale, tile=400):
    width = volume.shape[-1]
    out = jax.ShapeDtypeStruct((2, TOKENS, width), BF16)
    return pl.pallas_call(
        functools.partial(qkv_kernel, tile, scale),
        grid=(2, TOKENS // tile),
        in_specs=[scalars()]
        + volume_specs(width)
        + [whole((1, width)), whole((1, width)), whole(w_qkv.shape), whole((1, 3 * width))],
        out_specs=[tile_spec(tile, width)] * 2 + [group_spec(tile, width)] * 3,
        out_shape=[out] * 2 + [group_shape(width)] * 3,
        scratch_shapes=[
            pltpu.VMEM((PLACES * WT, width), F32),
            pltpu.VMEM((TOKENS, width), F32),
        ],
        compiler_params=pltpu.CompilerParams(vmem_limit_bytes=60 << 20),
        cost_estimate=cost(17),
        name="norm1_qkv",
    )(edges, volume, volume, above, below, gain[None], bias[None], w_qkv, qkv_bias[None])


def head_rows(transposed, head, dim):
    rows, lanes = transposed.shape
    parts = []
    if head:
        parts.append(jnp.zeros((head * dim, lanes), transposed.dtype))
    parts.append(transposed[head * dim : head * dim + dim])
    if (head + 1) * dim < rows:
        parts.append(jnp.zeros((rows - (head + 1) * dim, lanes), transposed.dtype))
    return jnp.concatenate(parts, axis=0)


def attend_kernel(
    dim, q_ref, k_ref, v_ref, far_ref, b0, b1, b2, b3, e0_ref, e1_ref, e2_ref, o_ref, r_ref, *scores
):
    biases = (b0, b1, b2, b3)
    e_refs = (e0_ref, e1_ref, e2_ref)
    far = far_ref[0]
    per = 128 // dim
    ones = jnp.ones((16, RECT[0].rows), BF16)
    operands = {}

    def prepare(rect):
        if rect not in operands:
            queries = q_ref[0, 0, rect.start : rect.start + rect.lanes, :].T
            values = v_ref[0, 0, rect.start : rect.start + rect.rows, :].T
            operands[rect] = queries, k_ref[0, 0, rect.start : rect.start + rect.rows, :], values, []
        return operands[rect]

    def score(rect, head, buffer):
        queries, keys, _, _ = prepare(rect)
        count, lanes = rect.count, rect.lanes
        raw = nn(keys, head_rows(queries, head, dim))[:count]
        raw = raw + biases[rect.table][head, :count, :lanes]
        buffer[:count, :lanes] = raw
        wide_far = wide(far, lanes)
        top = jnp.max(raw.reshape(count // 8, 8, lanes), axis=0) - wide_far
        return jnp.max(top, axis=0, keepdims=True) + wide_far

    def exponents(rect, head, buffer, top):
        count, rows, lanes = rect.count, rect.rows, rect.lanes
        exps = jnp.exp2(buffer[:count, :lanes].reshape(count // 8, 8, lanes) - top[None])
        exps = exps.reshape(count, lanes).astype(BF16)
        if rows > count:
            exps = jnp.concatenate([exps, jnp.zeros((rows - count, lanes), BF16)], axis=0)
        place = slice(rect.kind_row, rect.kind_row + rows), slice(head * lanes, head * lanes + lanes)
        e_refs[rect.kind][(0, 0) + place] = exps
        return exps

    def weigh(rect, head, exps):
        _, _, values, outs = prepare(rect)
        rows, lanes, start = rect.rows, rect.lanes, rect.start
        lhs = jnp.concatenate([values[head * dim : head * dim + dim], ones[:, :rows]], axis=0)
        out = nn(lhs, exps)
        inverse = 1.0 / out[dim : dim + 1]
        outs.append(out[:dim] * inverse)
        r_ref[0, 0, head : head + 1, rect.lane_start : rect.lane_start + lanes] = inverse
        if len(outs) == per:
            o_ref[0, 0, start : start + rows, :] = jnp.concatenate(outs, axis=0).T[:rows].astype(BF16)

    units = [(rect, head) for rect in RECT for head in range(per)]
    tops, exps = {}, {}
    for i in range(len(units) + 2):
        if i < len(units):
            tops[i] = score(*units[i], scores[i % len(scores)])
        if 0 <= i - 1 < len(units):
            exps[i - 1] = exponents(*units[i - 1], scores[(i - 1) % len(scores)], tops.pop(i - 1))
        if 0 <= i - 2:
            weigh(*units[i - 2], exps.pop(i - 2))


def head_group_specs(heads, per, biases):
    lane_tile = pl.BlockSpec((1, 1, TOKENS, 128), lambda g, w: (w, g, 0, 0))
    far = pl.BlockSpec((1, WT, 128), lambda g, w: (w, 0, 0))
    bias = [pl.BlockSpec((per,) + b[1:], lambda g, w: (g, 0, 0)) for b in biases]
    exps = [
        pl.BlockSpec((1, 1, KIND_ROWS[i], per * KIND_LANES[i]), lambda g, w: (w, g, 0, 0)) for i in range(3)
    ]
    return lane_tile, far, bias, exps


def exps_shapes(groups, per):
    return [jax.ShapeDtypeStruct((2, groups, KIND_ROWS[i], per * KIND_LANES[i]), BF16) for i in range(3)]


def attend(q, k, v, far, biases, dim):
    groups = q.shape[1]
    per = 128 // dim
    heads = groups * per
    lane_tile, far_spec, bias_specs, exps_specs = head_group_specs(heads, per, [b.shape for b in biases])
    return pl.pallas_call(
        functools.partial(attend_kernel, dim),
        grid=(groups, 2),
        in_specs=[lane_tile] * 3 + [far_spec] + bias_specs,
        out_specs=exps_specs + [lane_tile, pl.BlockSpec((1, 1, per, ALL_LANES), lambda g, w: (w, g, 0, 0))],
        out_shape=exps_shapes(groups, per)
        + [group_shape(groups * 128), jax.ShapeDtypeStruct((2, groups, per, ALL_LANES), F32)],
        scratch_shapes=[pltpu.VMEM((RECT[0].count, RECT[0].lanes), F32)] * 3,
        compiler_params=pltpu.CompilerParams(vmem_limit_bytes=60 << 20),
        cost_estimate=cost(55),
        name="attention",
    )(q, k, v, far, *biases)


def attend_back_kernel(
    dim,
    scale,
    q_ref,
    k_ref,
    v_ref,
    g_ref,
    o_ref,
    r_ref,
    n_ref,
    hot_ref,
    e0_ref,
    e1_ref,
    e2_ref,
    d_ref,
    gw_ref,
    sums_ref,
    strips_ref,
    a0,
    a1,
    a2,
    a3,
    acc_w,
    hots,
    hot_sem,
    *buffers,
):
    win = pl.program_id(1)
    first_group = pl.program_id(0) == 0
    hot_copy = pltpu.make_async_copy(hot_ref, hots, hot_sem)
    accs = (a0, a1, a2, a3)
    e_refs = (e0_ref, e1_ref, e2_ref)
    grads, queries, outgrads, probs = buffers[:2], buffers[2:4], buffers[4:6], buffers[6:]
    per = 128 // dim
    lane = lax.broadcasted_iota(jnp.int32, (1, 128), 1)
    mine = [((lane >= h * dim) & (lane < h * dim + dim)).astype(BF16) for h in range(per)]

    @pl.when(win == 0)
    def _():
        acc_w[...] = jnp.zeros_like(acc_w)
        sums_ref[...] = jnp.zeros_like(sums_ref)

    @pl.when(jnp.logical_and(first_group, win == 0))
    def _():
        hot_copy.start()

    operands, parity = {}, {}

    def prepare(index):
        if index not in operands:
            parity[index] = len(parity) % 2
            rect = RECT[index]
            rows, lanes, start = rect.rows, rect.lanes, rect.start
            out_grad = g_ref[0, 0, start : start + rows, :]
            if lanes > rows:
                out_grad = jnp.concatenate([out_grad, jnp.zeros((lanes - rows, 128), BF16)], axis=0)
            query = q_ref[0, 0, start : start + lanes, :]
            inverse = r_ref[0, 0, :, rect.lane_start : rect.lane_start + lanes]
            inverse = [jnp.broadcast_to(inverse[h : h + 1], (dim, lanes)) for h in range(per)]
            out_grad_t = (out_grad.T.astype(F32) * jnp.concatenate(inverse, axis=0)).astype(BF16)
            out_grad = out_grad_t.T
            out_t = o_ref[0, 0, start : start + lanes, :].T
            keys_t = k_ref[0, 0, start : start + rows, :].T
            product = out_grad_t.astype(F32) * out_t.astype(F32)
            for head in range(per):
                here = slice(head * lanes, head * lanes + lanes)
                queries[parity[index]][here, :] = query * mine[head]
                outgrads[parity[index]][here, :] = out_grad * mine[head]
            operands[index] = out_grad_t, keys_t, product, []
        return operands[index]

    def first(index, head, buffer):
        out_grad_t, _, product, _ = prepare(index)
        rect = RECT[index]
        values = v_ref[0, 0, rect.start : rect.start + rect.rows, :]
        buffer[: rect.rows, : rect.lanes] = nn(values, head_rows(out_grad_t, head, dim))
        return jnp.sum(product[head * dim : head * dim + dim], axis=0, keepdims=True)

    def second(index, head, buffer, inner):
        rect = RECT[index]
        count, rows, lanes = rect.count, rect.rows, rect.lanes
        here = slice(head * lanes, head * lanes + lanes)
        exps = e_refs[rect.kind][0, 0, rect.kind_row : rect.kind_row + rows, here].astype(F32)
        score_grad = exps * (buffer[:rows, :lanes] - inner)
        acc = accs[rect.table]
        total = score_grad[:count] + acc[head, :count, :lanes]
        if (count, lanes) == acc.shape[1:]:
            total = jnp.where(win == 0, score_grad[:count], total)
        acc[head, :count, :lanes] = total
        low = score_grad.astype(BF16)
        grads[parity[index]][:rows, here] = low
        return low

    def third(index, head, low):
        _, keys_t, _, dqs = prepare(index)
        dqs.append(nn(keys_t[head * dim : head * dim + dim], low))
        if len(dqs) < per:
            return
        rect = RECT[index]
        rows, lanes, start = rect.rows, rect.lanes, rect.start
        dq = jnp.concatenate(dqs, axis=0) * scale
        d_ref[0, start : start + rows, :128] = dq.T[:rows].astype(BF16)
        dk = nn(grads[parity[index]][:rows, : per * lanes], queries[parity[index]][: per * lanes, :])
        d_ref[0, start : start + rows, 128:256] = (dk * LN2).astype(BF16)
        exps = e_refs[rect.kind][0, 0, rect.kind_row : rect.kind_row + rows, :]
        dv = nn(exps, outgrads[parity[index]][: per * lanes, :])
        d_ref[0, start : start + rows, 256:] = dv.astype(BF16)

    order = sorted(range(len(RECT)), key=lambda i: (RECT[i].kind, -RECT[i].count))
    units = [(index, head) for index in order for head in range(per)]
    inners, lows = {}, {}
    for i in range(len(units) + 2):
        if i < len(units):
            inners[i] = first(*units[i], probs[i % len(probs)])
        if 0 <= i - 1 < len(units):
            lows[i - 1] = second(*units[i - 1], probs[(i - 1) % len(probs)], inners.pop(i - 1))
        if 0 <= i - 2:
            third(*units[i - 2], lows.pop(i - 2))

    all_grads = d_ref[0]
    acc_w[...] += lax.dot_general(n_ref[0], all_grads, (((0,), (0,)), ((), ())), preferred_element_type=F32)
    sums_ref[...] += column_sums(all_grads.astype(F32))

    @pl.when(win == 1)
    def _():
        gw_ref[...] = acc_w[...].astype(BF16)
        lane8 = lax.broadcasted_iota(jnp.int32, (WT, 128), 1)

        @pl.when(first_group)
        def _():
            hot_copy.wait()

        all_rows, all_cols = fold_tables(accs, per, hots)
        for head in range(per):
            by_rows, by_cols = all_rows[head], all_cols[head]
            for d in range(ACROSS):
                for e in range(ACROSS):
                    if abs(e - WIN_HW + 1) < BIAS_DIMS[1][0]:
                        turned_back = lane_roll(by_cols[e], (e - d) * WT)
                        by_rows[d] = by_rows[d] + jnp.where(lane_block(lane8, e), turned_back, 0.0)
                strips_ref[(head * ACROSS + d) * WT : (head * ACROSS + d + 1) * WT, :] = by_rows[d]


def attend_back(first, groups, q, k, v, out_grad, out, inverse, unit, exps, dim):
    width = q.shape[1] * 128
    per = 128 // dim
    shapes = bias_shapes(per)
    lane_tile = pl.BlockSpec((1, 1, TOKENS, 128), lambda g, w: (w, first + g, 0, 0))
    exps_specs = [
        pl.BlockSpec((1, 1, KIND_ROWS[i], per * KIND_LANES[i]), lambda g, w: (w, first + g, 0, 0))
        for i in range(3)
    ]
    strip = (per * ACROSS * WT, 128)
    most = per * RECT[0].lanes
    return pl.pallas_call(
        functools.partial(attend_back_kernel, dim, dim**-0.5),
        grid=(groups, 2),
        in_specs=[lane_tile] * 5
        + [
            pl.BlockSpec((1, 1, per, ALL_LANES), lambda g, w: (w, first + g, 0, 0)),
            pl.BlockSpec((1, TOKENS, width), lambda g, w: (w, 0, 0)),
            pl.BlockSpec(memory_space=pl.ANY),
        ]
        + exps_specs,
        out_specs=[
            pl.BlockSpec((1, TOKENS, 384), lambda g, w: (w, 0, g)),
            pl.BlockSpec((width, 384), lambda g, w: (g, 0)),
            pl.BlockSpec((8, 384), lambda g, w: (g, 0)),
            pl.BlockSpec(strip, lambda g, w: (g, 0)),
        ],
        out_shape=[
            jax.ShapeDtypeStruct((2, TOKENS, groups * 384), BF16),
            jax.ShapeDtypeStruct((groups * width, 384), BF16),
            jax.ShapeDtypeStruct((groups * 8, 384), F32),
            jax.ShapeDtypeStruct((groups * strip[0], 128), F32),
        ],
        scratch_shapes=[pltpu.VMEM(s, F32) for s in shapes]
        + [
            pltpu.VMEM((width, 384), F32),
            pltpu.VMEM((FOLD_ROWS, 512), BF16),
            pltpu.SemaphoreType.DMA,
        ]
        + [pltpu.VMEM((RECT[0].rows, most), BF16)] * 2
        + [pltpu.VMEM((most, 128), BF16)] * 4
        + [pltpu.VMEM((RECT[0].rows, RECT[0].lanes), F32)] * 3,
        compiler_params=pltpu.CompilerParams(vmem_limit_bytes=60 << 20),
        cost_estimate=cost(18 * groups),
        name="attention_back",
    )(q, k, v, out_grad, out, inverse, unit, fold_matrices(), *exps)


ERFC = (0.254829592, -0.284496736, 1.421413741, -1.453152027, 1.061405429)
ERFC_P = 0.3275911


def gelu_both(u):
    denominator = 1.0 + (ERFC_P * 0.5**0.5) * jnp.abs(u)
    t = pl.reciprocal(denominator, approx=True)
    bell = jnp.exp2((u * u) * (-0.5 * LOG2E))
    series = 0.5 * ERFC[4]
    for factor in ERFC[3::-1]:
        series = series * t + 0.5 * factor
    tail = series * t * bell
    area = jnp.where(u >= 0.0, 1.0 - tail, tail)
    return u * area, area + (u * (1.0 / np.sqrt(2.0 * np.pi))) * bell


def mlp_kernel(
    tile,
    steps,
    chunk,
    parts,
    planes,
    edge_ref,
    x_ref,
    att_ref,
    own_ref,
    alt_ref,
    above_ref,
    below_ref,
    da_ref,
    dm_ref,
    wp_ref,
    pb_ref,
    g_ref,
    b_ref,
    w1_ref,
    b1_ref,
    w2_ref,
    b2_ref,
    mixed_ref,
    up_ref,
    down_ref,
    mg_ref,
    og_ref,
    mine_ref,
    theirs_ref,
    small_ref,
    fc1b_ref,
    doubled,
    tokens,
    acc_p,
    acc_1,
    acc_2,
    result,
    n2g,
    *buffers,
):
    hiddens, slopes = buffers[:2], buffers[2:]
    win, step = pl.program_id(0), pl.program_id(1)
    width = x_ref.shape[-1]

    @pl.when((win == 0) & (step == 0))
    def _():
        acc_p[...] = jnp.zeros_like(acc_p)
        acc_1[...] = jnp.zeros_like(acc_1)
        acc_2[...] = jnp.zeros_like(acc_2)
        small_ref[...] = jnp.zeros_like(small_ref)
        fc1b_ref[...] = jnp.zeros_like(fc1b_ref)

    @pl.when(step == 0)
    def _():
        assemble_tokens(win, edge_ref, own_ref, alt_ref, above_ref, below_ref, doubled, tokens)

    here = pl.ds(pl.multiple_of(step * tile, 16), tile)
    da, dm = da_ref[0], dm_ref[0]
    attended = get_groups(att_ref)
    branch = nn(attended, wp_ref[...]) + pb_ref[...]
    middle = x_ref[0].astype(F32) + by_frame(branch, da)
    unit, inverse = norm_stats(middle)
    normed = (unit * g_ref[...] + b_ref[...]).astype(BF16)
    upstream = tokens[here, :]
    result_grad = by_frame(upstream, dm).astype(BF16)
    small_ref[0] += column_sums(result_grad.astype(F32))
    normed_t = normed.T
    result_grad_t = result_grad.T
    count = w1_ref.shape[1] // chunk
    lows = {}

    def widen(i):
        part = slice(i * chunk, i * chunk + chunk)
        hiddens[i % 2][...] = nn(normed, w1_ref[:, part])
        slopes[i % 2][...] = nt(result_grad, w2_ref[part, :])

    def activate(i):
        part = slice(i * chunk, i * chunk + chunk)
        active, slope = gelu_both(hiddens[i % 2][...] + b1_ref[:, part])
        hidden_grad = slopes[i % 2][...] * slope
        fc1b_ref[:, part] += column_sums(hidden_grad)
        lows[i] = active.astype(BF16), hidden_grad.astype(BF16)

    def narrow(i):
        part = slice(i * chunk, i * chunk + chunk)
        active, hidden_grad = lows.pop(i)
        forward = nn(active, w2_ref[part, :])
        backward = nt(hidden_grad, w1_ref[:, part])
        if i == 0:
            result[...] = forward
            n2g[...] = backward
        else:
            result[...] += forward
            n2g[...] += backward
        acc_2[:, part] += nn(result_grad_t, active)
        acc_1[:, part] += nn(normed_t, hidden_grad)

    for i in range(count + 2):
        if 0 <= i - 1 < count:
            activate(i - 1)
        if i < count:
            widen(i)
        if 0 <= i - 2:
            narrow(i - 2)
    mixed = middle + by_frame(result[...] + b2_ref[...], dm)
    mixed_ref[0] = mixed.astype(BF16)
    tokens[here, :] = mixed
    normed_grad = n2g[...]
    small_ref[1] += column_sums(normed_grad * unit)
    small_ref[2] += column_sums(normed_grad)
    middle_grad = upstream + norm_back(normed_grad * g_ref[...], unit, inverse)
    mg_ref[0] = middle_grad
    branch_grad = by_frame(middle_grad, da).astype(BF16)
    small_ref[3] += column_sums(branch_grad.astype(F32))
    acc_p[...] += nn(attended.T, branch_grad)
    put_groups(og_ref, nt(branch_grad, wp_ref[...]).astype(BF16))

    for late, message_ref in enumerate((up_ref, down_ref)):

        @pl.when((win == late) & (step == steps - 1))
        def _():
            pack_message(late, tokens, message_ref)

    @pl.when((win == 1) & (step == steps - 1))
    def _():
        blocks = acc_1.shape[1] // width
        piece = 2 * mine_ref.shape[0] // parts
        for core in range(2):

            @pl.when(edge_ref[2] == core)
            def _():
                for i in range(2 * blocks + 1):
                    part = slice(i % blocks * width, i % blocks * width + width)
                    if i < blocks:
                        block = acc_1[:, part]
                    elif i < 2 * blocks:
                        block = acc_2[:, part].T
                    else:
                        block = acc_p[...]
                    block = block.astype(BF16)
                    for row in range(0, width, 16):
                        at, within = divmod(i * width + row, piece)
                        chip, plane = divmod(at, 2 * planes)
                        owner, plane = divmod(plane, planes)
                        to = (chip * planes + plane) * piece + within
                        ref = mine_ref if owner == core else theirs_ref
                        ref[to : to + 16, :] = block[row : row + 16]


def mlp(
    parts, planes, edges, x, att, cot, above, below, drop_attn, drop_mlp, wp, pb, g, b, w1, b1, w2, b2, tile=400, chunk=256
):
    width, hidden = w1.shape
    steps = TOKENS // tile
    half = (up_to(2 * hidden + width, 16 * parts) // 2, width)
    frames = pl.BlockSpec((1, WT, 128), lambda w, j: (w, 0, 0))
    return pl.pallas_call(
        functools.partial(mlp_kernel, tile, steps, chunk, parts, planes),
        grid=(2, steps),
        in_specs=[scalars(), tile_spec(tile, width), group_spec(tile, width)]
        + volume_specs(width)
        + [
            frames,
            frames,
            whole(wp.shape),
            whole((1, width)),
            whole((1, width)),
            whole((1, width)),
            whole(w1.shape),
            whole((1, hidden)),
            whole(w2.shape),
            whole((1, width)),
        ],
        out_specs=[
            tile_spec(tile, width),
            whole((TOKENS // 2, width)),
            whole((TOKENS // 2, width)),
            tile_spec(tile, width),
            group_spec(tile, width),
            whole(half),
            whole(half),
            whole((4, 8, width)),
            whole((8, hidden)),
        ],
        out_shape=[
            jax.ShapeDtypeStruct((2, TOKENS, width), BF16),
            jax.ShapeDtypeStruct((TOKENS // 2, width), BF16),
            jax.ShapeDtypeStruct((TOKENS // 2, width), BF16),
            jax.ShapeDtypeStruct((2, TOKENS, width), F32),
            group_shape(width),
            jax.ShapeDtypeStruct(half, BF16),
            jax.ShapeDtypeStruct(half, BF16),
            jax.ShapeDtypeStruct((4, 8, width), F32),
            jax.ShapeDtypeStruct((8, hidden), F32),
        ],
        scratch_shapes=[
            pltpu.VMEM((PLACES * WT, width), F32),
            pltpu.VMEM((TOKENS, width), F32),
            pltpu.VMEM((width, width), F32),
            pltpu.VMEM((width, hidden), F32),
            pltpu.VMEM((width, hidden), F32),
            pltpu.VMEM((tile, width), F32),
            pltpu.VMEM((tile, width), F32),
        ]
        + [pltpu.VMEM((tile, chunk), F32)] * 4,
        compiler_params=pltpu.CompilerParams(vmem_limit_bytes=62 << 20),
        cost_estimate=cost(100),
        name="mlp",
    )(
        edges,
        x,
        att,
        cot,
        cot,
        above,
        below,
        drop_attn,
        drop_mlp,
        wp,
        pb[None],
        g[None],
        b[None],
        w1,
        b1[None],
        w2,
        b2[None],
    )


def qkv_back_kernel(late, count, tile, *refs):
    grads = refs[:count]
    x_ref, mg_ref, w_ref, g_ref = refs[count : count + 4]
    out_ref, message_ref, tokens = refs[-3:]
    products = {}

    def multiply(i):
        here = slice(i * tile, i * tile + tile)
        groups = [d[0, here, at : at + 384] for d in grads for at in range(0, d.shape[-1], 384)]
        thirds = [g[:, third * 128 : third * 128 + 128] for third in range(3) for g in groups]
        products[i] = nt(jnp.concatenate(thirds, axis=-1), w_ref[...])

    def norm(i):
        here = slice(i * tile, i * tile + tile)
        unit, inverse = norm_stats(x_ref[0, here, :].astype(F32))
        grad = mg_ref[0, here, :] + norm_back(products.pop(i) * g_ref[...], unit, inverse)
        out_ref[0, here, :] = grad
        tokens[here, :] = grad

    steps = tokens.shape[0] // tile
    for i in range(steps + 1):
        if i < steps:
            multiply(i)
        if i:
            norm(i - 1)
    pack_message(late, tokens, message_ref)


def qkv_back(win, grads, x, middle_grad, w_qkv, gain, previous=None):
    width = x.shape[-1]
    rows = TOKENS // 2
    tile = pl.BlockSpec((1, rows, width), lambda j: (win, j, 0))
    passed = [] if previous is None else [previous]
    return pl.pallas_call(
        functools.partial(qkv_back_kernel, win == 1, len(grads), 400),
        grid=(2,),
        in_specs=[pl.BlockSpec((1, rows, g.shape[-1]), lambda j: (win, j, 0)) for g in grads]
        + [tile] * 2
        + [whole(w_qkv.shape), whole((1, width))]
        + [pl.BlockSpec(memory_space=pl.ANY) for _ in passed],
        out_specs=[tile, pl.BlockSpec((rows // 2, width), lambda j: (j, 0))],
        out_shape=[
            jax.ShapeDtypeStruct((2, TOKENS, width), F32),
            jax.ShapeDtypeStruct((rows, width), BF16),
        ],
        scratch_shapes=[pltpu.VMEM((rows, width), F32)],
        input_output_aliases={len(grads) + 4: 0} if passed else {},
        compiler_params=pltpu.CompilerParams(vmem_limit_bytes=44 << 20),
        cost_estimate=cost(9),
        name="qkv_back",
    )(*grads, x, middle_grad, w_qkv, gain[None], *passed)


def place_kernel(edge_ref, own_ref, up_ref, down_ref, below_ref, above_ref, out_ref, doubled):
    vol = pl.program_id(0)
    edge = edge_ref[vol] == 1
    inner = jnp.logical_not(edge)
    for late, received, sent in ((False, below_ref, down_ref), (True, above_ref, up_ref)):
        mine = vol == int(late)

        @pl.when(jnp.logical_and(mine, inner))
        def _():
            spread_message(received, late, doubled)

        @pl.when(jnp.logical_and(mine, edge))
        def _():
            spread_message(sent, late, doubled)

    width = out_ref.shape[-1]
    from_other = row_half((WT, width)) == (vol == 0)
    for slot in range(0, len(SLOTS), 2):
        both = own_ref[0, slot * WT : slot * WT + 2 * WT, :].astype(F32)
        for k in range(2):
            place = SLOTS[slot + k]
            if place is None:
                continue
            other = doubled[(slot + k) * WT : (slot + k + 1) * WT, :]
            value = jnp.where(from_other, other, both[k * WT : k * WT + WT])
            out_ref[0, place[0], place[1]] = value.astype(out_ref.dtype)


def to_frames(edges, tokens, up, down, below, above):
    width = tokens.shape[-1]
    return pl.pallas_call(
        place_kernel,
        grid=(2,),
        in_specs=[scalars(), pl.BlockSpec((1, TOKENS, width), lambda v: (v, 0, 0))] + [whole(up.shape)] * 4,
        out_specs=pl.BlockSpec((1, SIDE, SIDE, WT, width), lambda v: (v, 0, 0, 0, 0)),
        out_shape=jax.ShapeDtypeStruct((2, SIDE, SIDE, WT, width), tokens.dtype),
        scratch_shapes=[pltpu.VMEM((TOKENS, width), F32)],
        compiler_params=pltpu.CompilerParams(vmem_limit_bytes=28 << 20),
        cost_estimate=cost(5),
        name="to_frames",
    )(edges, tokens, up, down, below, above)


def tie(value, *after):
    return lax.optimization_barrier((value,) + after)[0]


def pick(array, index, axis=0):
    return lax.dynamic_index_in_dim(array, index, axis, keepdims=False)


def add_low(*values):
    return sum(v.astype(F32) for v in values).astype(BF16)


class Sum:
    def __init__(self, buffer=None, mine=None, theirs=None):
        self.n = lax.axis_size("tm")
        self.size = lax.axis_size("dp")
        self.m = self.size // 2
        dp = lax.axis_index("dp")
        self.core, self.chip, self.plane = dp % 2, dp // 2, lax.axis_index("tm")
        if buffer is not None:
            rows, width = buffer.shape
            whole = buffer.reshape(self.m, 2, self.n, rows // (2 * self.m * self.n), width)
            mine, theirs = pick(whole, self.core, 1), pick(whole, 1 - self.core, 1)
        else:
            rows, width = mine.shape
            shape = (self.m, self.n, rows // (self.m * self.n), width)
            mine, theirs = mine.reshape(shape), theirs.reshape(shape)
        self.piece = mine.shape[2:]
        self.mine, self.theirs = mine, theirs

    def to_core(self, values):
        return lax.ppermute(values, "dp", [(i, i ^ 1) for i in range(self.size)])

    def to_chip(self, values, s):
        return lax.ppermute(values, "dp", [(i, i ^ (2 * s)) for i in range(self.size)])

    def to_plane(self, values, s):
        return lax.ppermute(values, "tm", [(i, i ^ s) for i in range(self.n)])

    def step0(self):
        self.got = self.to_core(self.theirs)
        return self

    def step1(self):
        parts = [add_low(pick(self.mine, self.chip ^ s), pick(self.got, self.chip ^ s)) for s in range(self.m)]
        self.mine = parts[0]
        self.got = [self.to_chip(parts[s], s) for s in range(1, self.m)]
        return parts[-1]

    def step2(self):
        total = add_low(self.mine, *self.got)
        parts = [pick(total, self.plane ^ s) for s in range(self.n)]
        self.mine = parts[0]
        self.got = [self.to_plane(parts[s], s) for s in range(1, self.n)]
        return parts[-1]

    def step3(self):
        self.mine = add_low(self.mine, *self.got)
        self.got = []
        return self.mine

    def gathered(self):
        return lax.all_gather(self.mine, ("dp", "tm"), tiled=True)

    def step3_back(self):
        self.step3()
        self.got = [self.to_plane(self.mine, s) for s in range(1, self.n)]
        return self.mine

    def step4_back(self):
        self.mine = jnp.stack([self.mine] + self.got)
        self.got = [self.to_chip(self.mine, s) for s in range(1, self.m)]
        return self.mine

    def step5_back(self):
        self.mine = jnp.stack([self.mine] + self.got)
        self.other = self.to_core(self.mine)
        return self.mine


EXTRA_TILES = 4
EXTRA_TABLE = 16


def pack_kernel(calls, width, *refs):
    pieces, strips, colsums = refs[:calls], refs[calls : 2 * calls], refs[2 * calls : 3 * calls]
    small_ref, fc1b_ref, out_ref, extra = refs[3 * calls :]
    extra[...] = jnp.zeros_like(extra)
    group, at = 0, 0
    for c in range(calls):
        rows = pieces[c].shape[0]
        out_ref[at : at + rows, :] = pieces[c][...]
        at += rows
        for g in range(rows // width):
            extra[group : group + 1, :] = jnp.sum(colsums[c][g * 8 : g * 8 + 8, :], axis=0, keepdims=True)
            group += 1
    vectors = [jnp.sum(small_ref[i], axis=0, keepdims=True) for i in range(4)]
    vectors.append(jnp.sum(fc1b_ref[...], axis=0, keepdims=True))
    vectors = jnp.concatenate(vectors, axis=1)
    for t in range(vectors.shape[1] // 128):
        row, lanes = EXTRA_TILES + t // 3, t % 3 * 128
        extra[row : row + 1, lanes : lanes + 128] = vectors[:, t * 128 : t * 128 + 128]
    counts = [s.shape[0] // WT for s in strips]
    totals = [jnp.zeros((rows, ACROSS * (2 * WT - 1)), F32) for rows in counts]
    for tk in range(WT):
        hot = hot_times(tk)
        for c in range(calls):
            for part in split3(strips[c][pl.ds(tk, counts[c], stride=WT), :]):
                totals[c] = totals[c] + nt(part, hot)
    row = EXTRA_TABLE
    for c in range(calls):
        extra[row : row + counts[c], : totals[c].shape[1]] = totals[c]
        row += counts[c]
    out_ref[at:, :] = extra[...].astype(BF16)


def pack(pieces, strips, colsums, small, fc1b, unit_rows):
    width, lanes = small.shape[-1], pieces[0].shape[1]
    main = sum(p.shape[0] for p in pieces)
    rows = up_to(main + EXTRA_TABLE + sum(s.shape[0] for s in strips) // WT, unit_rows)
    return pl.pallas_call(
        functools.partial(pack_kernel, len(pieces), width),
        out_shape=jax.ShapeDtypeStruct((rows, lanes), BF16),
        scratch_shapes=[pltpu.VMEM((rows - main, lanes), F32)],
        compiler_params=pltpu.CompilerParams(vmem_limit_bytes=24 << 20),
        cost_estimate=cost(4),
        name="pack_sums",
    )(*pieces, *strips, *colsums, small, fc1b)


def finish_kernel(m, n, groups, ids_ref, mine_ref, other_ref, w_ref, gain_ref, bias_ref, *refs):
    gw_ref, lg_ref, lb_ref, qb_ref, vb_ref, s0, s1, s2, s3, fc1b_ref, table_ref, total, sorted_rows = refs
    core, chip, plane = ids_ref[0], ids_ref[1], ids_ref[2]
    rows = mine_ref.shape[1]
    for c in range(m):
        for k in range(2):
            for z in range(n):
                at = (chip ^ c) * n + (plane ^ z)
                block = jnp.where(core == k, mine_ref[at].astype(F32), other_ref[at].astype(F32))
                first = ((c * 2 + k) * n + z) * rows
                total[first : first + rows, :] = block
    width = w_ref.shape[0]
    base = groups * width
    gain = gain_ref[...]
    bias = bias_ref[...]
    products = jnp.zeros((width, 128), F32)
    row = jnp.zeros((1, width), F32)
    for g in range(groups):
        part = total[g * width : (g + 1) * width, :]
        sums = total[base + g : base + g + 1, :]
        grad = gain * part + bias * sums
        for third in range(3):
            lanes = slice(third * 128, third * 128 + 128)
            at = third * width + g * 128
            gw_ref[:, at : at + 128] = grad[:, lanes]
            weight = w_ref[:, at : at + 128]
            products = products + weight.astype(F32) * part[:, lanes]
            for piece in split3(jnp.broadcast_to(sums[:, lanes], (8, 128))):
                row = row + nt(piece, weight)[:1]
        qb_ref[:, g * 128 : g * 128 + 128] = sums[:, :128]
        vb_ref[:, g * 128 : g * 128 + 128] = sums[:, 256:]
    lb_ref[...] = row
    ones = jnp.ones((8, 128), BF16)
    lg_ref[...] = sum(nt(ones, piece) for piece in split3(products))[:1]
    targets = [(ref, p) for ref in (s0, s1, s2, s3, fc1b_ref) for p in range(ref.shape[1] // 128)]
    for t, (ref, p) in enumerate(targets):
        at = base + EXTRA_TILES + t // 3
        ref[:, p * 128 : p * 128 + 128] = total[at : at + 1, t % 3 * 128 : t % 3 * 128 + 128]
    heads, entries = table_ref.shape
    times = 2 * WT - 1
    lane = lax.broadcasted_iota(jnp.int32, (heads, 128), 1)
    tiles = [None] * (up_to(entries, 128) // 128)
    for part in range(up_to(ACROSS * times, 128) // 128):
        sorted_rows[...] = total[base + EXTRA_TABLE :, part * 128 : part * 128 + 128]
        for dh in range(ACROSS):
            source = sorted_rows[pl.ds(dh, heads, stride=ACROSS), :]
            for dt in range(times):
                begin, end = max(dt * ACROSS, part * 128), min((dt + 1) * ACROSS, part * 128 + 128)
                if begin >= end:
                    continue
                move = dt * ACROSS * ACROSS + dh * ACROSS - dt * ACROSS
                rolled = lane_roll(source, move)
                for tile in range((begin + move) // 128, (end - 1 + move) // 128 + 1):
                    here = lane + tile * 128
                    value = jnp.where((here >= begin + move) & (here < end + move), rolled, 0.0)
                    tiles[tile] = value if tiles[tile] is None else tiles[tile] + value
    for tile, value in enumerate(tiles):
        stop = min(128, entries - tile * 128)
        table_ref[:, tile * 128 : tile * 128 + stop] = value[:, :stop]


def finish(sums, w_qkv, gain, bias, hidden, heads):
    width = w_qkv.shape[0]
    groups = width // 128
    rows, lanes = sums.piece
    count = sums.m * sums.n
    ids = jnp.stack([sums.core, sums.chip, sums.plane])
    vector = jax.ShapeDtypeStruct((1, width), F32)
    return pl.pallas_call(
        functools.partial(finish_kernel, sums.m, sums.n, groups),
        in_specs=[scalars()] + [pl.BlockSpec(memory_space=pltpu.VMEM)] * 5,
        out_specs=[pl.BlockSpec(memory_space=pltpu.VMEM)] * 11,
        out_shape=[jax.ShapeDtypeStruct(w_qkv.shape, F32)]
        + [vector] * 8
        + [
            jax.ShapeDtypeStruct((1, hidden), F32),
            jax.ShapeDtypeStruct((heads, ACROSS * ACROSS * (2 * WT - 1)), F32),
        ],
        scratch_shapes=[
            pltpu.VMEM((2 * count * rows, lanes), F32),
            pltpu.VMEM((2 * count * rows - groups * width - EXTRA_TABLE, 128), F32),
        ],
        compiler_params=pltpu.CompilerParams(vmem_limit_bytes=32 << 20),
        cost_estimate=cost(5),
        name="finish",
    )(
        ids,
        sums.mine.reshape(count, rows, lanes),
        sums.other.reshape(count, rows, lanes),
        w_qkv,
        gain[:, None],
        bias[:, None],
    )


def widen_kernel(blocks, in_ref, fc1_ref, fc2_ref, proj_ref):
    step = pl.program_id(0)

    @pl.when(step < blocks)
    def _():
        fc1_ref[...] = in_ref[...].astype(F32)

    @pl.when(jnp.logical_and(step >= blocks, step < 2 * blocks))
    def _():
        fc2_ref[...] = in_ref[...].astype(F32)

    @pl.when(step == 2 * blocks)
    def _():
        proj_ref[...] = in_ref[...].astype(F32)


def widen_grads(buffer, hidden):
    width = buffer.shape[1]
    blocks = hidden // width
    block = (width, width)
    return pl.pallas_call(
        functools.partial(widen_kernel, blocks),
        grid=(2 * blocks + 1,),
        in_specs=[pl.BlockSpec(block, lambda i: (i, 0))],
        out_specs=[
            pl.BlockSpec(block, lambda i: (0, jnp.minimum(i, blocks - 1))),
            pl.BlockSpec(block, lambda i: (jnp.clip(i - blocks, 0, blocks - 1), 0)),
            pl.BlockSpec(block, lambda i: (0, 0)),
        ],
        out_shape=[
            jax.ShapeDtypeStruct((width, hidden), F32),
            jax.ShapeDtypeStruct((hidden, width), F32),
            jax.ShapeDtypeStruct(block, F32),
        ],
        compiler_params=pltpu.CompilerParams(vmem_limit_bytes=14 << 20),
        cost_estimate=cost(5),
        name="widen_grads",
    )(buffer)


def neighbours():
    count = lax.axis_size("tm")
    down = [(i, i - 1) for i in range(1, count)]
    up = [(i, i + 1) for i in range(count - 1)]
    return down, up


def fetch_halves(field):
    down, up = neighbours()
    width = field.shape[-1]
    above = lax.ppermute(field[0, :, :, :SHIFT_T].reshape(PLACES * SHIFT_T, width), "tm", down)
    below = lax.ppermute(field[1, :, :, SHIFT_T:].reshape(PLACES * SHIFT_T, width), "tm", up)
    return above, below


def send_up(message):
    return lax.ppermute(message, "tm", neighbours()[1])


def send_down(message):
    return lax.ppermute(message, "tm", neighbours()[0])


def frame_facts(segments, keep):
    count = lax.axis_size("tm")
    me = lax.axis_index("tm")
    own = 2 * SHIFT_T
    first = me * own
    t = jnp.arange(SHIFT_T)
    zero, one = jnp.zeros((SHIFT_T,), jnp.int32), jnp.ones((SHIFT_T,), jnp.int32)
    top, bottom = me == count - 1, me == 0
    frames = jnp.stack(
        [
            jnp.concatenate([jnp.where(top, first + SHIFT_T + t, first + own + t), first + SHIFT_T + t]),
            jnp.concatenate([first + t, jnp.where(bottom, t, first - SHIFT_T + t)]),
        ]
    )
    volumes = jnp.stack(
        [jnp.concatenate([jnp.where(top, one, zero), zero]), jnp.concatenate([one, jnp.where(bottom, zero, one)])]
    )
    pick_frame = (frames[:, :, None] == jnp.arange(segments.shape[1])).astype(jnp.int32)
    by_volume = jnp.sum(pick_frame[:, :, None, :] * segments[None, None], axis=-1)
    segment = jnp.where(volumes == 0, by_volume[..., 0], by_volume[..., 1])
    key = segment + 8 * (frames < SHIFT_T) + 16 * volumes
    apart = (key[:, :, None] != key[:, None, :]).astype(F32) * FAR
    far = jnp.tile(apart, (1, 1, 128 // WT))
    seg_hot = (segment[:, :, None] == jnp.arange(keep.shape[2])).astype(F32)
    kept = jnp.where(volumes[:, :, None, None] == 0, keep[0], keep[1]).astype(F32)
    drops = jnp.sum(seg_hot[:, :, None, :] * kept, axis=-1) / KEEP_RATE
    drops = jnp.broadcast_to(drops[..., None], drops.shape + (128,))
    return far, drops[:, :, 0], drops[:, :, 1]


def shards(
    volume,
    segments,
    keep,
    ln1_gain,
    ln1_bias,
    w_qkv,
    q_bias,
    v_bias,
    rel_table,
    w_proj,
    proj_bias,
    ln2_gain,
    ln2_bias,
    w_fc1,
    fc1_bias,
    w_fc2,
    fc2_bias,
    cotangent,
):
    width = volume.shape[-1]
    heads = rel_table.shape[1]
    dim = width // heads
    hidden = w_fc1.shape[1]
    groups = width // 128
    me = lax.axis_index("tm")
    top, bottom = me == lax.axis_size("tm") - 1, me == 0
    planes = lax.axis_size("tm")
    parts = lax.axis_size("dp") * planes
    edges_in = jnp.stack([top, bottom, lax.axis_index("dp") % 2]).astype(jnp.int32)
    edges_out = jnp.stack([bottom, top]).astype(jnp.int32)
    places = volume.transpose(0, 2, 3, 1, 4)
    cot = cotangent.transpose(0, 2, 3, 1, 4)
    above, below = fetch_halves(places)
    far, drop_attn, drop_mlp = frame_facts(segments, keep)
    biases = make_bias(rel_table)
    qkv_bias = jnp.concatenate([q_bias, jnp.zeros_like(q_bias), v_bias])
    x, unit, q, k, v = make_qkv(
        edges_in, places, above, below, ln1_gain, ln1_bias, w_qkv, qkv_bias, dim**-0.5 * LOG2E
    )
    cot_above, cot_below = fetch_halves(tie(cot, q))
    *exps, att, inverse = attend(q, k, v, far, biases, dim)
    mixed, mixed_up, mixed_down, middle_grad, out_grad, g_mine, g_theirs, small2, small_fc1 = mlp(
        parts,
        planes,
        edges_in,
        x,
        att,
        cot,
        cot_above,
        cot_below,
        drop_attn,
        drop_mlp,
        w_proj,
        proj_bias,
        ln2_gain,
        ln2_bias,
        w_fc1,
        fc1_bias,
        w_fc2,
        fc2_bias,
    )
    mixed_below, mixed_above = send_up(mixed_up), send_down(mixed_down)
    mlp_sum = Sum(mine=g_mine, theirs=g_theirs).step0()
    grads, pieces, sums, strips = [], [], [], []
    first = 0
    for many, step in ((2, mlp_sum.step1), (1, mlp_sum.step2), (1, mlp_sum.step3)):
        wait = step()
        d, gw, colsum, strip = attend_back(first, many, q, k, v, tie(out_grad, wait), att, inverse, unit, exps, dim)
        first += many
        grads.append(d)
        pieces.append(gw)
        sums.append(colsum)
        strips.append(strip)
        mlp_sum.got = lax.optimization_barrier((mlp_sum.got, d))[0]
    all_mlp = mlp_sum.gathered()
    unit_rows = 8 * lax.axis_size("dp") * lax.axis_size("tm")
    qkv_sum = Sum(pack(pieces, strips, sums, small2, small_fc1, unit_rows)).step0()
    grad0, grad_up = qkv_back(0, grads, tie(x, qkv_sum.theirs), middle_grad, w_qkv, ln1_gain)
    below = send_up(grad_up)
    qkv_sum.got = tie(qkv_sum.got, grad0)
    wait = qkv_sum.step1()
    grad, grad_down = qkv_back(1, grads, tie(x, wait, grad_up), middle_grad, w_qkv, ln1_gain, grad0)
    above = send_down(grad_down)
    qkv_sum.got = lax.optimization_barrier((qkv_sum.got, grad))[0]
    wait = qkv_sum.step2()
    mixed_out = to_frames(edges_out, tie(mixed, wait), mixed_up, mixed_down, mixed_below, mixed_above)
    g_fc1, g_fc2, g_proj = widen_grads(tie(all_mlp, mixed_out), hidden)
    qkv_sum.got = lax.optimization_barrier((qkv_sum.got, g_fc1))[0]
    qkv_sum.step3_back()
    wait = qkv_sum.step4_back()
    volume_grad = to_frames(edges_out, tie(grad, wait), grad_up, grad_down, below, above)
    qkv_sum.got = lax.optimization_barrier((qkv_sum.got, volume_grad))[0]
    qkv_sum.step5_back()
    g_qkv, ln1_g, ln1_b, q_b, v_b, fc2_b, ln2_g, ln2_b, proj_b, fc1_b, table = finish(
        qkv_sum, w_qkv, ln1_gain, ln1_bias, hidden, heads
    )
    return (
        mixed_out.transpose(0, 3, 1, 2, 4),
        volume_grad.transpose(0, 3, 1, 2, 4),
        ln1_g[0],
        ln1_b[0],
        g_qkv,
        q_b[0],
        v_b[0],
        table.T,
        g_proj,
        proj_b[0],
        ln2_g[0],
        ln2_b[0],
        g_fc1,
        fc1_b[0],
        g_fc2,
        fc2_b[0],
    )


def solution(mesh):
    split = P("dp", "tm", None, None, None)
    return jax.shard_map(
        shards,
        mesh=mesh,
        in_specs=(split, P("dp", None), P("dp", None, None)) + (P(),) * 14 + (split,),
        out_specs=(split, split) + (P(),) * 14,
        check_vma=False,
    )
```
